32 devices in a mesh: dp: 4 (over y, x), seq: 8 (over z, core).
Axes of the slice: x: 2, y: 2, z: 4, core: 2. Of those that a mesh axis runs over, the one named last changes fastest.
Arguments:
- tokens: bfloat16 [10240, 2048], P(('dp', 'seq')), may hold values from -6 to 6
- lengths: int32 [4, 2], P('dp'), may hold values from 1 to 2048, 2560 in all within a row
- attention_gain: bfloat16 [2048], P('seq'), may hold values from 0.5 to 1.5
- query_weight: bfloat16 [2048, 2048], P('seq'), may hold values from -0.1875 to 0.1875
- key_weight: bfloat16 [2048, 256], P('seq'), may hold values from -0.1875 to 0.1875
- value_weight: bfloat16 [2048, 256], P('seq'), may hold values from -0.125 to 0.125
- output_weight: bfloat16 [2048, 2048], P('seq'), may hold values from -0.375 to 0.375
- feedforward_gain: bfloat16 [2048], P('seq'), may hold values from 0.5 to 1.5
- gate_weight: bfloat16 [2048, 5632], P('seq'), may hold values from -0.125 to 0.125
- up_weight: bfloat16 [2048, 5632], P('seq'), may hold values from -0.125 to 0.125
- down_weight: bfloat16 [5632, 2048], P('seq'), may hold values from -0.078125 to 0.078125
- cotangent: bfloat16 [10240, 2048], P(('dp', 'seq')), may hold values from -6 to 6
Outputs:
- layer_output: bfloat16 [10240, 2048], P(('dp', 'seq'))
- token_gradient: float32 [10240, 2048], P(('dp', 'seq'))
- attention_gain_gradient: float32 [2048], P('seq')
- query_gradient: float32 [2048, 2048], P('seq')
- key_gradient: float32 [2048, 256], P('seq')
- value_gradient: float32 [2048, 256], P('seq')
- output_gradient: float32 [2048, 2048], P('seq')
- feedforward_gain_gradient: float32 [2048], P('seq')
- gate_gradient: float32 [2048, 5632], P('seq')
- up_gradient: float32 [2048, 5632], P('seq')
- down_gradient: float32 [5632, 2048], P('seq')
The draws below stay inside these ranges and needn't reach their ends.
Inputs may be any that keep to these rules, and one draw needn't show every extreme that they name: Each row lists the lengths of the 2 sequences packed in order into one data group's 2560 tokens; a row sums to 2560 and its longest length is at most 2048.
All inputs are finite; a program needn't handle non-finite values.
Results may differ from the reference program's by a relative error of at most 0.022.
Values may be sent and summed in bfloat16 or wider, within the bound.
No kernel may reach another device: no remote copies, remote signals or barrier semaphores. Data moves between devices by JAX's collectives and lax.ppermute only.
A program may use at most 384 MiB of HBM per device.

```python
import math
import jax
import jax.numpy as jnp
import numpy as np
from jax import lax

D = 2048
HEADS = 32
HEAD_DIM = 64
KV_HEADS = 4
FF = 5632
MAXLEN = 2048
QBLOCK = 512
WINDOW = 2560
GROUP_TOK = 2560
NSEQ = 2
TOKENS = 10240
N_DP = 4


def block_scale(own_key, dims, cuts, smallest, high):
    def one(dim, shards_of):
        steps = jax.random.uniform(jax.random.fold_in(jax.random.fold_in(own_key, 6), dim), (shards_of,), jnp.float32, smallest / len(cuts), high / len(cuts))
        return jnp.repeat(jnp.exp(steps), dims[dim] // shards_of).reshape((-1,) + (1,) * (len(dims) - dim - 1))

    level = one(*cuts[0])
    for cut in cuts[1:]:
        level = level * one(*cut)
    return level


def length_profile(amount, total, reach, slope):
    weights = [(1 << 20) // math.isqrt(rank ** slope) + 1 for rank in range(2, amount + 1)]
    surplus, holding = total - reach - (amount - 1), [1] * (amount - 1)
    while surplus > 0:
        free = [i for i in range(amount - 1) if holding[i] < reach]
        pool, budget = sum([weights[i] for i in free]), surplus
        for i in free:
            extra = min(reach - holding[i], max(1, budget * weights[i] // pool), surplus)
            holding[i] = holding[i] + extra
            surplus = surplus - extra
    return np.array([reach] + holding)


def ragged(own_key, amount, total, reach, lean):
    if amount == 2:
        one = jax.random.randint(own_key, (), max(1, total - reach), min(reach, total - 1) + 1)
        return jnp.stack([one, total - one])
    sizes = jnp.asarray(length_profile(amount, total, reach, lean), jnp.int32)
    twos = (amount - 1) // 2
    donor, sink = sizes[1:1 + 2 * twos:2], sizes[2:2 + 2 * twos:2]
    slack = jnp.minimum(donor - 1, reach - sink)
    moved = jax.random.randint(jax.random.fold_in(own_key, 1), (twos,), 0, 1 << 20) % (slack + 1)
    sizes = sizes.at[1:1 + 2 * twos:2].set(donor - moved).at[2:2 + 2 * twos:2].set(sink + moved)
    return sizes[jax.random.permutation(jax.random.fold_in(own_key, 2), amount)]


def scatter_about(own_key, extent, width, limit, shards=(), kind=jnp.bfloat16):
    entries = jax.random.normal(own_key, extent, jnp.float32) * width
    if len(shards) > 0:
        entries = block_scale(own_key, extent, shards, -0.22, 0.18) * entries
    return jnp.clip(entries, min=-limit, max=limit).astype(kind)


def setup_inputs(seed: int = 0) -> dict:
    streams_of = jax.random.split(jax.random.key(seed), 13)
    return {
        "tokens": scatter_about(streams_of[0], (TOKENS, D), 1.0, 6.0, ((0, 32),)),
        "lengths": jax.vmap(lambda own: ragged(own, NSEQ, GROUP_TOK, MAXLEN, 2))(jax.random.split(streams_of[1], N_DP)).reshape((N_DP, NSEQ)).astype(jnp.int32),
        "attention_gain": jnp.clip(1.0 + 0.1 * jax.random.normal(streams_of[2], (D,), jnp.float32), 0.5, 1.5).astype(jnp.bfloat16),
        "query_weight": scatter_about(streams_of[3], (D, D), (D // 2) ** -0.5, 0.1875, ((0, 8),)),
        "key_weight": scatter_about(streams_of[4], (D, KV_HEADS * HEAD_DIM), (D // 2) ** -0.5, 0.1875, ((0, 8),)),
        "value_weight": scatter_about(streams_of[5], (D, KV_HEADS * HEAD_DIM), D ** -0.5, 0.125, ((0, 8),)),
        "output_weight": scatter_about(streams_of[6], (D, D), (D // 8) ** -0.5, 0.375, ((0, 8),)),
        "feedforward_gain": jnp.clip(1.0 + 0.1 * jax.random.normal(streams_of[7], (D,), jnp.float32), 0.5, 1.5).astype(jnp.bfloat16),
        "gate_weight": scatter_about(streams_of[8], (D, FF), D ** -0.5, 0.125, ((0, 8),)),
        "up_weight": scatter_about(streams_of[9], (D, FF), D ** -0.5, 0.125, ((0, 8),)),
        "down_weight": scatter_about(streams_of[10], (FF, D), FF ** -0.5, 0.078125, ((0, 8),)),
        "cotangent": scatter_about(streams_of[11], (TOKENS, D), 1.0, 6.0, ((0, 32),)),
    }


EPS = 1e-05
ROPE_BASE = 10000.0
NEG = -1e+30
HIGH = lax.Precision.HIGHEST

@jax.custom_vjp
def low(v):
    return lax.optimization_barrier(v.astype(jnp.bfloat16)).astype(jnp.float32)

@jax.custom_vjp
def low_back(v):
    return v

def low_keep(v):
    return (low(v), None)

def low_pass(kept, grad):
    return (grad,)

def back_keep(v):
    return (v, None)

def back_low(kept, grad):
    return (low(grad),)
low.defvjp(low_keep, low_pass)
low_back.defvjp(back_keep, back_low)

def product(left, right):
    return jnp.dot(left, right, precision=HIGH)

def layout(lengths_row, count):
    lengths_row = lengths_row.astype(jnp.int32)
    ends = jnp.cumsum(lengths_row).astype(jnp.int32)
    starts = (ends - lengths_row).astype(jnp.int32)
    index = jnp.arange(count, dtype=jnp.int32)
    segment = lax.optimization_barrier(jnp.sum((index[:, None] >= ends[None, :]).astype(jnp.int32), axis=1)).astype(jnp.int32)
    owner = segment[:, None] == jnp.arange(lengths_row.shape[0], dtype=jnp.int32)[None, :]
    first = lax.optimization_barrier(jnp.sum(jnp.where(owner, starts[None, :], 0), axis=1)).astype(jnp.int32)
    return (segment, (index - first).astype(jnp.int32))

def angles(position):
    half = HEAD_DIM // 2
    inverse = ROPE_BASE ** (-jnp.arange(half, dtype=jnp.float32) * 2.0 / HEAD_DIM)
    theta = position.astype(jnp.float32)[:, None] * inverse[None, :]
    return (jnp.cos(theta)[:, None, :], jnp.sin(theta)[:, None, :])

def rotate(values, cos_t, sin_t):
    half = values.shape[-1] // 2
    first = values[..., :half]
    second = values[..., half:]
    return jnp.concatenate([first * cos_t - second * sin_t, second * cos_t + first * sin_t], axis=-1)

def attend_group(query, keys, values, segment, position):
    blocks = query.shape[0] // QBLOCK
    scale = HEAD_DIM ** (-0.5)

    def one_block(number):
        row = number * QBLOCK
        first = jnp.maximum(row + QBLOCK - WINDOW, 0).astype(jnp.int32)
        q_rows = lax.dynamic_slice_in_dim(query, row, QBLOCK, 0)
        k_rows = lax.dynamic_slice_in_dim(keys, first, WINDOW, 0)
        v_rows = lax.dynamic_slice_in_dim(values, first, WINDOW, 0)
        seg_q = lax.dynamic_slice_in_dim(segment, row, QBLOCK, 0)
        pos_q = lax.dynamic_slice_in_dim(position, row, QBLOCK, 0)
        seg_k = lax.dynamic_slice_in_dim(segment, first, WINDOW, 0)
        pos_k = lax.dynamic_slice_in_dim(position, first, WINDOW, 0)
        raw = jnp.einsum('qhd,khd->hqk', q_rows, k_rows, precision=HIGH)
        scores = low_back(raw * scale)
        allowed = (seg_q[:, None] == seg_k[None, :]) & (pos_k[None, :] <= pos_q[:, None])
        scores = jnp.where(allowed[None], scores, NEG)
        weights = low(jax.nn.softmax(scores, axis=-1))
        return jnp.einsum('hqk,khd->qhd', weights, v_rows, precision=HIGH)
    stacked = lax.map(jax.checkpoint(one_block), jnp.arange(blocks, dtype=jnp.int32))
    return stacked.reshape(query.shape)

def forward(tokens, attention_gain, query_weight, key_weight, value_weight, output_weight, feedforward_gain, gate_weight, up_weight, down_weight, segment, position, cos_t, sin_t):
    count = tokens.shape[0]
    share = HEADS // KV_HEADS
    scale_one = lax.rsqrt(lax.optimization_barrier(jnp.mean(tokens * tokens, axis=1, keepdims=True)) + EPS)
    normed = low(tokens * scale_one * attention_gain)
    q_proj = low_back(product(normed, query_weight)).reshape(count, HEADS, HEAD_DIM)
    k_proj = low_back(product(normed, key_weight)).reshape(count, KV_HEADS, HEAD_DIM)
    v_proj = low_back(product(normed, value_weight)).reshape(count, KV_HEADS, HEAD_DIM)
    queries = low_back(low(rotate(q_proj, cos_t, sin_t)))
    keys = low_back(jnp.repeat(low(rotate(k_proj, cos_t, sin_t)), share, axis=1))
    values = low_back(jnp.repeat(low(v_proj), share, axis=1))
    pieces = []
    for group in range(N_DP):
        lower = group * GROUP_TOK
        upper = lower + GROUP_TOK
        pieces.append(attend_group(queries[lower:upper], keys[lower:upper], values[lower:upper], segment[lower:upper], position[lower:upper]))
    mixed = low_back(low(jnp.concatenate(pieces, axis=0))).reshape(count, D)
    attention_out = low_back(product(mixed, output_weight))
    middle = tokens + attention_out
    scale_two = lax.rsqrt(lax.optimization_barrier(jnp.mean(middle * middle, axis=1, keepdims=True)) + EPS)
    normed_two = low(middle * scale_two * feedforward_gain)
    gate = low_back(product(normed_two, gate_weight))
    up_part = low_back(product(normed_two, up_weight))
    hidden = low(jax.nn.silu(gate) * up_part)
    return middle + product(hidden, down_weight)

def reference(tokens, lengths, attention_gain, query_weight, key_weight, value_weight, output_weight, feedforward_gain, gate_weight, up_weight, down_weight, cotangent):
    segments = []
    positions = []
    for group in range(N_DP):
        seg_group, pos_group = layout(lengths[group], GROUP_TOK)
        segments.append(seg_group)
        positions.append(pos_group)
    segment = jnp.concatenate(segments, axis=0)
    position = jnp.concatenate(positions, axis=0)
    cos_t, sin_t = angles(position)

    def closed(*primals):
        return forward(*primals, segment, position, cos_t, sin_t)
    output, pullback = jax.vjp(closed, tokens.astype(jnp.float32), attention_gain.astype(jnp.float32), query_weight.astype(jnp.float32), key_weight.astype(jnp.float32), value_weight.astype(jnp.float32), output_weight.astype(jnp.float32), feedforward_gain.astype(jnp.float32), gate_weight.astype(jnp.float32), up_weight.astype(jnp.float32), down_weight.astype(jnp.float32))
    grads = pullback(cotangent.astype(jnp.float32))
    return (output.astype(jnp.bfloat16), grads[0], grads[1], grads[2], grads[3], grads[4], grads[5], grads[6], grads[7], grads[8], grads[9])
```

```python
import functools

import jax
import jax.numpy as jnp
from jax import lax
from jax.experimental import pallas as pl
from jax.experimental.pallas import tpu as pltpu
from jax.sharding import PartitionSpec as P

HEADS = 32
HEAD_DIM = 64
KV_HEADS = 4
EPS = 1e-05
ROPE_BASE = 10000.0
NEG = -1e30
VMEM_LIMIT = 56 * 2**20
BF = jnp.bfloat16
F32 = jnp.float32

NT = (((1,), (1,)), ((), ()))
TN = (((0,), (0,)), ((), ()))
NN = (((1,), (0,)), ((), ()))


def dot(left, right, dims=NN):
    return lax.dot_general(left, right, dims, preferred_element_type=F32)


def params(*semantics):
    return pltpu.CompilerParams(
        dimension_semantics=semantics, vmem_limit_bytes=VMEM_LIMIT
    )


def pick_kernel(which, gain, gate, up, out, *, shards):
    piece = gate.shape[1] // (4 * shards)
    for quarter in range(4):

        @pl.when(which[0] == quarter)
        def _():
            scale = gain[...]
            parts = []
            for source in (gate, up):
                whole = source[...].astype(F32) * scale
                for shard in range(shards):
                    first = (shard * 4 + quarter) * piece
                    parts.append(whole[:, first : first + piece])
            out[...] = jnp.concatenate(parts, axis=1).astype(BF)


def pick_columns(quarter, gain, gate, up, shards):
    rows, width = gate.shape
    return pl.pallas_call(
        functools.partial(pick_kernel, shards=shards),
        out_shape=jax.ShapeDtypeStruct((rows, width // 2), BF),
        in_specs=[
            pl.BlockSpec(memory_space=pltpu.SMEM),
            pl.BlockSpec(memory_space=pltpu.VMEM),
            pl.BlockSpec(memory_space=pltpu.VMEM),
            pl.BlockSpec(memory_space=pltpu.VMEM),
        ],
        out_specs=pl.BlockSpec(memory_space=pltpu.VMEM),
        compiler_params=params(),
        name="pick_columns",
    )(quarter, gain, gate, up)


def spread_kernel(grads, gain, gate, up, gate_out, up_out, gain_out, *, shards):
    half = grads.shape[2] // 2
    piece = half // shards
    total = 0.0
    for source, out, first in ((gate, gate_out, 0), (up, up_out, half)):
        parts = []
        for shard in range(shards):
            for quarter in range(4):
                begin = first + shard * piece
                parts.append(grads[quarter, :, begin : begin + piece].astype(F32))
        whole = jnp.concatenate(parts, axis=1)
        total = total + jnp.sum(
            whole * source[...].astype(F32), axis=1, keepdims=True
        )
        out[...] = whole * gain[...]
    gain_out[...] = total


def spread_columns(grads, gain, gate, up, shards):
    rows, width = gate.shape
    block = min(rows, 64)
    row = lambda cols: pl.BlockSpec((block, cols), lambda i: (i, 0))
    return pl.pallas_call(
        functools.partial(spread_kernel, shards=shards),
        grid=(rows // block,),
        out_shape=(
            jax.ShapeDtypeStruct((rows, width), F32),
            jax.ShapeDtypeStruct((rows, width), F32),
            jax.ShapeDtypeStruct((rows, 1), F32),
        ),
        in_specs=[
            pl.BlockSpec((4, block, width // 2), lambda i: (0, i, 0)),
            row(1),
            row(width),
            row(width),
        ],
        out_specs=(row(width), row(width), row(1)),
        compiler_params=params("arbitrary"),
        name="spread_columns",
    )(grads, gain, gate, up)


def turn(values, cos_t, sin_t):
    lane = lax.broadcasted_iota(jnp.int32, values.shape, 1)
    other = jnp.where(
        lane % 64 < 32, pltpu.roll(values, 96, 1), pltpu.roll(values, 32, 1)
    )
    return values * cos_t + other * sin_t


def project_kernel(x_ref, w_ref, cos_ref, sin_ref, hat_ref, q_ref, kv_ref):
    x = x_ref[...].astype(F32)
    scale = lax.rsqrt(jnp.mean(x * x, axis=1, keepdims=True) + EPS)
    hat = (x * scale).astype(BF)
    hat_ref[...] = hat
    out = dot(hat, w_ref[...])
    cos_t, sin_t = cos_ref[...], sin_ref[...]
    wide = q_ref.shape[1]
    for pair in range(wide // 128):
        part = turn(out[:, pair * 128 : pair * 128 + 128], cos_t, sin_t)
        q_ref[:, pair * 128 : pair * 128 + 128] = (part * HEAD_DIM**-0.5).astype(BF)
    kv = out[:, wide : wide + 128]
    lane = lax.broadcasted_iota(jnp.int32, kv.shape, 1)
    kv_ref[...] = jnp.where(lane < 64, turn(kv, cos_t, sin_t), kv).astype(BF)


def project(x, weight, cos_t, sin_t, rows):
    count, depth = x.shape
    wide = weight.shape[1] - 128
    row = lambda cols: pl.BlockSpec((rows, cols), lambda i: (i, 0))
    return pl.pallas_call(
        project_kernel,
        grid=(count // rows,),
        out_shape=(
            jax.ShapeDtypeStruct((count, depth), BF),
            jax.ShapeDtypeStruct((count, wide), BF),
            jax.ShapeDtypeStruct((count, 128), BF),
        ),
        in_specs=[
            row(depth),
            pl.BlockSpec(weight.shape, lambda i: (0, 0)),
            row(128),
            row(128),
        ],
        out_specs=(row(depth), row(wide), row(128)),
        compiler_params=params("arbitrary"),
        name="project",
    )(x, weight, cos_t, sin_t)


def stack_heads(source, target, rows, upper):
    lane = lax.broadcasted_iota(jnp.int32, (rows, 128), 1)
    keep = (lane >= 64) if upper else (lane < 64)
    for head in range(source.shape[1] // 64):
        slab = source[:, head // 2 * 128 : head // 2 * 128 + 128].astype(F32)
        if (head % 2 == 1) != upper:
            slab = pltpu.roll(slab, 64, 1)
        target[head * rows : head * rows + rows, :] = jnp.where(keep, slab, 0.0).astype(BF)


def allowed(bounds, chunk, rows):
    low = bounds[0:1, :] - chunk * rows
    high = bounds[1:2, :] - chunk * rows
    place = lax.broadcasted_iota(jnp.int32, (rows, bounds.shape[1]), 0)
    return (place >= low) & (place <= high)


def attend_kernel(where, q_ref, kv_ref, bound_ref, out_ref, lse_ref, stacked, *, rows):
    group = pl.program_id(0)
    first, last = where[group], where[4]
    stack_heads(q_ref, stacked, rows, False)
    bounds = bound_ref[0]
    lane = lax.broadcasted_iota(jnp.int32, (rows, 128), 1)
    for pair in range(q_ref.shape[1] // 128):
        queries = stacked[pair * 2 * rows : (pair + 1) * 2 * rows, :]

        def step(chunk, carry):
            top, total, acc = carry
            kv = kv_ref[chunk]
            scores = jnp.where(allowed(bounds, chunk, rows), dot(kv, queries, NT), NEG)
            peak = jnp.maximum(top, jnp.max(scores, axis=0, keepdims=True))
            fade = jnp.exp(top - peak)
            weights = jnp.exp(scores - peak)
            total = total * fade + jnp.sum(weights, axis=0, keepdims=True)
            acc = acc * fade + dot(kv, weights.astype(BF), TN)
            return peak, total, acc

        start = (
            jnp.full((1, 2 * rows), NEG, F32),
            jnp.zeros((1, 2 * rows), F32),
            jnp.zeros((128, 2 * rows), F32),
        )
        top, total, acc = lax.fori_loop(first, last + 1, step, start)
        lse_ref[0, pair : pair + 1, :] = top + jnp.log(total)
        flat = (acc / total).T
        out_ref[:, pair * 128 : pair * 128 + 128] = jnp.where(
            lane < 64, pltpu.roll(flat[:rows], 64, 1), flat[rows:]
        ).astype(BF)


def attend(where, queries, kv, bounds, rows):
    shards = kv.shape[0]
    wide = queries.shape[1]
    pairs = wide // 128
    return pl.pallas_call(
        functools.partial(attend_kernel, rows=rows),
        grid_spec=pltpu.PrefetchScalarGridSpec(
            num_scalar_prefetch=1,
            grid=(4,),
            in_specs=[
                pl.BlockSpec((rows, wide), lambda g, w: (g, 0)),
                pl.BlockSpec((shards, rows, 128), lambda g, w: (0, g, 0)),
                pl.BlockSpec((1, 2, 2 * rows), lambda g, w: (g, 0, 0)),
            ],
            out_specs=(
                pl.BlockSpec((rows, wide), lambda g, w: (g, 0)),
                pl.BlockSpec((1, pairs, 2 * rows), lambda g, w: (g, 0, 0)),
            ),
            scratch_shapes=[pltpu.VMEM((2 * pairs * rows, 128), BF)],
        ),
        out_shape=(
            jax.ShapeDtypeStruct((4 * rows, wide), BF),
            jax.ShapeDtypeStruct((4, pairs, 2 * rows), F32),
        ),
        compiler_params=params("arbitrary"),
        name="attend",
    )(where, queries, kv, bounds)


def attend_back_kernel(
    where,
    q_ref,
    kv_ref,
    bound_ref,
    up_ref,
    out_ref,
    lse_ref,
    cos_ref,
    sin_ref,
    dq_ref,
    dkv_ref,
    stacked,
    upward,
    dq_acc,
    *,
    rows,
):
    group = pl.program_id(0)
    first, last = where[group], where[4]
    shards = kv_ref.shape[0]
    pairs = q_ref.shape[1] // 128
    stack_heads(q_ref, stacked, rows, False)
    stack_heads(up_ref, upward, rows, True)
    bounds = bound_ref[0]
    lane = lax.broadcasted_iota(jnp.int32, (rows, 128), 1)
    deltas = []
    for pair in range(pairs):
        slab = up_ref[:, pair * 128 : pair * 128 + 128].astype(F32)
        slab = slab * out_ref[:, pair * 128 : pair * 128 + 128].astype(F32)
        both = jnp.concatenate(
            [jnp.where(lane < 64, slab, 0.0), jnp.where(lane < 64, 0.0, slab)], axis=0
        )
        deltas.append(jnp.sum(both.T, axis=0, keepdims=True))
        dq_acc[pair] = jnp.zeros((128, 2 * rows), F32)

    def clear(chunk, carry):
        dkv_ref[chunk] = jnp.zeros((rows, 128), BF)
        return carry

    lax.fori_loop(0, first, clear, 0)
    lax.fori_loop(last + 1, shards, clear, 0)

    def step(chunk, carry):
        kv = kv_ref[chunk]
        mask = allowed(bounds, chunk, rows)
        total = jnp.zeros((rows, 128), F32)
        for pair in range(pairs):
            queries = stacked[pair * 2 * rows : (pair + 1) * 2 * rows, :]
            ups = upward[pair * 2 * rows : (pair + 1) * 2 * rows, :]
            scores = dot(kv, queries, NT)
            weights = jnp.where(
                mask, jnp.exp(scores - lse_ref[0, pair : pair + 1, :]), 0.0
            )
            d_scores = (weights * (dot(kv, ups, NT) - deltas[pair])).astype(BF)
            total = total + dot(d_scores, queries) + dot(weights.astype(BF), ups)
            dq_acc[pair] += dot(kv, d_scores, TN)
        dkv_ref[chunk] = total.astype(BF)
        return carry

    lax.fori_loop(first, last + 1, step, 0)
    cos_t, sin_t = cos_ref[...], sin_ref[...]
    for pair in range(pairs):
        flat = dq_acc[pair].T
        slab = jnp.where(lane < 64, flat[:rows], pltpu.roll(flat[rows:], 64, 1))
        dq_ref[:, pair * 128 : pair * 128 + 128] = turn(
            slab * HEAD_DIM**-0.5, cos_t, -sin_t
        ).astype(BF)


def attend_back(where, queries, kv, bounds, upstream, out, lse, cos_t, sin_t, rows):
    shards = kv.shape[0]
    wide = queries.shape[1]
    pairs = wide // 128
    row = lambda cols: pl.BlockSpec((rows, cols), lambda g, w: (g, 0))
    every = pl.BlockSpec((shards, rows, 128), lambda g, w: (0, g, 0))
    return pl.pallas_call(
        functools.partial(attend_back_kernel, rows=rows),
        grid_spec=pltpu.PrefetchScalarGridSpec(
            num_scalar_prefetch=1,
            grid=(4,),
            in_specs=[
                row(wide),
                every,
                pl.BlockSpec((1, 2, 2 * rows), lambda g, w: (g, 0, 0)),
                row(wide),
                row(wide),
                pl.BlockSpec((1, pairs, 2 * rows), lambda g, w: (g, 0, 0)),
                row(128),
                row(128),
            ],
            out_specs=(row(wide), every),
            scratch_shapes=[
                pltpu.VMEM((2 * pairs * rows, 128), BF),
                pltpu.VMEM((2 * pairs * rows, 128), BF),
                pltpu.VMEM((pairs, 128, 2 * rows), F32),
            ],
        ),
        out_shape=(
            jax.ShapeDtypeStruct((4 * rows, wide), BF),
            jax.ShapeDtypeStruct(kv.shape, BF),
        ),
        compiler_params=params("arbitrary"),
        name="attend_back",
    )(where, queries, kv, bounds, upstream, out, lse, cos_t, sin_t)


def hop(value, step):
    return lax.ppermute(value, "dp", [(i, i ^ step) for i in range(4)])


def gather_plane(value):
    half = value.shape[0] // 2
    one = hop(value, 1)
    two = hop(value, 2)
    three = jnp.concatenate([hop(two[:half], 1), hop(one[half:], 2)], axis=0)
    return [value, one, two, three]


def reduce_plane(parts):
    own, one, two, three = parts
    half = own.shape[0] // 2
    by_one = hop(three[:half], 1)
    by_two = hop(three[half:], 2)
    add = lambda a, b: (a.astype(F32) + b.astype(F32)).astype(BF)
    two = jnp.concatenate([add(two[:half], by_one), two[half:]], axis=0)
    one = jnp.concatenate([one[:half], add(one[half:], by_two)], axis=0)
    return own.astype(F32) + hop(one, 1).astype(F32) + hop(two, 2).astype(F32)


def heads_to_tokens(value, rows):
    mine = lax.axis_index("dp")
    parts = [value[:rows]] + [
        hop(value[k * rows : (k + 1) * rows], k) for k in range(1, 4)
    ]
    return in_order(parts, mine, 1)


def in_order(parts, mine, axis):
    one = mine % 2 == 1
    two = mine // 2 == 1
    low = [jnp.where(one, parts[1], parts[0]), jnp.where(one, parts[0], parts[1])]
    high = [jnp.where(one, parts[3], parts[2]), jnp.where(one, parts[2], parts[3])]
    first = [jnp.where(two, b, a) for a, b in zip(low, high, strict=True)]
    second = [jnp.where(two, a, b) for a, b in zip(low, high, strict=True)]
    return jnp.concatenate(first + second, axis=axis)


def tokens_to_heads(value):
    mine = lax.axis_index("dp")
    wide = value.shape[1] // 4
    parts = [
        lax.dynamic_slice_in_dim(value, (mine ^ k) * wide, wide, 1) for k in range(4)
    ]
    return jnp.concatenate(
        [parts[0]] + [hop(parts[k], k) for k in range(1, 4)], axis=0
    )


def local(
    tokens,
    lengths,
    attention_gain,
    query_weight,
    key_weight,
    value_weight,
    output_weight,
    feedforward_gain,
    gate_weight,
    up_weight,
    down_weight,
    cotangent,
):
    rows, depth = tokens.shape
    shards = lax.axis_size("seq")
    mine = lax.axis_index("dp")
    place = lax.axis_index("seq")
    wide = HEADS // KV_HEADS * HEAD_DIM
    near = lambda v: lax.all_gather(v, "seq", axis=0, tiled=True)
    far = lambda v: lax.psum_scatter(v, "seq", scatter_dimension=0, tiled=True)

    gain_a = attention_gain.astype(F32)[:, None]
    gain_f = feedforward_gain.astype(F32)[:, None]
    own_qkv = jnp.concatenate(
        [
            lax.dynamic_slice_in_dim(query_weight, mine * wide, wide, 1),
            lax.dynamic_slice_in_dim(key_weight, mine * HEAD_DIM, HEAD_DIM, 1),
            lax.dynamic_slice_in_dim(value_weight, mine * HEAD_DIM, HEAD_DIM, 1),
        ],
        axis=1,
    )
    w_qkv = near((own_qkv.astype(F32) * gain_a).astype(BF))
    w_out = near(output_weight)
    w_gu = near(pick_columns(mine[None], gain_f, gate_weight, up_weight, shards))
    piece = down_weight.shape[0] // 4
    w_down = near(lax.dynamic_slice_in_dim(down_weight, mine * piece, piece, 0))

    every = lax.all_gather(lengths, "dp", axis=0, tiled=True)
    order = mine ^ jnp.arange(4, dtype=jnp.int32)
    chosen = order[:, None] == jnp.arange(4, dtype=jnp.int32)[None, :]
    sizes = jnp.sum(jnp.where(chosen[:, :, None], every[None], 0), axis=1)
    count = sizes.shape[1]
    before = jnp.arange(count)[:, None] <= jnp.arange(count)[None, :]
    ends = jnp.sum(jnp.where(before[None], sizes[:, :, None], 0), axis=1)
    index = place * rows + jnp.arange(rows, dtype=jnp.int32)
    passed = ends[:, None, :] <= index[None, :, None]
    begin = jnp.max(jnp.where(passed, ends[:, None, :], 0), axis=2)
    position = (index[None, :] - begin).astype(F32).reshape(4 * rows)
    half = HEAD_DIM // 2
    inverse = ROPE_BASE ** (-jnp.arange(half, dtype=F32) * 2.0 / HEAD_DIM)
    theta = position[:, None] * inverse[None, :]
    cos_h, sin_h = jnp.cos(theta), jnp.sin(theta)
    cos_t = jnp.concatenate([cos_h] * 4, axis=1)
    sin_t = jnp.concatenate([-sin_h, sin_h] * 2, axis=1)
    bounds = jnp.stack(
        [begin, jnp.broadcast_to(index[None, :], begin.shape)], axis=1
    )
    bounds = jnp.concatenate([bounds, bounds], axis=2)
    where = jnp.concatenate([begin[:, 0] // rows, place[None]])

    x = jnp.concatenate(gather_plane(tokens), axis=0)
    hat, queries, own_kv = project(x, w_qkv, cos_t, sin_t, rows)
    kv = lax.all_gather(own_kv, "seq", axis=0)
    mixed_heads, lse = attend(where, queries, kv, bounds, rows)
    mixed = heads_to_tokens(mixed_heads, rows)
    middle = tokens.astype(F32) + dot(mixed, w_out)
    scale_two = lax.rsqrt(jnp.mean(middle * middle, axis=1, keepdims=True) + EPS)
    hat_two = (middle * scale_two).astype(BF)

    hats = gather_plane(hat_two)
    dys = gather_plane(cotangent)
    columns = w_gu.shape[1] // 2
    hiddens, d_gus, outs, d_hats = [], [], [], []
    for hat_k, dy_k in zip(hats, dys, strict=True):
        both = dot(hat_k, w_gu)
        gate, up = both[:, :columns], both[:, columns:]
        d_hidden = dot(dy_k, w_down, NT)
        sigma = jax.nn.sigmoid(gate)
        silu = gate * sigma
        hidden = (silu * up).astype(BF)
        d_gate = d_hidden * up * (sigma + silu * (1.0 - sigma))
        d_gu = jnp.concatenate(
            [d_gate.astype(BF), (d_hidden * silu).astype(BF)], axis=1
        )
        hiddens.append(hidden)
        d_gus.append(d_gu)
        d_hats.append(dot(d_gu, w_gu, NT).astype(BF))
    for hidden in hiddens:
        outs.append(dot(hidden, w_down).astype(BF))
    e = reduce_plane(d_hats)
    layer_output = (middle + reduce_plane(outs)).astype(BF)
    hidden_all = jnp.concatenate(hiddens, axis=0)
    d_gu_all = jnp.concatenate(d_gus, axis=0)
    down_part = far(dot(hidden_all, jnp.concatenate(dys, axis=0), TN).astype(BF))
    gu_part = far(dot(jnp.concatenate(hats, axis=0), d_gu_all, TN).astype(BF))

    inner = jnp.mean(e * middle, axis=1, keepdims=True)
    d_middle = (
        cotangent.astype(F32)
        + scale_two * e
        - middle * (scale_two * scale_two * scale_two * inner)
    )
    d_attention = d_middle.astype(BF)

    d_mixed = dot(d_attention, w_out, NT).astype(BF)
    d_heads = tokens_to_heads(d_mixed)
    out_part = far(dot(mixed, d_attention, TN).astype(BF))
    dq, dkv = attend_back(
        where, queries, kv, bounds, d_heads, mixed_heads, lse, cos_t, sin_t, rows
    )
    own_dkv = far(dkv.reshape(shards * 4 * rows, 128)).astype(F32)
    first, second = own_dkv[:, :half], own_dkv[:, half : 2 * half]
    d_qkv = jnp.concatenate(
        [
            dq,
            (first * cos_h + second * sin_h).astype(BF),
            (second * cos_h - first * sin_h).astype(BF),
            own_dkv[:, HEAD_DIM:].astype(BF),
        ],
        axis=1,
    )
    f = reduce_plane(
        [
            dot(d_qkv[k * rows : (k + 1) * rows], w_qkv, NT).astype(BF)
            for k in range(4)
        ]
    )
    qkv_part = far(dot(hat, d_qkv, TN).astype(BF))
    inputs = tokens.astype(F32)
    scale_one = lax.rsqrt(jnp.mean(inputs * inputs, axis=1, keepdims=True) + EPS)
    inner = jnp.mean(f * inputs, axis=1, keepdims=True)
    token_gradient = (
        d_middle
        + scale_one * f
        - inputs * (scale_one * scale_one * scale_one * inner)
    )

    gu_all = lax.all_gather(gu_part, "dp", axis=0)
    gate_gradient, up_gradient, gain_f_gradient = spread_columns(
        gu_all, gain_f, gate_weight, up_weight, shards
    )
    down_gradient = lax.all_gather(down_part, "dp", axis=0, tiled=True).astype(F32)
    output_gradient = lax.psum(out_part, "dp").astype(F32)
    qkv_all = lax.all_gather(qkv_part, "dp", axis=0).astype(F32)
    join = lambda a, b: jnp.concatenate([qkv_all[k, :, a:b] for k in range(4)], axis=1)
    raw_q = join(0, wide)
    raw_k = join(wide, wide + HEAD_DIM)
    raw_v = join(wide + HEAD_DIM, wide + 2 * HEAD_DIM)
    gain_a_gradient = (
        jnp.sum(raw_q * query_weight.astype(F32), axis=1)
        + jnp.sum(raw_k * key_weight.astype(F32), axis=1)
        + jnp.sum(raw_v * value_weight.astype(F32), axis=1)
    )
    return (
        layer_output,
        token_gradient,
        gain_a_gradient,
        raw_q * gain_a,
        raw_k * gain_a,
        raw_v * gain_a,
        output_gradient,
        gain_f_gradient[:, 0],
        gate_gradient,
        up_gradient,
        down_gradient,
    )


def solution(mesh):
    both = P(("dp", "seq"), None)
    flat = P("seq")
    split = P("seq", None)
    return jax.shard_map(
        local,
        mesh=mesh,
        in_specs=(
            both,
            P("dp", None),
            flat,
            split,
            split,
            split,
            split,
            flat,
            split,
            split,
            split,
            both,
        ),
        out_specs=(
            both,
            both,
            flat,
            split,
            split,
            split,
            split,
            flat,
            split,
            split,
            split,
        ),
        check_vma=False,
    )
```

```python
import functools

import jax
import jax.numpy as jnp
from jax import lax
from jax.experimental import pallas as pl
from jax.experimental.pallas import tpu as pltpu
from jax.sharding import PartitionSpec as P

HEADS = 32
HEAD_DIM = 64
KV_HEADS = 4
EPS = 1e-05
ROPE_BASE = 10000.0
NEG = -1e30
TILE_FORTH = 2560
TILE_BACK = 2560
VMEM_LIMIT = 56 * 2**20
BF = jnp.bfloat16
F32 = jnp.float32

NT = (((1,), (1,)), ((), ()))
TN = (((0,), (0,)), ((), ()))
NN = (((1,), (0,)), ((), ()))


def dot(left, right, dims=NN):
    return lax.dot_general(left, right, dims, preferred_element_type=F32)


def params(*semantics):
    return pltpu.CompilerParams(
        dimension_semantics=semantics, vmem_limit_bytes=VMEM_LIMIT
    )


FREE = pl.CostEstimate(flops=1, bytes_accessed=1, transcendentals=0)
TIMES = {
    "project": 2,
    "attend": 400,
    "attend_back": 300,
    "merge": 1,
    "output_product": 3,
    "hidden_back": 4,
    "gate_product": 2,
    "up_gradient": 2,
    "up_product": 60,
    "back_product": 30,
    "down_gradient": 4,
    "gate_gradient": 4,
    "middle_back": 3,
    "down_product": 3,
    "output_gradient": 2,
    "project_back": 2,
    "qkv_gradient": 2,
    "sum_output": 1,
    "sum_tokens": 1,
    "spread_columns": 100,
    "pick_columns": 2,
}


def cost(name):
    time = TIMES[name]
    return pl.CostEstimate(
        flops=int(time * 8e8), bytes_accessed=int(time * 2.5e6), transcendentals=0
    )
ANYWHERE = pl.BlockSpec(memory_space=pl.ANY)
SCALARS = pl.BlockSpec(memory_space=pltpu.SMEM)
INSIDE = pl.BlockSpec(memory_space=pltpu.VMEM)


def array(shape, dtype=BF):
    return jax.ShapeDtypeStruct(tuple(shape), dtype)


def tie(value, *others):
    return pl.pallas_call(
        lambda *refs: None,
        out_shape=array(value.shape, value.dtype),
        in_specs=[ANYWHERE] * (1 + len(others)),
        out_specs=ANYWHERE,
        input_output_aliases={0: 0},
        cost_estimate=FREE,
        name="tie",
    )(value, *others)


def run(body, name, grid, ins, outs, needs=(), scratch=(), aliases=None):
    count, made = len(ins), len(outs)

    def kernel(*refs):
        body(refs[:count], refs[count + len(needs) :][:made], refs[count + len(needs) + made :])

    result = pl.pallas_call(
        kernel,
        grid=grid,
        out_shape=tuple(shape for shape, _ in outs),
        in_specs=[spec for _, spec in ins] + [ANYWHERE] * len(needs),
        out_specs=tuple(spec for _, spec in outs),
        scratch_shapes=list(scratch),
        input_output_aliases=aliases or {},
        compiler_params=params(*["arbitrary"] * len(grid)),
        cost_estimate=cost(name),
        name=name,
    )(*[value for value, _ in ins], *needs)
    return result


def whole(shape):
    return pl.BlockSpec(tuple(shape), lambda i: (0,) * len(shape), pipeline_mode=pl.Buffered(1))


def down_rows(rows, cols, at=None):
    return pl.BlockSpec((rows, cols), (lambda i: (i, 0)) if at is None else (lambda i: (at, 0)))


def along_cols(rows, cols, at=0):
    return pl.BlockSpec((rows, cols), lambda i: (at, i))


def pick_kernel(which, gain, gate, up, gate_out, up_out, *, shards):
    piece = gate.shape[1] // (4 * shards)
    scale = gain[...]
    for quarter in range(4):

        @pl.when(which[0] == quarter)
        def _():
            for source, out in ((gate, gate_out), (up, up_out)):
                whole = source[...].astype(F32) * scale
                parts = []
                for shard in range(shards):
                    first = (shard * 4 + quarter) * piece
                    parts.append(whole[:, first : first + piece])
                out[...] = jnp.concatenate(parts, axis=1).astype(BF)


def pick_columns(quarter, gain, gate, up, shards):
    rows, width = gate.shape
    vmem = pl.BlockSpec(memory_space=pltpu.VMEM)
    shape = jax.ShapeDtypeStruct((rows, width // 4), BF)
    return pl.pallas_call(
        functools.partial(pick_kernel, shards=shards),
        out_shape=(shape, shape),
        in_specs=[pl.BlockSpec(memory_space=pltpu.SMEM), vmem, vmem, vmem],
        out_specs=(vmem, vmem),
        compiler_params=params(),
        cost_estimate=cost("pick_columns"),
        name="pick_columns",
    )(quarter, gain, gate, up)


def spread_kernel(which, grads, gain, weight, out, gain_out, *, shards):
    piece = grads.shape[2] // shards
    chunks = [grads[which[0] ^ quarter].astype(F32) for quarter in range(4)]
    whole = jnp.concatenate(
        [
            chunks[quarter][:, shard * piece : (shard + 1) * piece]
            for shard in range(shards)
            for quarter in range(4)
        ],
        axis=1,
    )
    gain_out[...] = jnp.sum(whole * weight[...].astype(F32), axis=1, keepdims=True)
    out[...] = whole * gain[...]


def spread_columns(mine, grads, gain, weight, shards):
    rows, width = weight.shape
    block = min(rows, 64)
    row = lambda cols: pl.BlockSpec((block, cols), lambda i: (i, 0))
    return pl.pallas_call(
        functools.partial(spread_kernel, shards=shards),
        grid=(rows // block,),
        out_shape=(
            jax.ShapeDtypeStruct((rows, width), F32),
            jax.ShapeDtypeStruct((rows, 1), F32),
        ),
        in_specs=[
            pl.BlockSpec(memory_space=pltpu.SMEM),
            pl.BlockSpec((4, block, width // 4), lambda i: (0, i, 0)),
            row(1),
            row(width),
        ],
        out_specs=(row(width), row(1)),
        compiler_params=params("arbitrary"),
        cost_estimate=cost("spread_columns"),
        name="spread_columns",
    )(mine, grads, gain, weight)


def turn(values, cos_t, sin_t):
    lane = lax.broadcasted_iota(jnp.int32, values.shape, 1)
    other = jnp.where(
        lane % 64 < 32, pltpu.roll(values, 96, 1), pltpu.roll(values, 32, 1)
    )
    return values * cos_t + other * sin_t


def project_kernel(ins, outs, _):
    *xs, w_ref, cos_ref, sin_ref = ins
    hat_ref, q_ref, kv_ref = outs
    rows = hat_ref.shape[0] // len(xs)
    for i, x_ref in enumerate(xs):
        span = slice(i * rows, (i + 1) * rows)
        x = x_ref[...].astype(F32)
        scale = lax.rsqrt(jnp.mean(x * x, axis=1, keepdims=True) + EPS)
        hat_ref[span, :] = (x * scale).astype(BF)
    out = dot(hat_ref[...], w_ref[...])
    cos_t, sin_t = cos_ref[...], sin_ref[...]
    wide = q_ref.shape[1]
    for pair in range(wide // 128):
        part = turn(out[:, pair * 128 : pair * 128 + 128], cos_t, sin_t)
        q_ref[:, pair * 128 : pair * 128 + 128] = (part * HEAD_DIM**-0.5).astype(BF)
    kv = out[:, wide : wide + 128]
    lane = lax.broadcasted_iota(jnp.int32, kv.shape, 1)
    kv_ref[...] = jnp.where(lane < 64, turn(kv, cos_t, sin_t), kv).astype(BF)


def project(chunk, xs, weight, cos_t, sin_t, rows, before=()):
    depth, wide = weight.shape[0], weight.shape[1] - 128
    ins = [(x, whole(x.shape)) for x in xs] + [
        (weight, whole(weight.shape)),
        (cos_t, down_rows(rows, 128, chunk)),
        (sin_t, down_rows(rows, 128, chunk)),
    ]

    def body(refs, outs, scratch):
        project_kernel(refs[: len(xs) + 3], outs, scratch)

    first = len(ins)
    return run(
        body,
        "project",
        (1,),
        ins + [(b, ANYWHERE) for b in before],
        [
            (array((4 * rows, cols)), down_rows(rows, cols, chunk))
            for cols in (depth, wide, 128)
        ],
        aliases={first + i: i for i in range(len(before))},
    )


def stack_heads(source, target, rows, upper):
    lane = lax.broadcasted_iota(jnp.int32, (rows, 128), 1)
    keep = (lane >= 64) if upper else (lane < 64)
    for head in range(source.shape[1] // 64):
        slab = source[:, head // 2 * 128 : head // 2 * 128 + 128].astype(F32)
        if (head % 2 == 1) != upper:
            slab = pltpu.roll(slab, 64, 1)
        target[head * rows : head * rows + rows, :] = jnp.where(keep, slab, 0.0).astype(BF)


def allowed(bounds, chunk, rows):
    low = bounds[0:1, :] - chunk * rows
    high = bounds[1:2, :] - chunk * rows
    place = lax.broadcasted_iota(jnp.int32, (rows, bounds.shape[1]), 0)
    return (place >= low) & (place <= high)


def over_chunks(where, step):
    group = pl.program_id(0)
    first, split, last = where[group], where[4 + group], where[8]
    edge = split - first

    def edges(i, carry):
        step(jnp.where(i < edge, first + i, last), True)
        return carry

    def inner(chunk, carry):
        step(chunk, False)
        return carry

    lax.fori_loop(split, last, inner, 0)
    lax.fori_loop(0, edge + 1, edges, 0)


def tiles_of(width, tile):
    return [slice(i, i + tile) for i in range(0, width, tile)]


def attend_kernel(where, q_ref, kv_ref, bound_ref, *rest, rows):
    out_ref, lse_ref, stacked, tops, totals, accs = rest[-6:]
    pairs = q_ref.shape[1] // 128
    stack_heads(q_ref, stacked, rows, False)
    lane = lax.broadcasted_iota(jnp.int32, (rows, 128), 1)
    tops[...] = jnp.full(tops.shape, NEG, F32)
    totals[...] = jnp.zeros(totals.shape, F32)
    accs[...] = jnp.zeros(accs.shape, F32)

    def step(chunk, masked):
        kv = kv_ref[chunk]
        for tile in tiles_of(2 * pairs * rows, TILE_FORTH):
            scores = dot(kv, stacked[tile, :], NT)
            if masked:
                mask = allowed(bound_ref[0, :, tile], chunk, rows)
                scores = jnp.where(mask, scores, NEG)
            top = tops[:, tile]
            peak = jnp.maximum(top, jnp.max(scores, axis=0, keepdims=True))
            fade = jnp.exp(top - peak)
            weights = jnp.exp(scores - peak)
            tops[:, tile] = peak
            totals[:, tile] = totals[:, tile] * fade + jnp.sum(
                weights, axis=0, keepdims=True
            )
            accs[:, tile] = accs[:, tile] * fade + dot(kv, weights.astype(BF), TN)[64:128]

    over_chunks(where, step)
    lse_ref[0] = tops[...] + jnp.log(totals[...])
    for pair in range(pairs):
        both = slice(pair * 2 * rows, (pair + 1) * 2 * rows)
        half = accs[:, both] / totals[:, both]
        flat = jnp.concatenate([half, half], axis=0).T
        out_ref[:, pair * 128 : pair * 128 + 128] = jnp.where(
            lane < 64, flat[:rows], flat[rows:]
        ).astype(BF)


def attend(where, queries, kv, bounds, rows, needs=()):
    shards = kv.shape[0]
    wide = queries.shape[1]
    lanes = wide // 64 * rows
    return pl.pallas_call(
        functools.partial(attend_kernel, rows=rows),
        grid_spec=pltpu.PrefetchScalarGridSpec(
            num_scalar_prefetch=1,
            grid=(4,),
            in_specs=[
                pl.BlockSpec((rows, wide), lambda g, w: (g, 0)),
                pl.BlockSpec((shards, rows, 128), lambda g, w: (0, g, 0)),
                pl.BlockSpec((1, 2, lanes), lambda g, w: (g, 0, 0)),
                *[ANYWHERE] * len(needs),
            ],
            out_specs=(
                pl.BlockSpec((rows, wide), lambda g, w: (g, 0)),
                pl.BlockSpec((1, 1, lanes), lambda g, w: (g, 0, 0)),
            ),
            scratch_shapes=[
                pltpu.VMEM((lanes, 128), BF),
                pltpu.VMEM((1, lanes), F32),
                pltpu.VMEM((1, lanes), F32),
                pltpu.VMEM((64, lanes), F32),
            ],
        ),
        out_shape=(
            jax.ShapeDtypeStruct((4 * rows, wide), BF),
            jax.ShapeDtypeStruct((4, 1, lanes), F32),
        ),
        compiler_params=params("arbitrary"),
        cost_estimate=cost("attend"),
        name="attend",
    )(where, queries, kv, bounds, *needs)


def attend_back_kernel(
    where,
    q_ref,
    kv_ref,
    bound_ref,
    up_ref,
    out_ref,
    lse_ref,
    cos_ref,
    sin_ref,
    *rest,
    rows,
):
    dq_ref, dkv_ref, stacked, upward, dq_acc, deltas = rest[-6:]
    group = pl.program_id(0)
    first, last = where[group], where[8]
    shards = kv_ref.shape[0]
    pairs = q_ref.shape[1] // 128
    stack_heads(q_ref, stacked, rows, False)
    stack_heads(up_ref, upward, rows, True)
    lane = lax.broadcasted_iota(jnp.int32, (rows, 128), 1)
    for pair in range(pairs):
        slab = up_ref[:, pair * 128 : pair * 128 + 128].astype(F32)
        slab = slab * out_ref[:, pair * 128 : pair * 128 + 128].astype(F32)
        both = jnp.concatenate(
            [jnp.where(lane < 64, slab, 0.0), jnp.where(lane < 64, 0.0, slab)], axis=0
        )
        deltas[:, pair * 2 * rows : (pair + 1) * 2 * rows] = jnp.sum(
            both.T, axis=0, keepdims=True
        )
    dq_acc[...] = jnp.zeros(dq_acc.shape, F32)

    def clear(chunk, carry):
        dkv_ref[chunk] = jnp.zeros((rows, 128), BF)
        return carry

    lax.fori_loop(0, first, clear, 0)
    lax.fori_loop(last + 1, shards, clear, 0)

    def step(chunk, masked):
        kv = kv_ref[chunk]
        total = jnp.zeros((rows, 128), F32)
        for tile in tiles_of(2 * pairs * rows, TILE_BACK):
            queries = stacked[tile, :]
            ups = upward[tile, :]
            weights = jnp.exp(dot(kv, queries, NT) - lse_ref[0, :, tile])
            if masked:
                mask = allowed(bound_ref[0, :, tile], chunk, rows)
                weights = jnp.where(mask, weights, 0.0)
            d_scores = (weights * (dot(kv, ups, NT) - deltas[:, tile])).astype(BF)
            total = total + dot(d_scores, queries) + dot(weights.astype(BF), ups)
            dq_acc[:, tile] += dot(kv, d_scores, TN)[0:64]
        dkv_ref[chunk] = total.astype(BF)

    over_chunks(where, step)
    cos_t, sin_t = cos_ref[...], sin_ref[...]
    for pair in range(pairs):
        half = dq_acc[:, pair * 2 * rows : (pair + 1) * 2 * rows]
        flat = jnp.concatenate([half, half], axis=0).T
        slab = jnp.where(lane < 64, flat[:rows], flat[rows:])
        dq_ref[:, pair * 128 : pair * 128 + 128] = turn(
            slab * HEAD_DIM**-0.5, cos_t, -sin_t
        ).astype(BF)


def attend_back(
    where, queries, kv, bounds, upstream, out, lse, cos_t, sin_t, rows, needs=()
):
    shards = kv.shape[0]
    wide = queries.shape[1]
    lanes = wide // 64 * rows
    row = lambda cols: pl.BlockSpec((rows, cols), lambda g, w: (g, 0))
    every = pl.BlockSpec((shards, rows, 128), lambda g, w: (0, g, 0))
    line = lambda count: pl.BlockSpec((1, count, lanes), lambda g, w: (g, 0, 0))
    return pl.pallas_call(
        functools.partial(attend_back_kernel, rows=rows),
        grid_spec=pltpu.PrefetchScalarGridSpec(
            num_scalar_prefetch=1,
            grid=(4,),
            in_specs=[
                row(wide),
                every,
                line(2),
                row(wide),
                row(wide),
                line(1),
                row(128),
                row(128),
                *[ANYWHERE] * len(needs),
            ],
            out_specs=(row(wide), every),
            scratch_shapes=[
                pltpu.VMEM((lanes, 128), BF),
                pltpu.VMEM((lanes, 128), BF),
                pltpu.VMEM((64, lanes), F32),
                pltpu.VMEM((1, lanes), F32),
            ],
        ),
        out_shape=(
            jax.ShapeDtypeStruct((4 * rows, wide), BF),
            jax.ShapeDtypeStruct(kv.shape, BF),
        ),
        compiler_params=params("arbitrary"),
        cost_estimate=cost("attend_back"),
        name="attend_back",
    )(where, queries, kv, bounds, upstream, out, lse, cos_t, sin_t, *needs)


def row_product(name, left, right, dims, block, needs=()):
    total = left.shape[1] if dims is TN else left.shape[0]
    cols = right.shape[0] if dims is NT else right.shape[1]
    spec = (
        along_cols(left.shape[0], block) if dims is TN else down_rows(block, left.shape[1])
    )

    def body(ins, outs, _):
        outs[0][...] = dot(ins[0][...], ins[1][...], dims).astype(BF)

    return run(
        body,
        name,
        (total // block,),
        [(left, spec), (right, whole(right.shape))],
        [(array((total, cols)), down_rows(block, cols))],
        needs,
    )[0]


def column_product(name, left, right, dims, block, needs=()):
    total = left.shape[1] if dims is TN else left.shape[0]
    cols = right.shape[0] if dims is NT else right.shape[1]
    spec = (
        down_rows(block, right.shape[1]) if dims is NT else along_cols(right.shape[0], block)
    )

    def body(ins, outs, _):
        outs[0][...] = dot(ins[0][...], ins[1][...], dims).astype(BF)

    return run(
        body,
        name,
        (cols // block,),
        [(left, whole(left.shape)), (right, spec)],
        [(array((total, cols)), along_cols(total, block))],
        needs,
    )[0]


def gate_product(hat, w_gate, d_hidden, rows):
    columns = w_gate.shape[1]

    def body(ins, outs, _):
        gate = dot(ins[0][...], ins[1][...])
        outs[0][...] = gate.astype(BF)
        outs[1][...] = (ins[2][...].astype(F32) * gate * jax.nn.sigmoid(gate)).astype(BF)

    return run(
        body,
        "gate_product",
        (4,),
        [
            (hat, down_rows(rows, hat.shape[1])),
            (w_gate, whole(w_gate.shape)),
            (d_hidden, down_rows(rows, columns)),
        ],
        [(array((4 * rows, columns)), down_rows(rows, columns))] * 2,
    )


def up_product(hat, w_up, gate, d_hidden, rows, needs):
    columns = w_up.shape[1]

    def body(ins, outs, _):
        up = dot(ins[0][...], ins[1][...])
        gate = ins[2][...].astype(F32)
        sigma = jax.nn.sigmoid(gate)
        silu = gate * sigma
        outs[0][...] = (silu * up).astype(BF)
        slope = sigma + silu * (1.0 - sigma)
        outs[1][...] = (ins[3][...].astype(F32) * up * slope).astype(BF)

    return run(
        body,
        "up_product",
        (4,),
        [
            (hat, down_rows(rows, hat.shape[1])),
            (w_up, whole(w_up.shape)),
            (gate, down_rows(rows, columns)),
            (d_hidden, down_rows(rows, columns)),
        ],
        [(array((4 * rows, columns)), down_rows(rows, columns))] * 2,
        needs,
    )


def chunk_outs(chunks, rows, cols, block):
    outs = []
    for k in chunks:
        parts = 2 if k == 3 else 1
        outs += [(array((rows // parts, cols)), along_cols(rows // parts, block))] * parts
    return outs


def put_chunk(outs, value):
    rows = outs[0].shape[0]
    if rows == value.shape[0]:
        outs[0][...] = value.astype(BF)
        return outs[1:]
    outs[0][...] = value[:rows].astype(BF)
    outs[1][...] = value[rows:].astype(BF)
    return outs[2:]


def back_product(chunks, d_gate, d_up, w_gate, w_up, rows, needs=()):
    depth, columns = w_gate.shape
    block = depth // 4
    count = len(chunks)

    def body(ins, outs, _):
        w_one, w_two = ins[2 * count][...], ins[2 * count + 1][...]
        left = outs
        for i in range(count):
            left = put_chunk(
                left, dot(ins[i][...], w_one, NT) + dot(ins[count + i][...], w_two, NT)
            )

    return run(
        body,
        "back_product",
        (depth // block,),
        [(d_gate, down_rows(rows, columns, k)) for k in chunks]
        + [(d_up, down_rows(rows, columns, k)) for k in chunks]
        + [(w_gate, down_rows(block, columns)), (w_up, down_rows(block, columns))],
        chunk_outs(chunks, rows, depth, block),
        needs,
    )


def down_product(hidden, w_down, rows, needs):
    columns, depth = w_down.shape
    block = depth // 4

    def body(ins, outs, _):
        left = outs
        for k in range(4):
            left = put_chunk(left, dot(ins[0][k * rows : (k + 1) * rows, :], ins[1][...]))

    return run(
        body,
        "down_product",
        (4,),
        [(hidden, whole(hidden.shape)), (w_down, along_cols(columns, block))],
        chunk_outs(range(4), rows, depth, block),
        needs,
    )


def output_product(spot, mixes, w_outs, tokens):
    rows, depth = tokens.shape
    quarter, side = depth // 4, depth // 2
    flat = [w for pair in w_outs for w in pair]

    def body(ins, outs, _):
        mine, core = ins[0][0], ins[0][1]
        mix, weights, x = ins[1:5], ins[5:13], ins[13]
        mixed, middle, hat = outs
        place = lambda k: pl.ds(pl.multiple_of((mine ^ k) * quarter, 128), quarter)
        for k in range(4):
            mixed[:, place(k)] = mix[k][...]
        near = mixed[:, pl.ds(pl.multiple_of(core * side, 128), side)]
        other = mixed[:, pl.ds(pl.multiple_of((1 - core) * side, 128), side)]
        for k in range(4):
            part = dot(near, weights[2 * k][...]) + dot(other, weights[2 * k + 1][...])
            middle[:, place(k)] = part + x[:, place(k)].astype(F32)
        value = middle[...]
        scale = lax.rsqrt(jnp.mean(value * value, axis=1, keepdims=True) + EPS)
        hat[...] = (value * scale).astype(BF)

    return run(
        body,
        "output_product",
        (),
        [(spot, SCALARS)] + [(v, INSIDE) for v in (*mixes, *flat, tokens)],
        [
            (array((rows, depth)), INSIDE),
            (array((rows, depth), F32), INSIDE),
            (array((rows, depth)), INSIDE),
        ],
    )


def norm_back(upstream, value):
    scale = lax.rsqrt(jnp.mean(value * value, axis=1, keepdims=True) + EPS)
    inner = jnp.mean(upstream * value, axis=1, keepdims=True)
    return scale * upstream - value * (scale * scale * scale * inner)


def middle_back(spot, parts, middle, dy, w_outs, needs):
    rows, depth = middle.shape
    quarter, side = depth // 4, depth // 2
    flat = [w for pair in w_outs for w in pair]

    def body(ins, outs, scratch):
        mine, core = ins[0][0], ins[0][1]
        one, two, three, value, grad = ins[1:6]
        weights = ins[6:14]
        d_mixed, d_all = scratch
        upstream = one[...].astype(F32) + two[...].astype(F32) + three[...].astype(F32)
        d_middle = grad[...].astype(F32) + norm_back(upstream, value[...])
        outs[0][...] = d_middle
        d_all[...] = d_middle.astype(BF)
        place = lambda k: pl.ds(pl.multiple_of((mine ^ k) * quarter, 128), quarter)
        near, other = 0.0, 0.0
        for k in range(4):
            part = d_all[:, place(k)]
            outs[1 + k][...] = part
            near = near + dot(part, weights[2 * k][...], NT)
            other = other + dot(part, weights[2 * k + 1][...], NT)
        d_mixed[:, pl.ds(pl.multiple_of(core * side, 128), side)] = near.astype(BF)
        d_mixed[:, pl.ds(pl.multiple_of((1 - core) * side, 128), side)] = other.astype(BF)
        for k in range(4):
            outs[5 + k][...] = d_mixed[:, place(k)]

    return run(
        body,
        "middle_back",
        (),
        [(spot, SCALARS)] + [(v, INSIDE) for v in (*parts, middle, dy, *flat)],
        [(array((rows, depth), F32), INSIDE)] + [(array((rows, quarter)), INSIDE)] * 8,
        needs,
        [pltpu.VMEM((rows, depth), BF), pltpu.VMEM((rows, depth), BF)],
    )


def project_back(dq, d_kv, cos_t, sin_t, weight, rows, needs):
    depth, wide = weight.shape
    block = depth // 4

    def body(ins, outs, _):
        dq_ref, kv_ref, cos_ref, sin_ref, w_ref = ins
        joined = outs[0]

        @pl.when(pl.program_id(0) == 0)
        def _():
            joined[:, : wide - 128] = dq_ref[...]
            values = kv_ref[...].astype(F32)
            lane = lax.broadcasted_iota(jnp.int32, values.shape, 1)
            turned = turn(values, cos_ref[...], -sin_ref[...])
            joined[:, wide - 128 :] = jnp.where(lane < 64, turned, values).astype(BF)

        left = outs[1:]
        for k in range(4):
            left = put_chunk(
                left, dot(joined[k * rows : (k + 1) * rows, :], w_ref[...], NT)
            )

    return run(
        body,
        "project_back",
        (4,),
        [(v, whole(v.shape)) for v in (dq, d_kv, cos_t, sin_t)]
        + [(weight, down_rows(block, wide))],
        [(array((4 * rows, wide)), whole((4 * rows, wide)))]
        + chunk_outs(range(4), rows, depth, block),
        needs,
    )


def sum_output(parts, middle, rows, needs):
    def body(ins, outs, _):
        one, two, three, value = (r[...].astype(F32) for r in ins)
        outs[0][...] = (one + two + three + value).astype(BF)

    block = rows // 4
    spec = down_rows(block, middle.shape[1])
    return run(
        body,
        "sum_output",
        (4,),
        [(v, spec) for v in (*parts, middle)],
        [(array(middle.shape), spec)],
        needs,
    )[0]


def sum_tokens(parts, tokens, d_middle, rows, needs=()):
    def body(ins, outs, _):
        one, two, three, value, grad = (r[...].astype(F32) for r in ins)
        outs[0][...] = grad + norm_back(one + two + three, value)

    block = rows // 4
    spec = down_rows(block, tokens.shape[1])
    return run(
        body,
        "sum_tokens",
        (4,),
        [(v, spec) for v in (*parts, tokens, d_middle)],
        [(array(tokens.shape, F32), spec)],
        needs,
    )[0]


def hop(value, step):
    return lax.ppermute(value, "dp", [(i, i ^ step) for i in range(4)])


def gather_plane(value, hold=None, start=None):
    half = value.shape[0] // 2
    one = hop(value, 1)
    two = hop(value, 2)
    if hold is not None:
        one, two = tie(one, *hold), tie(two, *hold)
    return [value, one, two, hop(two[:half], 1), hop(one[half:], 2)]


def join(parts):
    return jnp.concatenate(parts, axis=0)


def gather_direct(value):
    return [value] + [hop(value, k) for k in range(1, 4)]


def merge(one, two, by_one, by_two):
    def body(ins, outs, _):
        half = ins[2].shape[0]
        add = lambda a, b: (a.astype(F32) + b.astype(F32)).astype(BF)
        outs[0][:half, :] = ins[0][:half, :]
        outs[0][half:, :] = add(ins[0][half:, :], ins[3][...])
        outs[1][:half, :] = add(ins[1][:half, :], ins[2][...])
        outs[1][half:, :] = ins[1][half:, :]

    return run(
        body,
        "merge",
        (),
        [(v, INSIDE) for v in (one, two, by_one, by_two)],
        [(array(one.shape), INSIDE)] * 2,
    )


def core_swap(value):
    size = lax.axis_size("seq")
    return lax.ppermute(value, "seq", [(i, i ^ 1) for i in range(size)])


def in_order(parts, axis, dtype=None):
    mine = lax.axis_index("dp")
    shape = list(parts[0].shape)
    size = shape[axis]
    shape[axis] = 4 * size
    out = jnp.zeros(shape, dtype or parts[0].dtype)
    for k, part in enumerate(parts):
        out = lax.dynamic_update_slice_in_dim(
            out, part.astype(out.dtype), (mine ^ k) * size, axis
        )
    return out


def local(
    tokens,
    lengths,
    attention_gain,
    query_weight,
    key_weight,
    value_weight,
    output_weight,
    feedforward_gain,
    gate_weight,
    up_weight,
    down_weight,
    cotangent,
):
    rows, depth = tokens.shape
    shards = lax.axis_size("seq")
    mine = lax.axis_index("dp")
    place = lax.axis_index("seq")
    core = place % 2
    spot = jnp.stack([mine, core])
    wide = HEADS // KV_HEADS * HEAD_DIM
    side = depth // 2
    near = lambda v: lax.all_gather(v, "seq", axis=0, tiled=True)
    far = lambda v: lax.psum_scatter(v, "seq", scatter_dimension=0, tiled=True)

    gain_a = attention_gain.astype(F32)[:, None]
    gain_f = feedforward_gain.astype(F32)[:, None]
    own_qkv = jnp.concatenate(
        [
            lax.dynamic_slice_in_dim(query_weight, mine * wide, wide, 1),
            lax.dynamic_slice_in_dim(key_weight, mine * HEAD_DIM, HEAD_DIM, 1),
            lax.dynamic_slice_in_dim(value_weight, mine * HEAD_DIM, HEAD_DIM, 1),
        ],
        axis=1,
    )
    w_qkv = near((own_qkv.astype(F32) * gain_a).astype(BF))
    own_out = near(
        lax.dynamic_slice_in_dim(output_weight, mine * (depth // 4), depth // 4, 1)
    )
    piece = down_weight.shape[0] // 4
    w_down = near(lax.dynamic_slice_in_dim(down_weight, mine * piece, piece, 0))
    own_gate, own_up = pick_columns(mine[None], gain_f, gate_weight, up_weight, shards)
    w_gate = near(own_gate)
    w_up = near(own_up)

    sizes = join([lengths] + [hop(lengths, k) for k in range(1, 4)])
    count = sizes.shape[1]
    before = jnp.arange(count)[:, None] <= jnp.arange(count)[None, :]
    ends = jnp.sum(jnp.where(before[None], sizes[:, :, None], 0), axis=1)
    index = place * rows + jnp.arange(rows, dtype=jnp.int32)
    passed = ends[:, None, :] <= index[None, :, None]
    begin = jnp.max(jnp.where(passed, ends[:, None, :], 0), axis=2)
    position = (index[None, :] - begin).astype(F32).reshape(4 * rows)
    half = HEAD_DIM // 2
    inverse = ROPE_BASE ** (-jnp.arange(half, dtype=F32) * 2.0 / HEAD_DIM)
    theta = position[:, None] * inverse[None, :]
    cos_h, sin_h = jnp.cos(theta), jnp.sin(theta)
    cos_t = jnp.concatenate([cos_h] * 4, axis=1)
    sin_t = jnp.concatenate([-sin_h, sin_h] * 2, axis=1)
    bounds = jnp.stack([begin, jnp.broadcast_to(index[None, :], begin.shape)], axis=1)
    bounds = jnp.concatenate([bounds] * (wide // HEAD_DIM), axis=2)
    first = begin[:, 0] // rows
    split = jnp.clip((begin[:, rows - 1] + rows - 1) // rows, first, place)
    where = jnp.concatenate([first, split, place[None]])

    xs = gather_plane(tokens)
    made = ()
    for k, pieces in enumerate((xs[0:1], xs[1:2], xs[2:3], xs[3:5])):
        made = project(k, pieces, w_qkv, cos_t, sin_t, rows, made)
    hat, queries, own_kv = made
    kv = lax.all_gather(own_kv, "seq", axis=0)
    dy_one, dy_two = (hop(tie(cotangent, xs[3], xs[4]), k) for k in (1, 2))
    halves = lambda value: [
        lax.dynamic_slice_in_dim(value, c * side, side, 0) for c in (core, 1 - core)
    ]
    own_pair = halves(own_out)
    got = gather_direct(tie(own_pair[0], dy_one, dy_two))[1:]
    mixed_heads, lse = attend(where, queries, kv, bounds, rows, (dy_one, dy_two))
    part = rows // 2
    dy_far = [hop(dy_two[:part], 1), hop(dy_one[part:], 2)]
    mixed_heads = tie(mixed_heads, *dy_far, *got)
    got = [tie(g, mixed_heads) for g in got]
    w_outs = [own_pair] + [(g, core_swap(g)) for g in got]
    mixes = [mixed_heads[:rows]] + [
        hop(mixed_heads[k * rows : (k + 1) * rows], k) for k in range(1, 4)
    ]
    mixed, middle, hat_two = output_product(spot, mixes, w_outs, tokens)

    dy_all = join([cotangent, dy_one, dy_two, *dy_far])
    d_hidden = row_product("hidden_back", dy_all, w_down, NT, rows, (hat_two,))
    hats = gather_plane(hat_two, (d_hidden,))
    hat_all = join(hats)
    mixes_all = gather_plane(tie(mixed, hats[3], hats[4]))
    gate, d_up = gate_product(hat_all, w_gate, d_hidden, rows)
    up_raw = row_product("up_gradient", hat_all, d_up, TN, wide)
    up_part = far(up_raw)
    hidden, d_gate = up_product(
        hat_all, w_up, gate, d_hidden, rows, (up_raw, mixes_all[1], mixes_all[2])
    )
    back = functools.partial(
        back_product, d_gate=d_gate, d_up=d_up, w_gate=w_gate, w_up=w_up, rows=rows
    )
    far_one, far_two = back((3,))
    by_one, by_two = hop(far_one, 1), hop(far_two, 2)
    d_one, d_two = back((1, 2), needs=(far_one, mixes_all[3], mixes_all[4]))
    (d_own,) = back((0,), needs=(d_one,))
    to_one, to_two = merge(d_one, d_two, by_one, by_two)
    down_raw = column_product("down_gradient", hidden, dy_all, TN, wide, (to_one, d_own))
    gate_raw = row_product("gate_gradient", hat_all, d_gate, TN, wide, (down_raw,))
    down_part = far(down_raw)
    gate_part = far(gate_raw)
    mixed_all = join(mixes_all)
    d_middle, *blocks = middle_back(
        spot,
        (d_own, hop(to_one, 1), hop(to_two, 2)),
        middle,
        cotangent,
        w_outs,
        (gate_raw, up_part, mixed_all),
    )
    d_attention, d_mixes = blocks[:4], blocks[4:]

    d_heads = join([d_mixes[0]] + [hop(d_mixes[k], k) for k in range(1, 4)])
    outs = down_product(hidden, w_down, rows, (d_mixes[0],))
    outs_one, outs_two = hop(outs[3], 1), hop(outs[4], 2)
    d_attention = [d_attention[0]] + [
        hop(tie(d_attention[k], outs[4]), k) for k in range(1, 4)
    ]
    ups = gather_direct(up_part)
    dq, dkv = attend_back(
        where, queries, kv, bounds, d_heads, mixed_heads, lse, cos_t, sin_t, rows, (outs[4],)
    )
    dkv = tie(
        dkv, down_part, gate_part, outs_one, outs_two, *d_attention[1:], *ups[1:]
    )
    own_dkv = far(dkv.reshape(shards * 4 * rows, 128))
    to_one, to_two = merge(outs[1], outs[2], outs_one, tie(outs_two, dkv))
    outs = (outs[0], hop(to_one, 1), hop(to_two, 2))
    d_attention[0] = tie(d_attention[0], to_one)
    out_raw = row_product("output_gradient", mixed_all, join(d_attention), TN, wide)
    own_dkv = tie(own_dkv, out_raw)
    out_part = far(tie(out_raw, own_dkv))
    downs_one, downs_two = (hop(tie(down_part, to_one), k) for k in (1, 2))
    d_qkv, *fs = project_back(
        dq, own_dkv, cos_t, sin_t, w_qkv, rows, (*outs[1:], downs_one, downs_two)
    )
    layer_output = sum_output(outs, middle, rows, (fs[4],))
    f_one, f_two = hop(fs[3], 1), hop(fs[4], 2)
    qkv_raw = row_product("qkv_gradient", hat, d_qkv, TN, wide, (fs[4],))
    qkv_part = far(qkv_raw)
    to_one, to_two = merge(fs[1], fs[2], f_one, f_two)
    half_piece = piece // 2
    downs = [
        down_part,
        downs_one,
        downs_two,
        hop(tie(downs_two[:half_piece], to_one), 1),
        hop(tie(downs_one[half_piece:], to_one), 2),
    ]
    gates = gather_plane(tie(gate_part, to_one))
    token_gradient = sum_tokens(
        (fs[0], hop(to_one, 1), hop(to_two, 2)), tokens, d_middle, rows
    )

    gate_gradient, gain_g = spread_columns(
        mine[None],
        jnp.stack([*gates[:3], join(gates[3:])]),
        gain_f,
        gate_weight,
        shards,
    )
    up_gradient, gain_u = spread_columns(
        mine[None], jnp.stack([tie(u, fs[3]) for u in ups]), gain_f, up_weight, shards
    )
    down_gradient = in_order([*downs[:3], join(downs[3:])], 0, F32)
    output_gradient = in_order(gather_direct(out_part), 1, F32)
    qkv_all = gather_direct(qkv_part)
    pick = lambda a, b: in_order([part[:, a:b] for part in qkv_all], 1, F32)
    raw_q = pick(0, wide)
    raw_k = pick(wide, wide + HEAD_DIM)
    raw_v = pick(wide + HEAD_DIM, wide + 2 * HEAD_DIM)
    gain_a_gradient = (
        jnp.sum(raw_q * query_weight.astype(F32), axis=1)
        + jnp.sum(raw_k * key_weight.astype(F32), axis=1)
        + jnp.sum(raw_v * value_weight.astype(F32), axis=1)
    )
    return (
        layer_output,
        token_gradient,
        gain_a_gradient,
        raw_q * gain_a,
        raw_k * gain_a,
        raw_v * gain_a,
        output_gradient,
        (gain_g + gain_u)[:, 0],
        gate_gradient,
        up_gradient,
        down_gradient,
    )


def solution(mesh):
    both = P(("dp", "seq"), None)
    flat = P("seq")
    split = P("seq", None)
    return jax.shard_map(
        local,
        mesh=mesh,
        in_specs=(
            both,
            P("dp", None),
            flat,
            split,
            split,
            split,
            split,
            flat,
            split,
            split,
            split,
            both,
        ),
        out_specs=(
            both,
            both,
            flat,
            split,
            split,
            split,
            split,
            flat,
            split,
            split,
            split,
        ),
        check_vma=False,
    )
```

```python
import functools

import jax
import jax.numpy as jnp
from jax import lax
from jax.experimental import pallas as pl
from jax.experimental.pallas import tpu as pltpu
from jax.sharding import PartitionSpec as P

HEADS = 32
HEAD_DIM = 64
KV_HEADS = 4
EPS = 1e-05
ROPE_BASE = 10000.0
NEG = -1e30
TILE_FORTH = 2560
TILE_BACK = 2560
VMEM_LIMIT = 56 * 2**20
BF = jnp.bfloat16
F32 = jnp.float32

NT = (((1,), (1,)), ((), ()))
TN = (((0,), (0,)), ((), ()))
NN = (((1,), (0,)), ((), ()))


def dot(left, right, dims=NN):
    return lax.dot_general(left, right, dims, preferred_element_type=F32)


def params(*semantics):
    return pltpu.CompilerParams(
        dimension_semantics=semantics, vmem_limit_bytes=VMEM_LIMIT
    )


FREE = pl.CostEstimate(flops=1, bytes_accessed=1, transcendentals=0)
TIMES = {
    "project": 0.1,
    "attend": 400,
    "attend_back": 1000,
    "merge": 1,
    "output_product": 3,
    "hidden_back": 4,
    "gate_product": 2,
    "up_gradient": 2,
    "up_product": 100,
    "back_product": 4,
    "back_first": 4,
    "down_gradient": 0.2,
    "gate_gradient": 2,
    "middle_back": 200,
    "down_product": 4,
    "output_gradient": 2,
    "project_back": 2,
    "sum_output": 100,
    "sum_tokens": 100,
    "spread_columns": 300,
    "pick_columns": 2,
    "finish": 3,
}


def cost(name):
    time = TIMES[name]
    return pl.CostEstimate(
        flops=int(time * 8e8), bytes_accessed=int(time * 2.5e6), transcendentals=0
    )
ANYWHERE = pl.BlockSpec(memory_space=pl.ANY)
SCALARS = pl.BlockSpec(memory_space=pltpu.SMEM)
INSIDE = pl.BlockSpec(memory_space=pltpu.VMEM)


def array(shape, dtype=BF):
    return jax.ShapeDtypeStruct(tuple(shape), dtype)


def tie(value, *others):
    return pl.pallas_call(
        lambda *refs: None,
        out_shape=array(value.shape, value.dtype),
        in_specs=[ANYWHERE] * (1 + len(others)),
        out_specs=ANYWHERE,
        input_output_aliases={0: 0},
        cost_estimate=FREE,
        name="tie",
    )(value, *others)


def run(body, name, grid, ins, outs, needs=(), scratch=(), aliases=None):
    count, made = len(ins), len(outs)

    def kernel(*refs):
        body(refs[:count], refs[count + len(needs) :][:made], refs[count + len(needs) + made :])

    result = pl.pallas_call(
        kernel,
        grid=grid,
        out_shape=tuple(shape for shape, _ in outs),
        in_specs=[spec for _, spec in ins] + [ANYWHERE] * len(needs),
        out_specs=tuple(spec for _, spec in outs),
        scratch_shapes=list(scratch),
        input_output_aliases=aliases or {},
        compiler_params=params(*["arbitrary"] * len(grid)),
        cost_estimate=cost(name),
        name=name,
    )(*[value for value, _ in ins], *needs)
    return result


def whole(shape):
    return pl.BlockSpec(tuple(shape), lambda i: (0,) * len(shape), pipeline_mode=pl.Buffered(1))


def down_rows(rows, cols, at=None):
    return pl.BlockSpec((rows, cols), (lambda i: (i, 0)) if at is None else (lambda i: (at, 0)))


def along_cols(rows, cols, at=0):
    return pl.BlockSpec((rows, cols), lambda i: (at, i))


def pick_kernel(which, gain, gate, up, gate_out, up_out, *, shards):
    piece = gate.shape[1] // (4 * shards)
    scale = gain[...]
    for quarter in range(4):

        @pl.when(which[0] == quarter)
        def _():
            for source, out in ((gate, gate_out), (up, up_out)):
                whole = source[...].astype(F32) * scale
                parts = []
                for shard in range(shards):
                    first = (shard * 4 + quarter) * piece
                    parts.append(whole[:, first : first + piece])
                out[...] = jnp.concatenate(parts, axis=1).astype(BF)


def pick_columns(quarter, gain, gate, up, shards):
    rows, width = gate.shape
    vmem = pl.BlockSpec(memory_space=pltpu.VMEM)
    shape = jax.ShapeDtypeStruct((rows, width // 4), BF)
    return pl.pallas_call(
        functools.partial(pick_kernel, shards=shards),
        out_shape=(shape, shape),
        in_specs=[pl.BlockSpec(memory_space=pltpu.SMEM), vmem, vmem, vmem],
        out_specs=(vmem, vmem),
        compiler_params=params(),
        cost_estimate=cost("pick_columns"),
        name="pick_columns",
    )(quarter, gain, gate, up)


def spread_kernel(which, grads, gain, weight, out, gain_out, *, shards):
    piece = grads.shape[2] // shards
    chunks = [grads[which[0] ^ quarter].astype(F32) for quarter in range(4)]
    whole = jnp.concatenate(
        [
            chunks[quarter][:, shard * piece : (shard + 1) * piece]
            for shard in range(shards)
            for quarter in range(4)
        ],
        axis=1,
    )
    gain_out[...] = jnp.sum(whole * weight[...].astype(F32), axis=1, keepdims=True)
    out[...] = whole * gain[...]


def spread_columns(mine, grads, gain, weight, shards):
    rows, width = weight.shape
    block = min(rows, 64)
    row = lambda cols: pl.BlockSpec((block, cols), lambda i: (i, 0))
    return pl.pallas_call(
        functools.partial(spread_kernel, shards=shards),
        grid=(rows // block,),
        out_shape=(
            jax.ShapeDtypeStruct((rows, width), F32),
            jax.ShapeDtypeStruct((rows, 1), F32),
        ),
        in_specs=[
            pl.BlockSpec(memory_space=pltpu.SMEM),
            pl.BlockSpec((4, block, width // 4), lambda i: (0, i, 0)),
            row(1),
            row(width),
        ],
        out_specs=(row(width), row(1)),
        compiler_params=params("arbitrary"),
        cost_estimate=cost("spread_columns"),
        name="spread_columns",
    )(mine, grads, gain, weight)


def turn(values, cos_t, sin_t):
    lane = lax.broadcasted_iota(jnp.int32, values.shape, 1)
    other = jnp.where(
        lane % 64 < 32, pltpu.roll(values, 96, 1), pltpu.roll(values, 32, 1)
    )
    return values * cos_t + other * sin_t


def project_kernel(ins, outs, _):
    *xs, w_ref, cos_ref, sin_ref = ins
    hat_ref, q_ref, kv_ref = outs
    rows = hat_ref.shape[0] // len(xs)
    for i, x_ref in enumerate(xs):
        span = slice(i * rows, (i + 1) * rows)
        x = x_ref[...].astype(F32)
        scale = lax.rsqrt(jnp.mean(x * x, axis=1, keepdims=True) + EPS)
        hat_ref[span, :] = (x * scale).astype(BF)
    out = dot(hat_ref[...], w_ref[...])
    cos_t, sin_t = cos_ref[...], sin_ref[...]
    wide = q_ref.shape[1]
    for pair in range(wide // 128):
        part = turn(out[:, pair * 128 : pair * 128 + 128], cos_t, sin_t)
        q_ref[:, pair * 128 : pair * 128 + 128] = (part * HEAD_DIM**-0.5).astype(BF)
    kv = out[:, wide : wide + 128]
    lane = lax.broadcasted_iota(jnp.int32, kv.shape, 1)
    kv_ref[...] = jnp.where(lane < 64, turn(kv, cos_t, sin_t), kv).astype(BF)


def project(chunk, xs, weight, cos_t, sin_t, rows, before=()):
    depth, wide = weight.shape[0], weight.shape[1] - 128
    ins = [(x, whole(x.shape)) for x in xs] + [
        (weight, whole(weight.shape)),
        (cos_t, down_rows(rows, 128, chunk)),
        (sin_t, down_rows(rows, 128, chunk)),
    ]

    def body(refs, outs, scratch):
        project_kernel(refs[: len(xs) + 3], outs, scratch)

    first = len(ins)
    return run(
        body,
        "project",
        (1,),
        ins + [(b, ANYWHERE) for b in before],
        [
            (array((4 * rows, cols)), down_rows(rows, cols, chunk))
            for cols in (depth, wide, 128)
        ],
        aliases={first + i: i for i in range(len(before))},
    )


def stack_heads(source, target, rows, upper):
    lane = lax.broadcasted_iota(jnp.int32, (rows, 128), 1)
    keep = (lane >= 64) if upper else (lane < 64)
    for head in range(source.shape[1] // 64):
        slab = source[:, head // 2 * 128 : head // 2 * 128 + 128].astype(F32)
        if (head % 2 == 1) != upper:
            slab = pltpu.roll(slab, 64, 1)
        target[head * rows : head * rows + rows, :] = jnp.where(keep, slab, 0.0).astype(BF)


def allowed(bounds, chunk, rows):
    low = bounds[0:1, :] - chunk * rows
    high = bounds[1:2, :] - chunk * rows
    place = lax.broadcasted_iota(jnp.int32, (rows, bounds.shape[1]), 0)
    return (place >= low) & (place <= high)


def over_chunks(where, step):
    group = pl.program_id(0)
    first, split, last = where[group], where[4 + group], where[8]
    edge = split - first

    def edges(i, carry):
        step(jnp.where(i < edge, first + i, last), True)
        return carry

    def inner(chunk, carry):
        step(chunk, False)
        return carry

    lax.fori_loop(split, last, inner, 0)
    lax.fori_loop(0, edge + 1, edges, 0)


def tiles_of(width, tile):
    return [slice(i, i + tile) for i in range(0, width, tile)]


def attend_kernel(where, q_ref, kv_ref, bound_ref, *rest, rows):
    out_ref, lse_ref, stacked, tops, totals, accs = rest[-6:]
    pairs = q_ref.shape[1] // 128
    stack_heads(q_ref, stacked, rows, False)
    lane = lax.broadcasted_iota(jnp.int32, (rows, 128), 1)
    tops[...] = jnp.full(tops.shape, NEG, F32)
    totals[...] = jnp.zeros(totals.shape, F32)
    accs[...] = jnp.zeros(accs.shape, F32)

    def step(chunk, masked):
        kv = kv_ref[chunk]
        for tile in tiles_of(2 * pairs * rows, TILE_FORTH):
            scores = dot(kv, stacked[tile, :], NT)
            if masked:
                mask = allowed(bound_ref[0, :, tile], chunk, rows)
                scores = jnp.where(mask, scores, NEG)
            top = tops[:, tile]
            peak = jnp.maximum(top, jnp.max(scores, axis=0, keepdims=True))
            fade = jnp.exp(top - peak)
            weights = jnp.exp(scores - peak)
            tops[:, tile] = peak
            totals[:, tile] = totals[:, tile] * fade + jnp.sum(
                weights, axis=0, keepdims=True
            )
            accs[:, tile] = accs[:, tile] * fade + dot(kv, weights.astype(BF), TN)[64:128]

    over_chunks(where, step)
    lse_ref[0] = tops[...] + jnp.log(totals[...])
    for pair in range(pairs):
        both = slice(pair * 2 * rows, (pair + 1) * 2 * rows)
        half = accs[:, both] / totals[:, both]
        flat = jnp.concatenate([half, half], axis=0).T
        out_ref[:, pair * 128 : pair * 128 + 128] = jnp.where(
            lane < 64, flat[:rows], flat[rows:]
        ).astype(BF)


def attend(where, queries, kv, bounds, rows, needs=()):
    shards = kv.shape[0]
    wide = queries.shape[1]
    lanes = wide // 64 * rows
    return pl.pallas_call(
        functools.partial(attend_kernel, rows=rows),
        grid_spec=pltpu.PrefetchScalarGridSpec(
            num_scalar_prefetch=1,
            grid=(4,),
            in_specs=[
                pl.BlockSpec((rows, wide), lambda g, w: (g, 0)),
                pl.BlockSpec((shards, rows, 128), lambda g, w: (0, g, 0)),
                pl.BlockSpec((1, 2, lanes), lambda g, w: (g, 0, 0)),
                *[ANYWHERE] * len(needs),
            ],
            out_specs=(
                pl.BlockSpec((rows, wide), lambda g, w: (g, 0)),
                pl.BlockSpec((1, 1, lanes), lambda g, w: (g, 0, 0)),
            ),
            scratch_shapes=[
                pltpu.VMEM((lanes, 128), BF),
                pltpu.VMEM((1, lanes), F32),
                pltpu.VMEM((1, lanes), F32),
                pltpu.VMEM((64, lanes), F32),
            ],
        ),
        out_shape=(
            jax.ShapeDtypeStruct((4 * rows, wide), BF),
            jax.ShapeDtypeStruct((4, 1, lanes), F32),
        ),
        compiler_params=params("arbitrary"),
        cost_estimate=cost("attend"),
        name="attend",
    )(where, queries, kv, bounds, *needs)


def attend_back_kernel(
    where,
    q_ref,
    kv_ref,
    bound_ref,
    up_ref,
    out_ref,
    lse_ref,
    cos_ref,
    sin_ref,
    *rest,
    rows,
):
    dq_ref, dkv_ref, stacked, upward, dq_acc, deltas = rest[-6:]
    group = pl.program_id(0)
    first, last = where[group], where[8]
    shards = kv_ref.shape[0]
    pairs = q_ref.shape[1] // 128
    stack_heads(q_ref, stacked, rows, False)
    stack_heads(up_ref, upward, rows, True)
    lane = lax.broadcasted_iota(jnp.int32, (rows, 128), 1)
    for pair in range(pairs):
        slab = up_ref[:, pair * 128 : pair * 128 + 128].astype(F32)
        slab = slab * out_ref[:, pair * 128 : pair * 128 + 128].astype(F32)
        both = jnp.concatenate(
            [jnp.where(lane < 64, slab, 0.0), jnp.where(lane < 64, 0.0, slab)], axis=0
        )
        deltas[:, pair * 2 * rows : (pair + 1) * 2 * rows] = jnp.sum(
            both.T, axis=0, keepdims=True
        )
    dq_acc[...] = jnp.zeros(dq_acc.shape, F32)

    def clear(chunk, carry):
        dkv_ref[chunk] = jnp.zeros((rows, 128), BF)
        return carry

    lax.fori_loop(0, first, clear, 0)
    lax.fori_loop(last + 1, shards, clear, 0)

    def step(chunk, masked):
        kv = kv_ref[chunk]
        total = jnp.zeros((rows, 128), F32)
        for tile in tiles_of(2 * pairs * rows, TILE_BACK):
            queries = stacked[tile, :]
            ups = upward[tile, :]
            weights = jnp.exp(dot(kv, queries, NT) - lse_ref[0, :, tile])
            if masked:
                mask = allowed(bound_ref[0, :, tile], chunk, rows)
                weights = jnp.where(mask, weights, 0.0)
            d_scores = (weights * (dot(kv, ups, NT) - deltas[:, tile])).astype(BF)
            total = total + dot(d_scores, queries) + dot(weights.astype(BF), ups)
            dq_acc[:, tile] += dot(kv, d_scores, TN)[0:64]
        dkv_ref[chunk] = total.astype(BF)

    over_chunks(where, step)
    cos_t, sin_t = cos_ref[...], sin_ref[...]
    for pair in range(pairs):
        half = dq_acc[:, pair * 2 * rows : (pair + 1) * 2 * rows]
        flat = jnp.concatenate([half, half], axis=0).T
        slab = jnp.where(lane < 64, flat[:rows], flat[rows:])
        dq_ref[:, pair * 128 : pair * 128 + 128] = turn(
            slab * HEAD_DIM**-0.5, cos_t, -sin_t
        ).astype(BF)


def attend_back(
    where, queries, kv, bounds, upstream, out, lse, cos_t, sin_t, rows, needs=()
):
    shards = kv.shape[0]
    wide = queries.shape[1]
    lanes = wide // 64 * rows
    row = lambda cols: pl.BlockSpec((rows, cols), lambda g, w: (g, 0))
    every = pl.BlockSpec((shards, rows, 128), lambda g, w: (0, g, 0))
    line = lambda count: pl.BlockSpec((1, count, lanes), lambda g, w: (g, 0, 0))
    return pl.pallas_call(
        functools.partial(attend_back_kernel, rows=rows),
        grid_spec=pltpu.PrefetchScalarGridSpec(
            num_scalar_prefetch=1,
            grid=(4,),
            in_specs=[
                row(wide),
                every,
                line(2),
                row(wide),
                row(wide),
                line(1),
                row(128),
                row(128),
                *[ANYWHERE] * len(needs),
            ],
            out_specs=(row(wide), every),
            scratch_shapes=[
                pltpu.VMEM((lanes, 128), BF),
                pltpu.VMEM((lanes, 128), BF),
                pltpu.VMEM((64, lanes), F32),
                pltpu.VMEM((1, lanes), F32),
            ],
        ),
        out_shape=(
            jax.ShapeDtypeStruct((4 * rows, wide), BF),
            jax.ShapeDtypeStruct(kv.shape, BF),
        ),
        compiler_params=params("arbitrary"),
        cost_estimate=cost("attend_back"),
        name="attend_back",
    )(where, queries, kv, bounds, upstream, out, lse, cos_t, sin_t, *needs)


def row_product(name, left, right, dims, block, needs=()):
    total = left.shape[1] if dims is TN else left.shape[0]
    cols = right.shape[0] if dims is NT else right.shape[1]
    spec = (
        along_cols(left.shape[0], block) if dims is TN else down_rows(block, left.shape[1])
    )

    def body(ins, outs, _):
        outs[0][...] = dot(ins[0][...], ins[1][...], dims).astype(BF)

    return run(
        body,
        name,
        (total // block,),
        [(left, spec), (right, whole(right.shape))],
        [(array((total, cols)), down_rows(block, cols))],
        needs,
    )[0]


def column_product(name, left, right, dims, block, needs=()):
    total = left.shape[1] if dims is TN else left.shape[0]
    cols = right.shape[0] if dims is NT else right.shape[1]
    spec = (
        down_rows(block, right.shape[1]) if dims is NT else along_cols(right.shape[0], block)
    )

    def body(ins, outs, _):
        outs[0][...] = dot(ins[0][...], ins[1][...], dims).astype(BF)

    return run(
        body,
        name,
        (cols // block,),
        [(left, whole(left.shape)), (right, spec)],
        [(array((total, cols)), along_cols(total, block))],
        needs,
    )[0]


def output_gradient_of(mixed, d_heads, block, needs):
    total, cols = d_heads.shape[0], d_heads.shape[1] // 2

    def body(ins, outs, _):
        outs[0][...] = dot(ins[0][...], ins[1][...], TN).astype(BF)

    return run(
        body,
        "output_gradient",
        (mixed.shape[1] // block,),
        [
            (mixed, along_cols(total, block)),
            (d_heads, pl.BlockSpec((total, cols), lambda i: (0, 1))),
        ],
        [(array((mixed.shape[1], cols)), down_rows(block, cols))],
        needs,
    )[0]


def gate_product(hats, w_gate, d_hidden, rows):
    depth, columns = w_gate.shape

    def body(ins, outs, _):
        for k in range(4):

            @pl.when(pl.program_id(0) == k)
            def _():
                outs[2][: rows // 2, :] = ins[2 * k][...]
                outs[2][rows // 2 :, :] = ins[2 * k + 1][...]

        gate = dot(outs[2][...], ins[8][...])
        outs[0][...] = gate.astype(BF)
        outs[1][...] = (ins[9][...].astype(F32) * gate * jax.nn.sigmoid(gate)).astype(BF)

    return run(
        body,
        "gate_product",
        (4,),
        [(h, whole(h.shape)) for h in hats]
        + [(w_gate, whole(w_gate.shape)), (d_hidden, down_rows(rows, columns))],
        [(array((4 * rows, cols)), down_rows(rows, cols)) for cols in (columns, columns, depth)],
    )


def up_product(chunks, hat, w_up, gate, d_hidden, rows, needs, before=()):
    columns = w_up.shape[1]
    first = chunks[0]

    def body(ins, outs, _):
        up = dot(ins[0][...], ins[1][...])
        gate = ins[2][...].astype(F32)
        sigma = jax.nn.sigmoid(gate)
        silu = gate * sigma
        outs[0][...] = (silu * up).astype(BF)
        slope = sigma + silu * (1.0 - sigma)
        outs[1][...] = (ins[3][...].astype(F32) * up * slope).astype(BF)

    spec = lambda cols: pl.BlockSpec((rows, cols), lambda i: (first + i, 0))
    ins = [
        (hat, spec(hat.shape[1])),
        (w_up, whole(w_up.shape)),
        (gate, spec(columns)),
        (d_hidden, spec(columns)),
    ]
    return run(
        body,
        "up_product",
        (len(chunks),),
        ins + [(b, ANYWHERE) for b in before],
        [(array((4 * rows, columns)), spec(columns))] * 2,
        needs,
        aliases={len(ins) + i: i for i in range(len(before))},
    )


def chunk_outs(chunks, rows, cols, block):
    outs = []
    for k in chunks:
        parts = 1 if k == 0 else 2
        outs += [(array((rows // parts, cols)), along_cols(rows // parts, block))] * parts
    return outs


def put_chunk(outs, value):
    rows = outs[0].shape[0]
    if rows == value.shape[0]:
        outs[0][...] = value.astype(BF)
        return outs[1:]
    outs[0][...] = value[:rows].astype(BF)
    outs[1][...] = value[rows:].astype(BF)
    return outs[2:]


def back_product(chunks, d_gate, d_up, w_gate, w_up, rows, needs=()):
    depth, columns = w_gate.shape
    block = depth // 4
    count = len(chunks)

    def body(ins, outs, _):
        w_one, w_two = ins[2 * count][...], ins[2 * count + 1][...]
        left = outs
        for i in range(count):
            left = put_chunk(
                left, dot(ins[i][...], w_one, NT) + dot(ins[count + i][...], w_two, NT)
            )

    return run(
        body,
        "back_first" if 3 in chunks else "back_product",
        (depth // block,),
        [(d_gate, down_rows(rows, columns, k)) for k in chunks]
        + [(d_up, down_rows(rows, columns, k)) for k in chunks]
        + [(w_gate, down_rows(block, columns)), (w_up, down_rows(block, columns))],
        chunk_outs(chunks, rows, depth, block),
        needs,
    )


def down_product(hidden, w_down, rows, needs):
    columns, depth = w_down.shape
    block = depth // 4

    def body(ins, outs, _):
        left = outs
        for k in range(4):
            left = put_chunk(left, dot(ins[0][k * rows : (k + 1) * rows, :], ins[1][...]))

    return run(
        body,
        "down_product",
        (4,),
        [(hidden, whole(hidden.shape)), (w_down, along_cols(columns, block))],
        chunk_outs(range(4), rows, depth, block),
        needs,
    )


def spans(spot, count, size):
    return [pl.ds(pl.multiple_of(spot[1 + k], 128), size) for k in range(count)]


def output_product(spot, mixes, w_outs, tokens):
    rows, depth = tokens.shape
    quarter = depth // 4
    flat = [w for pair in w_outs for w in pair]
    count = spot.shape[0] - 1

    def body(ins, outs, scratch):
        mine = ins[0][0]
        blocks = spans(ins[0], count, depth // count)
        mix, weights, x = ins[1:5], ins[5:13], ins[13]
        mixed_one, mixed_two, middle, hat_one, hat_two = outs
        mixed = scratch[0]
        half = rows // 2
        place = lambda k: pl.ds(pl.multiple_of((mine ^ k) * quarter, 128), quarter)
        for k in range(4):
            mixed[:, place(k)] = mix[k][...]
        mixed_one[...] = mixed[:half, :]
        mixed_two[...] = mixed[half:, :]
        sides = [mixed[:, block] for block in blocks]
        near = jnp.concatenate(sides[: count // 2], axis=1)
        other = jnp.concatenate(sides[count // 2 :], axis=1)
        for k in range(4):
            part = dot(near, weights[2 * k][...]) + dot(other, weights[2 * k + 1][...])
            middle[:, place(k)] = part + x[:, place(k)].astype(F32)
        value = middle[...]
        scale = lax.rsqrt(jnp.mean(value * value, axis=1, keepdims=True) + EPS)
        hat_one[...] = (value * scale)[:half].astype(BF)
        hat_two[...] = (value * scale)[half:].astype(BF)

    piece = (array((rows // 2, depth)), INSIDE)
    return run(
        body,
        "output_product",
        (),
        [(spot, SCALARS)] + [(v, INSIDE) for v in (*mixes, *flat, tokens)],
        [piece, piece, (array((rows, depth), F32), INSIDE), piece, piece],
        scratch=[pltpu.VMEM((rows, depth), BF)],
    )


def sum_parts(parts):
    own, *others = (p[...].astype(F32) for p in parts)
    return own + jnp.concatenate([others[0] + others[2], others[1] + others[3]], axis=0)


def norm_back(upstream, value):
    scale = lax.rsqrt(jnp.mean(value * value, axis=1, keepdims=True) + EPS)
    inner = jnp.mean(upstream * value, axis=1, keepdims=True)
    return scale * upstream - value * (scale * scale * scale * inner)


def middle_back(spot, parts, middle, dy, w_outs, needs):
    rows, depth = middle.shape
    quarter = depth // 4
    flat = [w for pair in w_outs for w in pair]
    count = spot.shape[0] - 1

    def body(ins, outs, scratch):
        mine = ins[0][0]
        blocks = spans(ins[0], count, depth // count)
        value, grad = ins[6:8]
        weights = ins[8:16]
        d_mixed, d_all = scratch
        upstream = sum_parts(ins[1:6])
        d_middle = grad[...].astype(F32) + norm_back(upstream, value[...])
        outs[0][...] = d_middle
        d_all[...] = d_middle.astype(BF)
        place = lambda k: pl.ds(pl.multiple_of((mine ^ k) * quarter, 128), quarter)
        near, other = 0.0, 0.0
        for k in range(4):
            part = d_all[:, place(k)]
            outs[1 + k][:, quarter:] = part
            near = near + dot(part, weights[2 * k][...], NT)
            other = other + dot(part, weights[2 * k + 1][...], NT)
        both = jnp.concatenate([near, other], axis=1).astype(BF)
        for k, block in enumerate(blocks):
            d_mixed[:, block] = both[:, k * (depth // count) : (k + 1) * (depth // count)]
        for k in range(4):
            outs[1 + k][:, :quarter] = d_mixed[:, place(k)]

    return run(
        body,
        "middle_back",
        (),
        [(spot, SCALARS)] + [(v, INSIDE) for v in (*parts, middle, dy, *flat)],
        [(array((rows, depth), F32), INSIDE)] + [(array((rows, 2 * quarter)), INSIDE)] * 4,
        needs,
        [pltpu.VMEM((rows, depth), BF), pltpu.VMEM((rows, depth), BF)],
    )


def project_back(dq, d_kv, cos_t, sin_t, weight, rows, hat, before):
    depth, wide = weight.shape
    block = depth // 4
    first = before.shape[1]

    def body(ins, outs, scratch):
        dq_ref, kv_ref, cos_ref, sin_ref, w_ref, hat_ref, before_ref = ins
        joined = scratch[0]

        @pl.when(pl.program_id(0) == 0)
        def _():
            joined[:, : wide - 128] = dq_ref[...]
            values = kv_ref[...].astype(F32)
            lane = lax.broadcasted_iota(jnp.int32, values.shape, 1)
            turned = turn(values, cos_ref[...], -sin_ref[...])
            joined[:, wide - 128 :] = jnp.where(lane < 64, turned, values).astype(BF)

        outs[0][:, :first] = before_ref[...]
        outs[0][:, first:] = dot(hat_ref[...], joined[...], TN).astype(BF)
        left = outs[1:]
        for k in range(4):
            left = put_chunk(
                left, dot(joined[k * rows : (k + 1) * rows, :], w_ref[...], NT)
            )

    return run(
        body,
        "project_back",
        (4,),
        [(v, whole(v.shape)) for v in (dq, d_kv, cos_t, sin_t)]
        + [
            (weight, down_rows(block, wide)),
            (hat, along_cols(4 * rows, block)),
            (before, down_rows(block, first)),
        ],
        [(array((depth, first + wide)), down_rows(block, first + wide))]
        + chunk_outs(range(4), rows, depth, block),
        scratch=[pltpu.VMEM((4 * rows, wide), BF)],
    )


def sum_output(parts, middle, needs):
    def body(ins, outs, _):
        outs[0][...] = (sum_parts(ins[:5]) + ins[5][...]).astype(BF)

    return run(
        body,
        "sum_output",
        (),
        [(v, INSIDE) for v in (*parts, middle)],
        [(array(middle.shape), INSIDE)],
        needs,
    )[0]


def sum_tokens(parts, tokens, d_middle, needs=()):
    def body(ins, outs, _):
        outs[0][...] = ins[6][...] + norm_back(sum_parts(ins[:5]), ins[5][...].astype(F32))

    return run(
        body,
        "sum_tokens",
        (),
        [(v, INSIDE) for v in (*parts, tokens, d_middle)],
        [(array(tokens.shape, F32), INSIDE)],
        needs,
    )[0]


def finish_attention(mine, parts, gain, output, query, key, value):
    rows, depth = output.shape
    quarter, wide = depth // 4, query.shape[1] // 4
    weights = (query, key, value)

    def body(ins, outs, scratch):
        scale, total = ins[5][...], 0.0
        joined = scratch[0]
        for k in range(4):
            joined[ins[0][0] ^ k] = ins[1 + k][...]
        begin = 0
        for i, size in enumerate((quarter, wide, HEAD_DIM, HEAD_DIM)):
            raw = jnp.concatenate(
                [joined[k][:, begin : begin + size].astype(F32) for k in range(4)], axis=1
            )
            begin += size
            if i == 0:
                outs[0][...] = raw
            else:
                weight = ins[5 + i][...].astype(F32)
                total = total + jnp.sum(raw * weight, axis=1, keepdims=True)
                outs[i][...] = raw * scale
        outs[4][...] = total

    return run(
        body,
        "finish",
        (),
        [(mine, SCALARS)] + [(v, INSIDE) for v in (*parts, gain, *weights)],
        [(array(w.shape, F32), INSIDE) for w in (output, *weights)]
        + [(array((rows, 1), F32), INSIDE)],
        scratch=[pltpu.VMEM((4, rows, parts[0].shape[1]), BF)],
    )


def hop(value, step):
    return lax.ppermute(value, "dp", [(i, i ^ step) for i in range(4)])


def gather_halves(one, two, hold=()):
    next_two, other_one = hop(two, 1), hop(one, 2)
    next_one, other_two = hop(one, 1), hop(two, 2)
    if hold:
        hold = (*hold, next_one, other_two)
        next_two, other_one = tie(next_two, *hold), tie(other_one, *hold)
    far = [hop(other_one, 1), hop(next_two, 2)]
    return [one, two, next_one, next_two, other_one, other_two, *far]


def gather_plane(value, hold=()):
    half = value.shape[0] // 2
    one = hop(value, 1)
    two = hop(value, 2)
    if hold:
        one, two = tie(one, *hold), tie(two, *hold)
    return [value, one, two, hop(two[:half], 1), hop(one[half:], 2)]


def join(parts):
    return jnp.concatenate(parts, axis=0)


def gather_direct(value):
    return [value] + [hop(value, k) for k in range(1, 4)]


def reduce_first(parts):
    return hop(parts[5], 1), hop(parts[6], 2)


def reduce_plain(parts, hold=None):
    one_a, two_b = parts[1], parts[4]
    if hold is not None:
        one_a, two_b = tie(one_a, hold), tie(two_b, hold)
    return hop(one_a, 1), hop(two_b, 2)


def reduce_second(parts, came, needs=()):
    own, _, one_b, two_a = parts[:4]
    by_one, by_two, next_a, other_b = came

    def body(ins, outs, _):
        for k in range(2):
            outs[k][...] = (ins[k][...].astype(F32) + ins[2 + k][...].astype(F32)).astype(BF)

    one_b, two_a = run(
        body,
        "merge",
        (),
        [(v, INSIDE) for v in (one_b, two_a, by_two, by_one)],
        [(array(one_b.shape), INSIDE)] * 2,
        needs,
    )
    return one_b, (own, next_a, hop(one_b, 1), hop(two_a, 2), other_b)


def core_swap(value):
    size = lax.axis_size("seq")
    return lax.ppermute(value, "seq", [(i, i ^ 1) for i in range(size)])


def in_order(parts, axis, dtype=None):
    mine = lax.axis_index("dp")
    shape = list(parts[0].shape)
    size = shape[axis]
    shape[axis] = 4 * size
    out = jnp.zeros(shape, dtype or parts[0].dtype)
    for k, part in enumerate(parts):
        out = lax.dynamic_update_slice_in_dim(
            out, part.astype(out.dtype), (mine ^ k) * size, axis
        )
    return out


def local(
    tokens,
    lengths,
    attention_gain,
    query_weight,
    key_weight,
    value_weight,
    output_weight,
    feedforward_gain,
    gate_weight,
    up_weight,
    down_weight,
    cotangent,
):
    rows, depth = tokens.shape
    shards = lax.axis_size("seq")
    mine = lax.axis_index("dp")
    place = lax.axis_index("seq")
    core = place % 2
    wide = HEADS // KV_HEADS * HEAD_DIM
    side = depth // 2
    near = lambda v: lax.all_gather(v, "seq", axis=0, tiled=True)
    far = lambda v: lax.psum_scatter(v, "seq", scatter_dimension=0, tiled=True)

    gain_a = attention_gain.astype(F32)[:, None]
    gain_f = feedforward_gain.astype(F32)[:, None]
    own_qkv = jnp.concatenate(
        [
            lax.dynamic_slice_in_dim(query_weight, mine * wide, wide, 1),
            lax.dynamic_slice_in_dim(key_weight, mine * HEAD_DIM, HEAD_DIM, 1),
            lax.dynamic_slice_in_dim(value_weight, mine * HEAD_DIM, HEAD_DIM, 1),
        ],
        axis=1,
    )
    w_qkv = near((own_qkv.astype(F32) * gain_a).astype(BF))
    own_block = lax.dynamic_slice_in_dim(
        output_weight, mine * (depth // 4), depth // 4, 1
    )
    sizes = join([lengths] + [hop(lengths, k) for k in range(1, 4)])
    xs = gather_plane(tokens)
    own_out = near(tie(own_block, w_qkv, xs[1], xs[2], sizes))
    spot = jnp.stack([mine, core * side, (1 - core) * side])
    piece = down_weight.shape[0] // 4
    w_down = near(lax.dynamic_slice_in_dim(down_weight, mine * piece, piece, 0))
    own_gate, own_up = pick_columns(mine[None], gain_f, gate_weight, up_weight, shards)
    w_gate = near(own_gate)
    w_up = near(own_up)

    count = sizes.shape[1]
    before = jnp.arange(count)[:, None] <= jnp.arange(count)[None, :]
    ends = jnp.sum(jnp.where(before[None], sizes[:, :, None], 0), axis=1)
    index = place * rows + jnp.arange(rows, dtype=jnp.int32)
    passed = ends[:, None, :] <= index[None, :, None]
    begin = jnp.max(jnp.where(passed, ends[:, None, :], 0), axis=2)
    position = (index[None, :] - begin).astype(F32).reshape(4 * rows)
    half = HEAD_DIM // 2
    inverse = ROPE_BASE ** (-jnp.arange(half, dtype=F32) * 2.0 / HEAD_DIM)
    theta = position[:, None] * inverse[None, :]
    cos_h, sin_h = jnp.cos(theta), jnp.sin(theta)
    cos_t = jnp.concatenate([cos_h] * 4, axis=1)
    sin_t = jnp.concatenate([-sin_h, sin_h] * 2, axis=1)
    bounds = jnp.stack([begin, jnp.broadcast_to(index[None, :], begin.shape)], axis=1)
    bounds = jnp.concatenate([bounds] * (wide // HEAD_DIM), axis=2)
    low = begin[:, 0] // rows
    split = jnp.clip((begin[:, rows - 1] + rows - 1) // rows, low, place)
    where = jnp.concatenate([low, split, place[None]])

    made = ()
    for k, pieces in enumerate((xs[0:1], xs[1:2], xs[2:3], xs[3:5])):
        made = project(k, pieces, w_qkv, cos_t, sin_t, rows, made)
    hat, queries, own_kv = made
    own_half, own_rest = (
        lax.dynamic_slice_in_dim(own_out, c * side, side, 0) for c in (core, 1 - core)
    )
    kv = lax.all_gather(tie(own_kv, own_half), "seq", axis=0)
    own_half = tie(own_half, xs[3], xs[4])
    own_half, got_one, got_two, far_one, far_two = gather_plane(own_half)
    got = [own_half, got_one, got_two]
    swapped = [own_rest, core_swap(got_one), core_swap(got_two)]
    dy_own = tie(cotangent, got_one, got_two)
    dy_one, dy_two = hop(dy_own, 1), hop(dy_own, 2)
    mixed_heads, lse = attend(
        where, queries, kv, bounds, rows, (got_one, got_two, *swapped[1:])
    )
    mixed_heads = tie(mixed_heads, far_one, far_two, dy_one, dy_two)
    got.append(join([tie(far_one, mixed_heads), far_two]))
    swapped.append(core_swap(got[3]))
    w_outs = list(zip(got, swapped, strict=True))
    mixes = [mixed_heads[:rows]] + [
        hop(mixed_heads[k * rows : (k + 1) * rows], k) for k in range(1, 4)
    ]
    mixed_one, mixed_two, middle, hat_one, hat_two = output_product(
        spot, mixes, w_outs, tokens
    )

    part = rows // 2
    dy_far = hop(tie(dy_two[:part], *mixes), 1), hop(tie(dy_one[part:], *mixes), 2)
    dy_all = join([tie(dy_own, hat_one), dy_one, dy_two, *dy_far])
    d_hidden = row_product("hidden_back", dy_all, w_down, NT, rows, (hat_two,))
    hats = gather_halves(hat_one, hat_two, (d_hidden,))
    mixes_all = gather_halves(tie(mixed_one, *hats[6:]), tie(mixed_two, *hats[6:]))
    gate, d_up, hat_all = gate_product(hats, w_gate, d_hidden, rows)
    up_raw = row_product("up_gradient", hat_all, d_up, TN, wide)
    up_part = far(up_raw)
    ups_of = functools.partial(
        up_product, hat=hat_all, w_up=w_up, gate=gate, d_hidden=d_hidden, rows=rows
    )
    back = functools.partial(back_product, d_up=d_up, w_gate=w_gate, w_up=w_up, rows=rows)
    some = ups_of((3,), needs=(up_raw, *mixes_all[2:6]))
    far_one, far_two = back((3,), d_gate=some[1], needs=mixes_all[6:])
    hidden, d_gate = ups_of((0, 1, 2), needs=(far_one,), before=some)
    came = reduce_first([None] * 5 + [far_one, far_two])
    down_raw = column_product("down_gradient", hidden, dy_all, TN, wide)
    down_part = far(down_raw)
    sides = back((1, 2), d_gate=d_gate, needs=(down_raw, *came))
    came += reduce_plain((None, *sides))
    first, terms = reduce_second((None, *sides), came)
    (d_own,) = back((0,), d_gate=d_gate, needs=(first,))
    terms = (d_own, *terms[1:])
    mixed_all = join(mixes_all)
    d_middle, *blocks = middle_back(
        spot, terms, middle, cotangent, w_outs, (up_part, mixed_all)
    )

    d_heads = join([blocks[0]] + [hop(blocks[k], k) for k in range(1, 4)])
    gate_raw = row_product("gate_gradient", hat_all, d_gate, TN, wide, (blocks[0],))
    gate_part = far(gate_raw)
    outs = down_product(hidden, w_down, rows, (gate_raw,))
    ups_one, ups_two = hop(up_part, 1), hop(up_part, 2)
    down_part = tie(down_part, gate_raw)
    downs_one, downs_two = hop(down_part, 1), hop(down_part, 2)
    dq, dkv = attend_back(
        where, queries, kv, bounds, d_heads, mixed_heads, lse, cos_t, sin_t, rows, (outs[6], ups_one, ups_two, downs_one, downs_two)
    )
    came = reduce_first(outs)
    ups_far, downs_far = hop(up_part, 3), hop(down_part, 3)
    dkv = tie(dkv, gate_part, *came, downs_far, ups_far)
    came += reduce_plain(outs, dkv)
    own_dkv = far(dkv.reshape(shards * 4 * rows, 128))
    first, terms = reduce_second(outs, came, (dkv,))
    out_raw = output_gradient_of(mixed_all, d_heads, wide, (first,))
    gate_part = tie(gate_part, dkv)
    gates_one, gates_two = hop(gate_part, 1), hop(gate_part, 2)
    own_dkv = tie(own_dkv, out_raw, *terms[1:], gates_one, gates_two)
    both_raw, *fs = project_back(
        dq, own_dkv, cos_t, sin_t, w_qkv, rows, hat, out_raw
    )
    both_part = far(both_raw)
    layer_output = sum_output(terms, middle, (fs[6],))
    came = (*reduce_first(fs), *reduce_plain(fs))
    first, terms = reduce_second(fs, came, came[2:])
    gates_far = hop(tie(gate_part, first), 3)
    token_gradient = sum_tokens(terms, tokens, d_middle)

    gate_gradient, gain_g = spread_columns(
        mine[None],
        jnp.stack([gate_part, gates_one, gates_two, gates_far]),
        gain_f,
        gate_weight,
        shards,
    )
    up_gradient, gain_u = spread_columns(
        mine[None], jnp.stack([tie(up_part, both_raw), ups_one, ups_two, ups_far]), gain_f, up_weight, shards
    )
    down_gradient = in_order([down_part, downs_one, downs_two, downs_far], 0, F32)
    gradients = finish_attention(
        mine[None],
        gather_direct(both_part),
        gain_a,
        output_weight,
        query_weight,
        key_weight,
        value_weight,
    )
    output_gradient, query_gradient, key_gradient, value_gradient, gain_a_gradient = gradients
    return (
        layer_output,
        token_gradient,
        gain_a_gradient[:, 0],
        query_gradient,
        key_gradient,
        value_gradient,
        output_gradient,
        (gain_g + gain_u)[:, 0],
        gate_gradient,
        up_gradient,
        down_gradient,
    )


def solution(mesh):
    both = P(("dp", "seq"), None)
    flat = P("seq")
    split = P("seq", None)
    return jax.shard_map(
        local,
        mesh=mesh,
        in_specs=(
            both,
            P("dp", None),
            flat,
            split,
            split,
            split,
            split,
            flat,
            split,
            split,
            split,
            both,
        ),
        out_specs=(
            both,
            both,
            flat,
            split,
            split,
            split,
            split,
            flat,
            split,
            split,
            split,
        ),
        check_vma=False,
    )
```

```python
import functools

import jax
import jax.numpy as jnp
from jax import lax
from jax.experimental import pallas as pl
from jax.experimental.pallas import tpu as pltpu
from jax.sharding import PartitionSpec as P

HEADS = 32
HEAD_DIM = 64
KV_HEADS = 4
EPS = 1e-05
ROPE_BASE = 10000.0
NEG = -1e30
TILE_FORTH = 2560
TILE_BACK = 2560
VMEM_LIMIT = 56 * 2**20
BF = jnp.bfloat16
F32 = jnp.float32

NT = (((1,), (1,)), ((), ()))
TN = (((0,), (0,)), ((), ()))
NN = (((1,), (0,)), ((), ()))


def dot(left, right, dims=NN):
    return lax.dot_general(left, right, dims, preferred_element_type=F32)


def params(*semantics):
    return pltpu.CompilerParams(
        dimension_semantics=semantics, vmem_limit_bytes=VMEM_LIMIT
    )


FREE = pl.CostEstimate(flops=1, bytes_accessed=1, transcendentals=0)
TIMES = {
    "project": 0.1,
    "attend": 400,
    "attend_back": 1000,
    "merge": 1,
    "output_product": 3,
    "hidden_back": 4,
    "gate_product": 2,
    "up_gradient": 2,
    "up_product": 100,
    "back_product": 4,
    "back_first": 4,
    "down_gradient": 0.2,
    "gate_gradient": 2,
    "middle_back": 200,
    "down_product": 4,
    "output_gradient": 2,
    "project_back": 2,
    "sum_output": 100,
    "sum_tokens": 100,
    "spread_up": 300,
    "spread_gate": 0.1,
    "pick_columns": 2,
    "finish": 3,
}


def cost(name):
    time = TIMES[name]
    return pl.CostEstimate(
        flops=int(time * 8e8), bytes_accessed=int(time * 2.5e6), transcendentals=0
    )
ANYWHERE = pl.BlockSpec(memory_space=pl.ANY)
SCALARS = pl.BlockSpec(memory_space=pltpu.SMEM)
INSIDE = pl.BlockSpec(memory_space=pltpu.VMEM)


def array(shape, dtype=BF):
    return jax.ShapeDtypeStruct(tuple(shape), dtype)


def tie(value, *others):
    return pl.pallas_call(
        lambda *refs: None,
        out_shape=array(value.shape, value.dtype),
        in_specs=[ANYWHERE] * (1 + len(others)),
        out_specs=ANYWHERE,
        input_output_aliases={0: 0},
        cost_estimate=FREE,
        name="tie",
    )(value, *others)


def run(body, name, grid, ins, outs, needs=(), scratch=(), aliases=None):
    count, made = len(ins), len(outs)

    def kernel(*refs):
        body(refs[:count], refs[count + len(needs) :][:made], refs[count + len(needs) + made :])

    result = pl.pallas_call(
        kernel,
        grid=grid,
        out_shape=tuple(shape for shape, _ in outs),
        in_specs=[spec for _, spec in ins] + [ANYWHERE] * len(needs),
        out_specs=tuple(spec for _, spec in outs),
        scratch_shapes=list(scratch),
        input_output_aliases=aliases or {},
        compiler_params=params(*["arbitrary"] * len(grid)),
        cost_estimate=cost(name),
        name=name,
    )(*[value for value, _ in ins], *needs)
    return result


def whole(shape):
    return pl.BlockSpec(tuple(shape), lambda i: (0,) * len(shape), pipeline_mode=pl.Buffered(1))


def down_rows(rows, cols, at=None):
    return pl.BlockSpec((rows, cols), (lambda i: (i, 0)) if at is None else (lambda i: (at, 0)))


def along_cols(rows, cols, at=0):
    return pl.BlockSpec((rows, cols), lambda i: (at, i))


def pick_kernel(which, gain, gate, up, gate_out, up_out, *, shards):
    piece = gate.shape[1] // (4 * shards)
    scale = gain[...]
    for quarter in range(4):

        @pl.when(which[0] == quarter)
        def _():
            for source, out in ((gate, gate_out), (up, up_out)):
                whole = source[...].astype(F32) * scale
                parts = []
                for shard in range(shards):
                    first = (shard * 4 + quarter) * piece
                    parts.append(whole[:, first : first + piece])
                out[...] = jnp.concatenate(parts, axis=1).astype(BF)


def pick_columns(quarter, gain, gate, up, shards):
    rows, width = gate.shape
    vmem = pl.BlockSpec(memory_space=pltpu.VMEM)
    shape = jax.ShapeDtypeStruct((rows, width // 4), BF)
    return pl.pallas_call(
        functools.partial(pick_kernel, shards=shards),
        out_shape=(shape, shape),
        in_specs=[pl.BlockSpec(memory_space=pltpu.SMEM), vmem, vmem, vmem],
        out_specs=(vmem, vmem),
        compiler_params=params(),
        cost_estimate=cost("pick_columns"),
        name="pick_columns",
    )(quarter, gain, gate, up)


def spread_kernel(which, grads, gain, weight, out, gain_out, *, shards):
    piece = grads.shape[2] // shards
    chunks = [grads[which[0] ^ quarter].astype(F32) for quarter in range(4)]
    whole = jnp.concatenate(
        [
            chunks[quarter][:, shard * piece : (shard + 1) * piece]
            for shard in range(shards)
            for quarter in range(4)
        ],
        axis=1,
    )
    gain_out[...] = jnp.sum(whole * weight[...].astype(F32), axis=1, keepdims=True)
    out[...] = whole * gain[...]


def spread_columns(name, mine, grads, gain, weight, shards):
    rows, width = weight.shape
    block = min(rows, 64)
    row = lambda cols: pl.BlockSpec((block, cols), lambda i: (i, 0))
    return pl.pallas_call(
        functools.partial(spread_kernel, shards=shards),
        grid=(rows // block,),
        out_shape=(
            jax.ShapeDtypeStruct((rows, width), F32),
            jax.ShapeDtypeStruct((rows, 1), F32),
        ),
        in_specs=[
            pl.BlockSpec(memory_space=pltpu.SMEM),
            pl.BlockSpec((4, block, width // 4), lambda i: (0, i, 0)),
            row(1),
            row(width),
        ],
        out_specs=(row(width), row(1)),
        compiler_params=params("arbitrary"),
        cost_estimate=cost(name),
        name=name,
    )(mine, grads, gain, weight)


def turn(values, cos_t, sin_t):
    lane = lax.broadcasted_iota(jnp.int32, values.shape, 1)
    other = jnp.where(
        lane % 64 < 32, pltpu.roll(values, 96, 1), pltpu.roll(values, 32, 1)
    )
    return values * cos_t + other * sin_t


def project_kernel(ins, outs, _):
    *xs, w_ref, cos_ref, sin_ref = ins
    hat_ref, q_ref, kv_ref = outs
    rows = hat_ref.shape[0] // len(xs)
    for i, x_ref in enumerate(xs):
        span = slice(i * rows, (i + 1) * rows)
        x = x_ref[...].astype(F32)
        scale = lax.rsqrt(jnp.mean(x * x, axis=1, keepdims=True) + EPS)
        hat_ref[span, :] = (x * scale).astype(BF)
    out = dot(hat_ref[...], w_ref[...])
    cos_t, sin_t = cos_ref[...], sin_ref[...]
    wide = q_ref.shape[1]
    for pair in range(wide // 128):
        part = turn(out[:, pair * 128 : pair * 128 + 128], cos_t, sin_t)
        q_ref[:, pair * 128 : pair * 128 + 128] = (part * HEAD_DIM**-0.5).astype(BF)
    kv = out[:, wide : wide + 128]
    lane = lax.broadcasted_iota(jnp.int32, kv.shape, 1)
    kv_ref[...] = jnp.where(lane < 64, turn(kv, cos_t, sin_t), kv).astype(BF)


def project(chunk, xs, weight, cos_t, sin_t, rows, before=()):
    depth, wide = weight.shape[0], weight.shape[1] - 128
    ins = [(x, whole(x.shape)) for x in xs] + [
        (weight, whole(weight.shape)),
        (cos_t, down_rows(rows, 128, chunk)),
        (sin_t, down_rows(rows, 128, chunk)),
    ]

    def body(refs, outs, scratch):
        project_kernel(refs[: len(xs) + 3], outs, scratch)

    first = len(ins)
    return run(
        body,
        "project",
        (1,),
        ins + [(b, ANYWHERE) for b in before],
        [
            (array((4 * rows, cols)), down_rows(rows, cols, chunk))
            for cols in (depth, wide, 128)
        ],
        aliases={first + i: i for i in range(len(before))},
    )


def stack_heads(source, target, rows, upper):
    lane = lax.broadcasted_iota(jnp.int32, (rows, 128), 1)
    keep = (lane >= 64) if upper else (lane < 64)
    for head in range(source.shape[1] // 64):
        slab = source[:, head // 2 * 128 : head // 2 * 128 + 128].astype(F32)
        if (head % 2 == 1) != upper:
            slab = pltpu.roll(slab, 64, 1)
        target[head * rows : head * rows + rows, :] = jnp.where(keep, slab, 0.0).astype(BF)


def allowed(bounds, chunk, rows):
    low = bounds[0:1, :] - chunk * rows
    high = bounds[1:2, :] - chunk * rows
    place = lax.broadcasted_iota(jnp.int32, (rows, bounds.shape[1]), 0)
    return (place >= low) & (place <= high)


def over_chunks(where, step):
    group = pl.program_id(0)
    first, split, last = where[group], where[4 + group], where[8]
    edge = split - first

    def edges(i, carry):
        step(jnp.where(i < edge, first + i, last), True)
        return carry

    def inner(chunk, carry):
        step(chunk, False)
        return carry

    lax.fori_loop(split, last, inner, 0)
    lax.fori_loop(0, edge + 1, edges, 0)


def tiles_of(width, tile):
    return [slice(i, i + tile) for i in range(0, width, tile)]


def attend_kernel(where, q_ref, kv_ref, bound_ref, *rest, rows):
    out_ref, lse_ref, stacked, tops, totals, accs = rest[-6:]
    pairs = q_ref.shape[1] // 128
    stack_heads(q_ref, stacked, rows, False)
    lane = lax.broadcasted_iota(jnp.int32, (rows, 128), 1)
    tops[...] = jnp.full(tops.shape, NEG, F32)
    totals[...] = jnp.zeros(totals.shape, F32)
    accs[...] = jnp.zeros(accs.shape, F32)

    def step(chunk, masked):
        kv = kv_ref[chunk]
        for tile in tiles_of(2 * pairs * rows, TILE_FORTH):
            scores = dot(kv, stacked[tile, :], NT)
            if masked:
                mask = allowed(bound_ref[0, :, tile], chunk, rows)
                scores = jnp.where(mask, scores, NEG)
            top = tops[:, tile]
            peak = jnp.maximum(top, jnp.max(scores, axis=0, keepdims=True))
            fade = jnp.exp(top - peak)
            weights = jnp.exp(scores - peak)
            tops[:, tile] = peak
            totals[:, tile] = totals[:, tile] * fade + jnp.sum(
                weights, axis=0, keepdims=True
            )
            accs[:, tile] = accs[:, tile] * fade + dot(kv, weights.astype(BF), TN)[64:128]

    over_chunks(where, step)
    lse_ref[0] = tops[...] + jnp.log(totals[...])
    for pair in range(pairs):
        both = slice(pair * 2 * rows, (pair + 1) * 2 * rows)
        half = accs[:, both] / totals[:, both]
        flat = jnp.concatenate([half, half], axis=0).T
        out_ref[:, pair * 128 : pair * 128 + 128] = jnp.where(
            lane < 64, flat[:rows], flat[rows:]
        ).astype(BF)


def attend(where, queries, kv, bounds, rows, needs=()):
    shards = kv.shape[0]
    wide = queries.shape[1]
    lanes = wide // 64 * rows
    return pl.pallas_call(
        functools.partial(attend_kernel, rows=rows),
        grid_spec=pltpu.PrefetchScalarGridSpec(
            num_scalar_prefetch=1,
            grid=(4,),
            in_specs=[
                pl.BlockSpec((rows, wide), lambda g, w: (g, 0)),
                pl.BlockSpec((shards, rows, 128), lambda g, w: (0, g, 0)),
                pl.BlockSpec((1, 2, lanes), lambda g, w: (g, 0, 0)),
                *[ANYWHERE] * len(needs),
            ],
            out_specs=(
                pl.BlockSpec((rows, wide), lambda g, w: (g, 0)),
                pl.BlockSpec((1, 1, lanes), lambda g, w: (g, 0, 0)),
            ),
            scratch_shapes=[
                pltpu.VMEM((lanes, 128), BF),
                pltpu.VMEM((1, lanes), F32),
                pltpu.VMEM((1, lanes), F32),
                pltpu.VMEM((64, lanes), F32),
            ],
        ),
        out_shape=(
            jax.ShapeDtypeStruct((4 * rows, wide), BF),
            jax.ShapeDtypeStruct((4, 1, lanes), F32),
        ),
        compiler_params=params("arbitrary"),
        cost_estimate=cost("attend"),
        name="attend",
    )(where, queries, kv, bounds, *needs)


def attend_back_kernel(
    where,
    q_ref,
    kv_ref,
    bound_ref,
    up_ref,
    out_ref,
    lse_ref,
    cos_ref,
    sin_ref,
    *rest,
    rows,
):
    dq_ref, dkv_ref, stacked, upward, dq_acc, deltas = rest[-6:]
    group = pl.program_id(0)
    first, last = where[group], where[8]
    shards = kv_ref.shape[0]
    pairs = q_ref.shape[1] // 128
    stack_heads(q_ref, stacked, rows, False)
    stack_heads(up_ref, upward, rows, True)
    lane = lax.broadcasted_iota(jnp.int32, (rows, 128), 1)
    for pair in range(pairs):
        slab = up_ref[:, pair * 128 : pair * 128 + 128].astype(F32)
        slab = slab * out_ref[:, pair * 128 : pair * 128 + 128].astype(F32)
        both = jnp.concatenate(
            [jnp.where(lane < 64, slab, 0.0), jnp.where(lane < 64, 0.0, slab)], axis=0
        )
        deltas[:, pair * 2 * rows : (pair + 1) * 2 * rows] = jnp.sum(
            both.T, axis=0, keepdims=True
        )
    dq_acc[...] = jnp.zeros(dq_acc.shape, F32)

    def clear(chunk, carry):
        dkv_ref[chunk] = jnp.zeros((rows, 128), BF)
        return carry

    lax.fori_loop(0, first, clear, 0)
    lax.fori_loop(last + 1, shards, clear, 0)

    def step(chunk, masked):
        kv = kv_ref[chunk]
        total = jnp.zeros((rows, 128), F32)
        for tile in tiles_of(2 * pairs * rows, TILE_BACK):
            queries = stacked[tile, :]
            ups = upward[tile, :]
            weights = jnp.exp(dot(kv, queries, NT) - lse_ref[0, :, tile])
            if masked:
                mask = allowed(bound_ref[0, :, tile], chunk, rows)
                weights = jnp.where(mask, weights, 0.0)
            d_scores = (weights * (dot(kv, ups, NT) - deltas[:, tile])).astype(BF)
            total = total + dot(d_scores, queries) + dot(weights.astype(BF), ups)
            dq_acc[:, tile] += dot(kv, d_scores, TN)[0:64]
        dkv_ref[chunk] = total.astype(BF)

    over_chunks(where, step)
    cos_t, sin_t = cos_ref[...], sin_ref[...]
    for pair in range(pairs):
        half = dq_acc[:, pair * 2 * rows : (pair + 1) * 2 * rows]
        flat = jnp.concatenate([half, half], axis=0).T
        slab = jnp.where(lane < 64, flat[:rows], flat[rows:])
        dq_ref[:, pair * 128 : pair * 128 + 128] = turn(
            slab * HEAD_DIM**-0.5, cos_t, -sin_t
        ).astype(BF)


def attend_back(
    where, queries, kv, bounds, upstream, out, lse, cos_t, sin_t, rows, needs=()
):
    shards = kv.shape[0]
    wide = queries.shape[1]
    lanes = wide // 64 * rows
    row = lambda cols: pl.BlockSpec((rows, cols), lambda g, w: (g, 0))
    every = pl.BlockSpec((shards, rows, 128), lambda g, w: (0, g, 0))
    line = lambda count: pl.BlockSpec((1, count, lanes), lambda g, w: (g, 0, 0))
    return pl.pallas_call(
        functools.partial(attend_back_kernel, rows=rows),
        grid_spec=pltpu.PrefetchScalarGridSpec(
            num_scalar_prefetch=1,
            grid=(4,),
            in_specs=[
                row(wide),
                every,
                line(2),
                row(wide),
                row(wide),
                line(1),
                row(128),
                row(128),
                *[ANYWHERE] * len(needs),
            ],
            out_specs=(row(wide), every),
            scratch_shapes=[
                pltpu.VMEM((lanes, 128), BF),
                pltpu.VMEM((lanes, 128), BF),
                pltpu.VMEM((64, lanes), F32),
                pltpu.VMEM((1, lanes), F32),
            ],
        ),
        out_shape=(
            jax.ShapeDtypeStruct((4 * rows, wide), BF),
            jax.ShapeDtypeStruct(kv.shape, BF),
        ),
        compiler_params=params("arbitrary"),
        cost_estimate=cost("attend_back"),
        name="attend_back",
    )(where, queries, kv, bounds, upstream, out, lse, cos_t, sin_t, *needs)


def row_product(name, left, right, dims, block, needs=()):
    total = left.shape[1] if dims is TN else left.shape[0]
    cols = right.shape[0] if dims is NT else right.shape[1]
    spec = (
        along_cols(left.shape[0], block) if dims is TN else down_rows(block, left.shape[1])
    )

    def body(ins, outs, _):
        outs[0][...] = dot(ins[0][...], ins[1][...], dims).astype(BF)

    return run(
        body,
        name,
        (total // block,),
        [(left, spec), (right, whole(right.shape))],
        [(array((total, cols)), down_rows(block, cols))],
        needs,
    )[0]


def column_product(name, left, right, dims, block, needs=()):
    total = left.shape[1] if dims is TN else left.shape[0]
    cols = right.shape[0] if dims is NT else right.shape[1]
    spec = (
        down_rows(block, right.shape[1]) if dims is NT else along_cols(right.shape[0], block)
    )

    def body(ins, outs, _):
        outs[0][...] = dot(ins[0][...], ins[1][...], dims).astype(BF)

    return run(
        body,
        name,
        (cols // block,),
        [(left, whole(left.shape)), (right, spec)],
        [(array((total, cols)), along_cols(total, block))],
        needs,
    )[0]


def output_gradient_of(mixed, d_heads, block, needs):
    total, cols = d_heads.shape[0], d_heads.shape[1] // 2

    def body(ins, outs, _):
        outs[0][...] = dot(ins[0][...], ins[1][...], TN).astype(BF)

    return run(
        body,
        "output_gradient",
        (mixed.shape[1] // block,),
        [
            (mixed, along_cols(total, block)),
            (d_heads, pl.BlockSpec((total, cols), lambda i: (0, 1))),
        ],
        [(array((mixed.shape[1], cols)), down_rows(block, cols))],
        needs,
    )[0]


def gate_product(hats, w_gate, d_hidden, rows):
    depth, columns = w_gate.shape

    def body(ins, outs, _):
        for k in range(4):

            @pl.when(pl.program_id(0) == k)
            def _():
                outs[2][: rows // 2, :] = ins[2 * k][...]
                outs[2][rows // 2 :, :] = ins[2 * k + 1][...]

        gate = dot(outs[2][...], ins[8][...])
        outs[0][...] = gate.astype(BF)
        outs[1][...] = (ins[9][...].astype(F32) * gate * jax.nn.sigmoid(gate)).astype(BF)

    return run(
        body,
        "gate_product",
        (4,),
        [(h, whole(h.shape)) for h in hats]
        + [(w_gate, whole(w_gate.shape)), (d_hidden, down_rows(rows, columns))],
        [(array((4 * rows, cols)), down_rows(rows, cols)) for cols in (columns, columns, depth)],
    )


def up_product(chunks, hat, w_up, gate, d_hidden, rows, needs, before=()):
    columns = w_up.shape[1]
    first = chunks[0]

    def body(ins, outs, _):
        up = dot(ins[0][...], ins[1][...])
        gate = ins[2][...].astype(F32)
        sigma = jax.nn.sigmoid(gate)
        silu = gate * sigma
        outs[0][...] = (silu * up).astype(BF)
        slope = sigma + silu * (1.0 - sigma)
        outs[1][...] = (ins[3][...].astype(F32) * up * slope).astype(BF)

    spec = lambda cols: pl.BlockSpec((rows, cols), lambda i: (first + i, 0))
    ins = [
        (hat, spec(hat.shape[1])),
        (w_up, whole(w_up.shape)),
        (gate, spec(columns)),
        (d_hidden, spec(columns)),
    ]
    return run(
        body,
        "up_product",
        (len(chunks),),
        ins + [(b, ANYWHERE) for b in before],
        [(array((4 * rows, columns)), spec(columns))] * 2,
        needs,
        aliases={len(ins) + i: i for i in range(len(before))},
    )


def chunk_outs(chunks, rows, cols, block):
    outs = []
    for k in chunks:
        parts = 1 if k == 0 else 2
        outs += [(array((rows // parts, cols)), along_cols(rows // parts, block))] * parts
    return outs


def put_chunk(outs, value):
    rows = outs[0].shape[0]
    if rows == value.shape[0]:
        outs[0][...] = value.astype(BF)
        return outs[1:]
    outs[0][...] = value[:rows].astype(BF)
    outs[1][...] = value[rows:].astype(BF)
    return outs[2:]


def back_product(chunks, d_gate, d_up, w_gate, w_up, rows, needs=()):
    depth, columns = w_gate.shape
    block = depth // 4
    count = len(chunks)

    def body(ins, outs, _):
        w_one, w_two = ins[2 * count][...], ins[2 * count + 1][...]
        left = outs
        for i in range(count):
            left = put_chunk(
                left, dot(ins[i][...], w_one, NT) + dot(ins[count + i][...], w_two, NT)
            )

    return run(
        body,
        "back_first" if 3 in chunks else "back_product",
        (depth // block,),
        [(d_gate, down_rows(rows, columns, k)) for k in chunks]
        + [(d_up, down_rows(rows, columns, k)) for k in chunks]
        + [(w_gate, down_rows(block, columns)), (w_up, down_rows(block, columns))],
        chunk_outs(chunks, rows, depth, block),
        needs,
    )


def down_product(hidden, w_down, rows, needs):
    columns, depth = w_down.shape
    block = depth // 4

    def body(ins, outs, _):
        left = outs
        for k in range(4):
            left = put_chunk(left, dot(ins[0][k * rows : (k + 1) * rows, :], ins[1][...]))

    return run(
        body,
        "down_product",
        (4,),
        [(hidden, whole(hidden.shape)), (w_down, along_cols(columns, block))],
        chunk_outs(range(4), rows, depth, block),
        needs,
    )


def spans(spot, count, size):
    return [pl.ds(pl.multiple_of(spot[1 + k], 128), size) for k in range(count)]


def output_product(spot, mixes, w_outs, tokens):
    rows, depth = tokens.shape
    quarter = depth // 4
    flat = [w for pair in w_outs for w in pair]
    count = spot.shape[0] - 1

    def body(ins, outs, scratch):
        mine = ins[0][0]
        blocks = spans(ins[0], count, depth // count)
        mix, weights, x = ins[1:5], ins[5:13], ins[13]
        mixed_one, mixed_two, middle, hat_one, hat_two = outs
        mixed = scratch[0]
        half = rows // 2
        place = lambda k: pl.ds(pl.multiple_of((mine ^ k) * quarter, 128), quarter)
        for k in range(4):
            mixed[:, place(k)] = mix[k][...]
        mixed_one[...] = mixed[:half, :]
        mixed_two[...] = mixed[half:, :]
        sides = [mixed[:, block] for block in blocks]
        near = jnp.concatenate(sides[: count // 2], axis=1)
        other = jnp.concatenate(sides[count // 2 :], axis=1)
        for k in range(4):
            part = dot(near, weights[2 * k][...]) + dot(other, weights[2 * k + 1][...])
            middle[:, place(k)] = part + x[:, place(k)].astype(F32)
        value = middle[...]
        scale = lax.rsqrt(jnp.mean(value * value, axis=1, keepdims=True) + EPS)
        hat_one[...] = (value * scale)[:half].astype(BF)
        hat_two[...] = (value * scale)[half:].astype(BF)

    piece = (array((rows // 2, depth)), INSIDE)
    return run(
        body,
        "output_product",
        (),
        [(spot, SCALARS)] + [(v, INSIDE) for v in (*mixes, *flat, tokens)],
        [piece, piece, (array((rows, depth), F32), INSIDE), piece, piece],
        scratch=[pltpu.VMEM((rows, depth), BF)],
    )


def sum_parts(parts):
    own, *others = (p[...].astype(F32) for p in parts)
    return own + jnp.concatenate([others[0] + others[2], others[1] + others[3]], axis=0)


def norm_back(upstream, value):
    scale = lax.rsqrt(jnp.mean(value * value, axis=1, keepdims=True) + EPS)
    inner = jnp.mean(upstream * value, axis=1, keepdims=True)
    return scale * upstream - value * (scale * scale * scale * inner)


def middle_back(spot, parts, middle, dy, w_outs, needs):
    rows, depth = middle.shape
    quarter = depth // 4
    flat = [w for pair in w_outs for w in pair]
    count = spot.shape[0] - 1

    def body(ins, outs, scratch):
        mine = ins[0][0]
        blocks = spans(ins[0], count, depth // count)
        value, grad = ins[6:8]
        weights = ins[8:16]
        d_mixed, d_all = scratch
        upstream = sum_parts(ins[1:6])
        d_middle = grad[...].astype(F32) + norm_back(upstream, value[...])
        outs[0][...] = d_middle
        d_all[...] = d_middle.astype(BF)
        place = lambda k: pl.ds(pl.multiple_of((mine ^ k) * quarter, 128), quarter)
        near, other = 0.0, 0.0
        for k in range(4):
            part = d_all[:, place(k)]
            outs[1 + k][:, quarter:] = part
            near = near + dot(part, weights[2 * k][...], NT)
            other = other + dot(part, weights[2 * k + 1][...], NT)
        both = jnp.concatenate([near, other], axis=1).astype(BF)
        for k, block in enumerate(blocks):
            d_mixed[:, block] = both[:, k * (depth // count) : (k + 1) * (depth // count)]
        for k in range(4):
            outs[1 + k][:, :quarter] = d_mixed[:, place(k)]

    return run(
        body,
        "middle_back",
        (),
        [(spot, SCALARS)] + [(v, INSIDE) for v in (*parts, middle, dy, *flat)],
        [(array((rows, depth), F32), INSIDE)] + [(array((rows, 2 * quarter)), INSIDE)] * 4,
        needs,
        [pltpu.VMEM((rows, depth), BF), pltpu.VMEM((rows, depth), BF)],
    )


def project_back(dq, d_kv, cos_t, sin_t, weight, rows, hat, before):
    depth, wide = weight.shape
    block = depth // 4
    first = before.shape[1]

    def body(ins, outs, scratch):
        dq_ref, kv_ref, cos_ref, sin_ref, w_ref, hat_ref, before_ref = ins
        joined = scratch[0]

        @pl.when(pl.program_id(0) == 0)
        def _():
            joined[:, : wide - 128] = dq_ref[...]
            values = kv_ref[...].astype(F32)
            lane = lax.broadcasted_iota(jnp.int32, values.shape, 1)
            turned = turn(values, cos_ref[...], -sin_ref[...])
            joined[:, wide - 128 :] = jnp.where(lane < 64, turned, values).astype(BF)

        outs[0][:, :first] = before_ref[...]
        outs[0][:, first:] = dot(hat_ref[...], joined[...], TN).astype(BF)
        left = outs[1:]
        for k in range(4):
            left = put_chunk(
                left, dot(joined[k * rows : (k + 1) * rows, :], w_ref[...], NT)
            )

    return run(
        body,
        "project_back",
        (4,),
        [(v, whole(v.shape)) for v in (dq, d_kv, cos_t, sin_t)]
        + [
            (weight, down_rows(block, wide)),
            (hat, along_cols(4 * rows, block)),
            (before, down_rows(block, first)),
        ],
        [(array((depth, first + wide)), down_rows(block, first + wide))]
        + chunk_outs(range(4), rows, depth, block),
        scratch=[pltpu.VMEM((4 * rows, wide), BF)],
    )


def sum_output(parts, middle, needs):
    def body(ins, outs, _):
        outs[0][...] = (sum_parts(ins[:5]) + ins[5][...]).astype(BF)

    return run(
        body,
        "sum_output",
        (),
        [(v, INSIDE) for v in (*parts, middle)],
        [(array(middle.shape), INSIDE)],
        needs,
    )[0]


def sum_tokens(parts, tokens, d_middle, needs=()):
    def body(ins, outs, _):
        outs[0][...] = ins[6][...] + norm_back(sum_parts(ins[:5]), ins[5][...].astype(F32))

    return run(
        body,
        "sum_tokens",
        (),
        [(v, INSIDE) for v in (*parts, tokens, d_middle)],
        [(array(tokens.shape, F32), INSIDE)],
        needs,
    )[0]


def down_rows_in_order(spot, parts, needs):
    rows, cols = parts[0].shape
    if rows % 16:
        return in_order(parts, 0, F32)

    def body(ins, outs, _):
        for k in range(4):
            first = pl.multiple_of((ins[0][0] ^ k) * rows, 16)
            outs[0][pl.ds(first, rows), :] = ins[1 + k][...].astype(F32)

    return run(
        body,
        "finish",
        (),
        [(spot, SCALARS)] + [(v, INSIDE) for v in parts],
        [(array((4 * rows, cols), F32), INSIDE)],
        needs,
    )[0]


def finish_attention(mine, parts, gain, output, query, key, value):
    rows, depth = output.shape
    quarter, wide = depth // 4, query.shape[1] // 4
    weights = (query, key, value)

    def body(ins, outs, scratch):
        scale, total = ins[5][...], 0.0
        joined = scratch[0]
        for k in range(4):
            joined[ins[0][0] ^ k] = ins[1 + k][...]
        begin = 0
        for i, size in enumerate((quarter, wide, HEAD_DIM, HEAD_DIM)):
            raw = jnp.concatenate(
                [joined[k][:, begin : begin + size].astype(F32) for k in range(4)], axis=1
            )
            begin += size
            if i == 0:
                outs[0][...] = raw
            else:
                weight = ins[5 + i][...].astype(F32)
                total = total + jnp.sum(raw * weight, axis=1, keepdims=True)
                outs[i][...] = raw * scale
        outs[4][...] = total

    return run(
        body,
        "finish",
        (),
        [(mine, SCALARS)] + [(v, INSIDE) for v in (*parts, gain, *weights)],
        [(array(w.shape, F32), INSIDE) for w in (output, *weights)]
        + [(array((rows, 1), F32), INSIDE)],
        scratch=[pltpu.VMEM((4, rows, parts[0].shape[1]), BF)],
    )


def hop(value, step):
    return lax.ppermute(value, "dp", [(i, i ^ step) for i in range(4)])


def gather_halves(one, two, hold=()):
    next_two, other_one = hop(two, 1), hop(one, 2)
    next_one, other_two = hop(one, 1), hop(two, 2)
    if hold:
        hold = (*hold, next_one, other_two)
        next_two, other_one = tie(next_two, *hold), tie(other_one, *hold)
    far = [hop(other_one, 1), hop(next_two, 2)]
    return [one, two, next_one, next_two, other_one, other_two, *far]


def gather_plane(value, hold=()):
    half = value.shape[0] // 2
    one = hop(value, 1)
    two = hop(value, 2)
    if hold:
        one, two = tie(one, *hold), tie(two, *hold)
    return [value, one, two, hop(two[:half], 1), hop(one[half:], 2)]


def join(parts):
    return jnp.concatenate(parts, axis=0)


def gather_direct(value):
    return [value] + [hop(value, k) for k in range(1, 4)]


def reduce_first(parts):
    return hop(parts[5], 1), hop(parts[6], 2)


def reduce_plain(parts, hold=None):
    one_a, two_b = parts[1], parts[4]
    if hold is not None:
        one_a, two_b = tie(one_a, hold), tie(two_b, hold)
    return hop(one_a, 1), hop(two_b, 2)


def reduce_second(parts, came, needs=()):
    own, _, one_b, two_a = parts[:4]
    by_one, by_two, next_a, other_b = came

    def body(ins, outs, _):
        for k in range(2):
            outs[k][...] = (ins[k][...].astype(F32) + ins[2 + k][...].astype(F32)).astype(BF)

    one_b, two_a = run(
        body,
        "merge",
        (),
        [(v, INSIDE) for v in (one_b, two_a, by_two, by_one)],
        [(array(one_b.shape), INSIDE)] * 2,
        needs,
    )
    return one_b, (own, next_a, hop(one_b, 1), hop(two_a, 2), other_b)


def core_swap(value):
    size = lax.axis_size("seq")
    return lax.ppermute(value, "seq", [(i, i ^ 1) for i in range(size)])


def in_order(parts, axis, dtype=None):
    mine = lax.axis_index("dp")
    shape = list(parts[0].shape)
    size = shape[axis]
    shape[axis] = 4 * size
    out = jnp.zeros(shape, dtype or parts[0].dtype)
    for k, part in enumerate(parts):
        out = lax.dynamic_update_slice_in_dim(
            out, part.astype(out.dtype), (mine ^ k) * size, axis
        )
    return out


def local(
    tokens,
    lengths,
    attention_gain,
    query_weight,
    key_weight,
    value_weight,
    output_weight,
    feedforward_gain,
    gate_weight,
    up_weight,
    down_weight,
    cotangent,
):
    rows, depth = tokens.shape
    shards = lax.axis_size("seq")
    mine = lax.axis_index("dp")
    place = lax.axis_index("seq")
    core = place % 2
    wide = HEADS // KV_HEADS * HEAD_DIM
    side = depth // 2
    near = lambda v: lax.all_gather(v, "seq", axis=0, tiled=True)
    far = lambda v: lax.psum_scatter(v, "seq", scatter_dimension=0, tiled=True)

    gain_a = attention_gain.astype(F32)[:, None]
    gain_f = feedforward_gain.astype(F32)[:, None]
    own_qkv = jnp.concatenate(
        [
            lax.dynamic_slice_in_dim(query_weight, mine * wide, wide, 1),
            lax.dynamic_slice_in_dim(key_weight, mine * HEAD_DIM, HEAD_DIM, 1),
            lax.dynamic_slice_in_dim(value_weight, mine * HEAD_DIM, HEAD_DIM, 1),
        ],
        axis=1,
    )
    w_qkv = near((own_qkv.astype(F32) * gain_a).astype(BF))
    own_block = lax.dynamic_slice_in_dim(
        output_weight, mine * (depth // 4), depth // 4, 1
    )
    sizes = join([lengths] + [hop(lengths, k) for k in range(1, 4)])
    xs = gather_plane(tokens)
    own_out = near(tie(own_block, w_qkv, xs[1], xs[2], sizes))
    spot = jnp.stack([mine, core * side, (1 - core) * side])
    piece = down_weight.shape[0] // 4
    w_down = near(lax.dynamic_slice_in_dim(down_weight, mine * piece, piece, 0))
    own_gate, own_up = pick_columns(mine[None], gain_f, gate_weight, up_weight, shards)
    w_gate = near(own_gate)
    w_up = near(own_up)

    count = sizes.shape[1]
    before = jnp.arange(count)[:, None] <= jnp.arange(count)[None, :]
    ends = jnp.sum(jnp.where(before[None], sizes[:, :, None], 0), axis=1)
    index = place * rows + jnp.arange(rows, dtype=jnp.int32)
    passed = ends[:, None, :] <= index[None, :, None]
    begin = jnp.max(jnp.where(passed, ends[:, None, :], 0), axis=2)
    position = (index[None, :] - begin).astype(F32).reshape(4 * rows)
    half = HEAD_DIM // 2
    inverse = ROPE_BASE ** (-jnp.arange(half, dtype=F32) * 2.0 / HEAD_DIM)
    theta = position[:, None] * inverse[None, :]
    cos_h, sin_h = jnp.cos(theta), jnp.sin(theta)
    cos_t = jnp.concatenate([cos_h] * 4, axis=1)
    sin_t = jnp.concatenate([-sin_h, sin_h] * 2, axis=1)
    bounds = jnp.stack([begin, jnp.broadcast_to(index[None, :], begin.shape)], axis=1)
    bounds = jnp.concatenate([bounds] * (wide // HEAD_DIM), axis=2)
    low = begin[:, 0] // rows
    split = jnp.clip((begin[:, rows - 1] + rows - 1) // rows, low, place)
    where = jnp.concatenate([low, split, place[None]])

    made = ()
    for k, pieces in enumerate((xs[0:1], xs[1:2], xs[2:3], xs[3:5])):
        made = project(k, pieces, w_qkv, cos_t, sin_t, rows, made)
    hat, queries, own_kv = made
    own_half, own_rest = (
        lax.dynamic_slice_in_dim(own_out, c * side, side, 0) for c in (core, 1 - core)
    )
    kv = lax.all_gather(tie(own_kv, own_half), "seq", axis=0)
    own_half = tie(own_half, xs[3], xs[4])
    own_half, got_one, got_two, far_one, far_two = gather_plane(own_half)
    got = [own_half, got_one, got_two]
    swapped = [own_rest, core_swap(got_one), core_swap(got_two)]
    dy_own = tie(cotangent, got_one, got_two)
    dy_one, dy_two = hop(dy_own, 1), hop(dy_own, 2)
    mixed_heads, lse = attend(
        where, queries, kv, bounds, rows, (got_one, got_two, *swapped[1:])
    )
    mixed_heads = tie(mixed_heads, far_one, far_two, dy_one, dy_two)
    got.append(join([tie(far_one, mixed_heads), far_two]))
    swapped.append(core_swap(got[3]))
    w_outs = list(zip(got, swapped, strict=True))
    mixes = [mixed_heads[:rows]] + [
        hop(mixed_heads[k * rows : (k + 1) * rows], k) for k in range(1, 4)
    ]
    mixed_one, mixed_two, middle, hat_one, hat_two = output_product(
        spot, mixes, w_outs, tokens
    )

    part = rows // 2
    dy_far = hop(tie(dy_two[:part], *mixes), 1), hop(tie(dy_one[part:], *mixes), 2)
    dy_all = join([tie(dy_own, hat_one), dy_one, dy_two, *dy_far])
    d_hidden = row_product("hidden_back", dy_all, w_down, NT, rows, (hat_two,))
    hats = gather_halves(hat_one, hat_two, (d_hidden,))
    mixes_all = gather_halves(tie(mixed_one, *hats[6:]), tie(mixed_two, *hats[6:]))
    gate, d_up, hat_all = gate_product(hats, w_gate, d_hidden, rows)
    up_raw = row_product("up_gradient", hat_all, d_up, TN, wide)
    up_part = far(up_raw)
    ups_of = functools.partial(
        up_product, hat=hat_all, w_up=w_up, gate=gate, d_hidden=d_hidden, rows=rows
    )
    back = functools.partial(back_product, d_up=d_up, w_gate=w_gate, w_up=w_up, rows=rows)
    some = ups_of((3,), needs=(up_raw, *mixes_all[2:6]))
    far_one, far_two = back((3,), d_gate=some[1], needs=mixes_all[6:])
    hidden, d_gate = ups_of((0, 1, 2), needs=(far_one,), before=some)
    came = reduce_first([None] * 5 + [far_one, far_two])
    down_raw = column_product("down_gradient", hidden, dy_all, TN, wide)
    down_part = far(down_raw)
    sides = back((1, 2), d_gate=d_gate, needs=(down_raw, *came))
    came += reduce_plain((None, *sides))
    first, terms = reduce_second((None, *sides), came)
    (d_own,) = back((0,), d_gate=d_gate, needs=(first,))
    terms = (d_own, *terms[1:])
    mixed_all = join(mixes_all)
    d_middle, *blocks = middle_back(
        spot, terms, middle, cotangent, w_outs, (up_part, mixed_all)
    )

    d_heads = join([blocks[0]] + [hop(blocks[k], k) for k in range(1, 4)])
    gate_raw = row_product("gate_gradient", hat_all, d_gate, TN, wide, (blocks[0],))
    gate_part = far(gate_raw)
    outs = down_product(hidden, w_down, rows, (gate_raw,))
    ups_one, ups_two = hop(up_part, 1), hop(up_part, 2)
    dq, dkv = attend_back(
        where, queries, kv, bounds, d_heads, mixed_heads, lse, cos_t, sin_t, rows, (outs[6], ups_one, ups_two)
    )
    came = reduce_first(outs)
    downs_one, downs_two = hop(down_part, 1), hop(down_part, 2)
    ups_far = hop(up_part, 3)
    dkv = tie(dkv, gate_part, *came, downs_one, downs_two, ups_far)
    came += reduce_plain(outs, dkv)
    own_dkv = far(dkv.reshape(shards * 4 * rows, 128))
    first, terms = reduce_second(outs, came, (dkv,))
    out_raw = output_gradient_of(mixed_all, d_heads, wide, (first,))
    downs_far = hop(tie(down_part, dkv), 3)
    own_dkv = tie(own_dkv, out_raw, *terms[1:], downs_far)
    both_raw, *fs = project_back(
        dq, own_dkv, cos_t, sin_t, w_qkv, rows, hat, out_raw
    )
    both_part = far(both_raw)
    layer_output = sum_output(terms, middle, (fs[6],))
    came = (*reduce_first(fs), *reduce_plain(fs))
    first, terms = reduce_second(fs, came, came[2:])
    gates = gather_plane(tie(gate_part, first), (both_part,))
    token_gradient = sum_tokens(terms, tokens, d_middle)

    gate_gradient, gain_g = spread_columns(
        "spread_gate",
        mine[None],
        jnp.stack([*gates[:3], join(gates[3:])]),
        gain_f,
        gate_weight,
        shards,
    )
    up_gradient, gain_u = spread_columns(
        "spread_up", mine[None], jnp.stack([tie(up_part, both_raw), ups_one, ups_two, ups_far]), gain_f, up_weight, shards
    )
    down_gradient = down_rows_in_order(
        spot, [down_part, downs_one, downs_two, downs_far], (both_raw,)
    )
    gradients = finish_attention(
        mine[None],
        gather_direct(both_part),
        gain_a,
        output_weight,
        query_weight,
        key_weight,
        value_weight,
    )
    output_gradient, query_gradient, key_gradient, value_gradient, gain_a_gradient = gradients
    return (
        layer_output,
        token_gradient,
        gain_a_gradient[:, 0],
        query_gradient,
        key_gradient,
        value_gradient,
        output_gradient,
        (gain_g + gain_u)[:, 0],
        gate_gradient,
        up_gradient,
        down_gradient,
    )


def solution(mesh):
    both = P(("dp", "seq"), None)
    flat = P("seq")
    split = P("seq", None)
    return jax.shard_map(
        local,
        mesh=mesh,
        in_specs=(
            both,
            P("dp", None),
            flat,
            split,
            split,
            split,
            split,
            flat,
            split,
            split,
            split,
            both,
        ),
        out_specs=(
            both,
            both,
            flat,
            split,
            split,
            split,
            split,
            flat,
            split,
            split,
            split,
        ),
        check_vma=False,
    )
```

```python
import functools

import jax
import jax.numpy as jnp
from jax import lax
from jax.experimental import pallas as pl
from jax.experimental.pallas import tpu as pltpu
from jax.sharding import PartitionSpec as P

HEADS = 32
HEAD_DIM = 64
KV_HEADS = 4
EPS = 1e-05
ROPE_BASE = 10000.0
NEG = -1e30
TILE_FORTH = 2560
TILE_BACK = 2560
VMEM_LIMIT = 56 * 2**20
BF = jnp.bfloat16
F32 = jnp.float32

NT = (((1,), (1,)), ((), ()))
TN = (((0,), (0,)), ((), ()))
NN = (((1,), (0,)), ((), ()))


def dot(left, right, dims=NN):
    return lax.dot_general(left, right, dims, preferred_element_type=F32)


def params(*semantics):
    return pltpu.CompilerParams(
        dimension_semantics=semantics, vmem_limit_bytes=VMEM_LIMIT
    )


FREE = pl.CostEstimate(flops=1, bytes_accessed=1, transcendentals=0)
TIMES = {
    "project": 0.1,
    "attend": 400,
    "attend_back": 1000,
    "merge": 1,
    "output_product": 3,
    "hidden_back": 4,
    "gate_product": 2,
    "up_gradient": 2,
    "up_product": 100,
    "back_product": 4,
    "back_first": 4,
    "down_gradient": 0.2,
    "gate_gradient": 2,
    "middle_back": 200,
    "down_product": 4,
    "output_gradient": 2,
    "project_back": 50,
    "sum_output": 100,
    "sum_tokens": 100,
    "spread_up": 300,
    "spread_gate": 0.1,
    "pick_columns": 2,
    "finish": 3,
}


def cost(name):
    time = TIMES[name]
    return pl.CostEstimate(
        flops=int(time * 8e8), bytes_accessed=int(time * 2.5e6), transcendentals=0
    )
ANYWHERE = pl.BlockSpec(memory_space=pl.ANY)
SCALARS = pl.BlockSpec(memory_space=pltpu.SMEM)
INSIDE = pl.BlockSpec(memory_space=pltpu.VMEM)


def array(shape, dtype=BF):
    return jax.ShapeDtypeStruct(tuple(shape), dtype)


def tie(value, *others):
    return pl.pallas_call(
        lambda *refs: None,
        out_shape=array(value.shape, value.dtype),
        in_specs=[ANYWHERE] * (1 + len(others)),
        out_specs=ANYWHERE,
        input_output_aliases={0: 0},
        cost_estimate=FREE,
        name="tie",
    )(value, *others)


def run(body, name, grid, ins, outs, needs=(), scratch=(), aliases=None):
    count, made = len(ins), len(outs)

    def kernel(*refs):
        body(refs[:count], refs[count + len(needs) :][:made], refs[count + len(needs) + made :])

    result = pl.pallas_call(
        kernel,
        grid=grid,
        out_shape=tuple(shape for shape, _ in outs),
        in_specs=[spec for _, spec in ins] + [ANYWHERE] * len(needs),
        out_specs=tuple(spec for _, spec in outs),
        scratch_shapes=list(scratch),
        input_output_aliases=aliases or {},
        compiler_params=params(*["arbitrary"] * len(grid)),
        cost_estimate=cost(name),
        name=name,
    )(*[value for value, _ in ins], *needs)
    return result


def whole(shape):
    return pl.BlockSpec(tuple(shape), lambda i: (0,) * len(shape), pipeline_mode=pl.Buffered(1))


def down_rows(rows, cols, at=None):
    return pl.BlockSpec((rows, cols), (lambda i: (i, 0)) if at is None else (lambda i: (at, 0)))


def along_cols(rows, cols, at=0):
    return pl.BlockSpec((rows, cols), lambda i: (at, i))


def pick_kernel(which, gain, gate, up, gate_out, up_out, *, shards):
    piece = gate.shape[1] // (4 * shards)
    scale = gain[...]
    for quarter in range(4):

        @pl.when(which[0] == quarter)
        def _():
            for source, out in ((gate, gate_out), (up, up_out)):
                whole = source[...].astype(F32) * scale
                parts = []
                for shard in range(shards):
                    first = (shard * 4 + quarter) * piece
                    parts.append(whole[:, first : first + piece])
                out[...] = jnp.concatenate(parts, axis=1).astype(BF)


def pick_columns(quarter, gain, gate, up, shards):
    rows, width = gate.shape
    vmem = pl.BlockSpec(memory_space=pltpu.VMEM)
    shape = jax.ShapeDtypeStruct((rows, width // 4), BF)
    return pl.pallas_call(
        functools.partial(pick_kernel, shards=shards),
        out_shape=(shape, shape),
        in_specs=[pl.BlockSpec(memory_space=pltpu.SMEM), vmem, vmem, vmem],
        out_specs=(vmem, vmem),
        compiler_params=params(),
        cost_estimate=cost("pick_columns"),
        name="pick_columns",
    )(quarter, gain, gate, up)


def spread_kernel(which, grads, gain, weight, out, gain_out, *, shards):
    piece = grads.shape[2] // shards
    chunks = [grads[which[0] ^ quarter].astype(F32) for quarter in range(4)]
    whole = jnp.concatenate(
        [
            chunks[quarter][:, shard * piece : (shard + 1) * piece]
            for shard in range(shards)
            for quarter in range(4)
        ],
        axis=1,
    )
    gain_out[...] = jnp.sum(whole * weight[...].astype(F32), axis=1, keepdims=True)
    out[...] = whole * gain[...]


def spread_columns(name, mine, grads, gain, weight, shards):
    rows, width = weight.shape
    block = min(rows, 64)
    row = lambda cols: pl.BlockSpec((block, cols), lambda i: (i, 0))
    return pl.pallas_call(
        functools.partial(spread_kernel, shards=shards),
        grid=(rows // block,),
        out_shape=(
            jax.ShapeDtypeStruct((rows, width), F32),
            jax.ShapeDtypeStruct((rows, 1), F32),
        ),
        in_specs=[
            pl.BlockSpec(memory_space=pltpu.SMEM),
            pl.BlockSpec((4, block, width // 4), lambda i: (0, i, 0)),
            row(1),
            row(width),
        ],
        out_specs=(row(width), row(1)),
        compiler_params=params("arbitrary"),
        cost_estimate=cost(name),
        name=name,
    )(mine, grads, gain, weight)


def turn(values, cos_t, sin_t):
    lane = lax.broadcasted_iota(jnp.int32, values.shape, 1)
    other = jnp.where(
        lane % 64 < 32, pltpu.roll(values, 96, 1), pltpu.roll(values, 32, 1)
    )
    return values * cos_t + other * sin_t


def project_kernel(ins, outs, _):
    *xs, w_ref, cos_ref, sin_ref = ins
    hat_ref, q_ref, kv_ref = outs
    rows = hat_ref.shape[0] // len(xs)
    for i, x_ref in enumerate(xs):
        span = slice(i * rows, (i + 1) * rows)
        x = x_ref[...].astype(F32)
        scale = lax.rsqrt(jnp.mean(x * x, axis=1, keepdims=True) + EPS)
        hat_ref[span, :] = (x * scale).astype(BF)
    out = dot(hat_ref[...], w_ref[...])
    cos_t, sin_t = cos_ref[...], sin_ref[...]
    wide = q_ref.shape[1]
    for pair in range(wide // 128):
        part = turn(out[:, pair * 128 : pair * 128 + 128], cos_t, sin_t)
        q_ref[:, pair * 128 : pair * 128 + 128] = (part * HEAD_DIM**-0.5).astype(BF)
    kv = out[:, wide : wide + 128]
    lane = lax.broadcasted_iota(jnp.int32, kv.shape, 1)
    kv_ref[...] = jnp.where(lane < 64, turn(kv, cos_t, sin_t), kv).astype(BF)


def project(chunk, xs, weight, cos_t, sin_t, rows, before=()):
    depth, wide = weight.shape[0], weight.shape[1] - 128
    ins = [(x, whole(x.shape)) for x in xs] + [
        (weight, whole(weight.shape)),
        (cos_t, down_rows(rows, 128, chunk)),
        (sin_t, down_rows(rows, 128, chunk)),
    ]

    def body(refs, outs, scratch):
        project_kernel(refs[: len(xs) + 3], outs, scratch)

    first = len(ins)
    return run(
        body,
        "project",
        (1,),
        ins + [(b, ANYWHERE) for b in before],
        [
            (array((4 * rows, cols)), down_rows(rows, cols, chunk))
            for cols in (depth, wide, 128)
        ],
        aliases={first + i: i for i in range(len(before))},
    )


def stack_heads(source, target, rows, upper):
    lane = lax.broadcasted_iota(jnp.int32, (rows, 128), 1)
    keep = (lane >= 64) if upper else (lane < 64)
    for head in range(source.shape[1] // 64):
        slab = source[:, head // 2 * 128 : head // 2 * 128 + 128].astype(F32)
        if (head % 2 == 1) != upper:
            slab = pltpu.roll(slab, 64, 1)
        target[head * rows : head * rows + rows, :] = jnp.where(keep, slab, 0.0).astype(BF)


def allowed(bounds, chunk, rows):
    low = bounds[0:1, :] - chunk * rows
    high = bounds[1:2, :] - chunk * rows
    place = lax.broadcasted_iota(jnp.int32, (rows, bounds.shape[1]), 0)
    return (place >= low) & (place <= high)


def over_chunks(where, step):
    group = pl.program_id(0)
    first, split, last = where[group], where[4 + group], where[8]
    edge = split - first

    def edges(i, carry):
        step(jnp.where(i < edge, first + i, last), True)
        return carry

    def inner(chunk, carry):
        step(chunk, False)
        return carry

    lax.fori_loop(split, last, inner, 0)
    lax.fori_loop(0, edge + 1, edges, 0)


def tiles_of(width, tile):
    return [slice(i, i + tile) for i in range(0, width, tile)]


def attend_kernel(where, q_ref, kv_ref, bound_ref, *rest, rows):
    out_ref, lse_ref, stacked, tops, totals, accs = rest[-6:]
    pairs = q_ref.shape[1] // 128
    stack_heads(q_ref, stacked, rows, False)
    lane = lax.broadcasted_iota(jnp.int32, (rows, 128), 1)
    tops[...] = jnp.full(tops.shape, NEG, F32)
    totals[...] = jnp.zeros(totals.shape, F32)
    accs[...] = jnp.zeros(accs.shape, F32)

    def step(chunk, masked):
        kv = kv_ref[chunk]
        for tile in tiles_of(2 * pairs * rows, TILE_FORTH):
            scores = dot(kv, stacked[tile, :], NT)
            if masked:
                mask = allowed(bound_ref[0, :, tile], chunk, rows)
                scores = jnp.where(mask, scores, NEG)
            top = tops[:, tile]
            peak = jnp.maximum(top, jnp.max(scores, axis=0, keepdims=True))
            fade = jnp.exp(top - peak)
            weights = jnp.exp(scores - peak)
            tops[:, tile] = peak
            totals[:, tile] = totals[:, tile] * fade + jnp.sum(
                weights, axis=0, keepdims=True
            )
            accs[:, tile] = accs[:, tile] * fade + dot(kv, weights.astype(BF), TN)[64:128]

    over_chunks(where, step)
    lse_ref[0] = tops[...] + jnp.log(totals[...])
    for pair in range(pairs):
        both = slice(pair * 2 * rows, (pair + 1) * 2 * rows)
        half = accs[:, both] / totals[:, both]
        flat = jnp.concatenate([half, half], axis=0).T
        out_ref[:, pair * 128 : pair * 128 + 128] = jnp.where(
            lane < 64, flat[:rows], flat[rows:]
        ).astype(BF)


def attend(where, queries, kv, bounds, rows, needs=()):
    shards = kv.shape[0]
    wide = queries.shape[1]
    lanes = wide // 64 * rows
    return pl.pallas_call(
        functools.partial(attend_kernel, rows=rows),
        grid_spec=pltpu.PrefetchScalarGridSpec(
            num_scalar_prefetch=1,
            grid=(4,),
            in_specs=[
                pl.BlockSpec((rows, wide), lambda g, w: (g, 0)),
                pl.BlockSpec((shards, rows, 128), lambda g, w: (0, g, 0)),
                pl.BlockSpec((1, 2, lanes), lambda g, w: (g, 0, 0)),
                *[ANYWHERE] * len(needs),
            ],
            out_specs=(
                pl.BlockSpec((rows, wide), lambda g, w: (g, 0)),
                pl.BlockSpec((1, 1, lanes), lambda g, w: (g, 0, 0)),
            ),
            scratch_shapes=[
                pltpu.VMEM((lanes, 128), BF),
                pltpu.VMEM((1, lanes), F32),
                pltpu.VMEM((1, lanes), F32),
                pltpu.VMEM((64, lanes), F32),
            ],
        ),
        out_shape=(
            jax.ShapeDtypeStruct((4 * rows, wide), BF),
            jax.ShapeDtypeStruct((4, 1, lanes), F32),
        ),
        compiler_params=params("arbitrary"),
        cost_estimate=cost("attend"),
        name="attend",
    )(where, queries, kv, bounds, *needs)


def attend_back_kernel(
    where,
    q_ref,
    kv_ref,
    bound_ref,
    up_ref,
    out_ref,
    lse_ref,
    cos_ref,
    sin_ref,
    *rest,
    rows,
):
    dq_ref, dkv_ref, stacked, upward, dq_acc, deltas = rest[-6:]
    group = pl.program_id(0)
    first, last = where[group], where[8]
    shards = kv_ref.shape[0]
    pairs = q_ref.shape[1] // 128
    stack_heads(q_ref, stacked, rows, False)
    stack_heads(up_ref, upward, rows, True)
    lane = lax.broadcasted_iota(jnp.int32, (rows, 128), 1)
    for pair in range(pairs):
        slab = up_ref[:, pair * 128 : pair * 128 + 128].astype(F32)
        slab = slab * out_ref[:, pair * 128 : pair * 128 + 128].astype(F32)
        both = jnp.concatenate(
            [jnp.where(lane < 64, slab, 0.0), jnp.where(lane < 64, 0.0, slab)], axis=0
        )
        deltas[:, pair * 2 * rows : (pair + 1) * 2 * rows] = jnp.sum(
            both.T, axis=0, keepdims=True
        )
    dq_acc[...] = jnp.zeros(dq_acc.shape, F32)

    def clear(chunk, carry):
        dkv_ref[chunk] = jnp.zeros((rows, 128), BF)
        return carry

    lax.fori_loop(0, first, clear, 0)
    lax.fori_loop(last + 1, shards, clear, 0)

    def step(chunk, masked):
        kv = kv_ref[chunk]
        total = jnp.zeros((rows, 128), F32)
        for tile in tiles_of(2 * pairs * rows, TILE_BACK):
            queries = stacked[tile, :]
            ups = upward[tile, :]
            weights = jnp.exp(dot(kv, queries, NT) - lse_ref[0, :, tile])
            if masked:
                mask = allowed(bound_ref[0, :, tile], chunk, rows)
                weights = jnp.where(mask, weights, 0.0)
            d_scores = (weights * (dot(kv, ups, NT) - deltas[:, tile])).astype(BF)
            total = total + dot(d_scores, queries) + dot(weights.astype(BF), ups)
            dq_acc[:, tile] += dot(kv, d_scores, TN)[0:64]
        dkv_ref[chunk] = total.astype(BF)

    over_chunks(where, step)
    cos_t, sin_t = cos_ref[...], sin_ref[...]
    for pair in range(pairs):
        half = dq_acc[:, pair * 2 * rows : (pair + 1) * 2 * rows]
        flat = jnp.concatenate([half, half], axis=0).T
        slab = jnp.where(lane < 64, flat[:rows], flat[rows:])
        dq_ref[:, pair * 128 : pair * 128 + 128] = turn(
            slab * HEAD_DIM**-0.5, cos_t, -sin_t
        ).astype(BF)


def attend_back(
    where, queries, kv, bounds, upstream, out, lse, cos_t, sin_t, rows, needs=()
):
    shards = kv.shape[0]
    wide = queries.shape[1]
    lanes = wide // 64 * rows
    row = lambda cols: pl.BlockSpec((rows, cols), lambda g, w: (g, 0))
    every = pl.BlockSpec((shards, rows, 128), lambda g, w: (0, g, 0))
    line = lambda count: pl.BlockSpec((1, count, lanes), lambda g, w: (g, 0, 0))
    return pl.pallas_call(
        functools.partial(attend_back_kernel, rows=rows),
        grid_spec=pltpu.PrefetchScalarGridSpec(
            num_scalar_prefetch=1,
            grid=(4,),
            in_specs=[
                row(wide),
                every,
                line(2),
                row(wide),
                row(wide),
                line(1),
                row(128),
                row(128),
                *[ANYWHERE] * len(needs),
            ],
            out_specs=(row(wide), every),
            scratch_shapes=[
                pltpu.VMEM((lanes, 128), BF),
                pltpu.VMEM((lanes, 128), BF),
                pltpu.VMEM((64, lanes), F32),
                pltpu.VMEM((1, lanes), F32),
            ],
        ),
        out_shape=(
            jax.ShapeDtypeStruct((4 * rows, wide), BF),
            jax.ShapeDtypeStruct(kv.shape, BF),
        ),
        compiler_params=params("arbitrary"),
        cost_estimate=cost("attend_back"),
        name="attend_back",
    )(where, queries, kv, bounds, upstream, out, lse, cos_t, sin_t, *needs)


def row_product(name, left, right, dims, block, needs=()):
    total = left.shape[1] if dims is TN else left.shape[0]
    cols = right.shape[0] if dims is NT else right.shape[1]
    spec = (
        along_cols(left.shape[0], block) if dims is TN else down_rows(block, left.shape[1])
    )

    def body(ins, outs, _):
        outs[0][...] = dot(ins[0][...], ins[1][...], dims).astype(BF)

    return run(
        body,
        name,
        (total // block,),
        [(left, spec), (right, whole(right.shape))],
        [(array((total, cols)), down_rows(block, cols))],
        needs,
    )[0]


def column_product(name, left, right, dims, block, needs=()):
    total = left.shape[1] if dims is TN else left.shape[0]
    cols = right.shape[0] if dims is NT else right.shape[1]
    spec = (
        down_rows(block, right.shape[1]) if dims is NT else along_cols(right.shape[0], block)
    )

    def body(ins, outs, _):
        outs[0][...] = dot(ins[0][...], ins[1][...], dims).astype(BF)

    return run(
        body,
        name,
        (cols // block,),
        [(left, whole(left.shape)), (right, spec)],
        [(array((total, cols)), along_cols(total, block))],
        needs,
    )[0]


def output_gradient_of(mixed, d_heads, block, needs):
    total, cols = d_heads.shape[0], d_heads.shape[1] // 2

    def body(ins, outs, _):
        outs[0][...] = dot(ins[0][...], ins[1][...], TN).astype(BF)

    return run(
        body,
        "output_gradient",
        (mixed.shape[1] // block,),
        [
            (mixed, along_cols(total, block)),
            (d_heads, pl.BlockSpec((total, cols), lambda i: (0, 1))),
        ],
        [(array((mixed.shape[1], cols)), down_rows(block, cols))],
        needs,
    )[0]


def gate_product(hats, w_gate, d_hidden, rows):
    depth, columns = w_gate.shape

    def body(ins, outs, _):
        for k in range(4):

            @pl.when(pl.program_id(0) == k)
            def _():
                outs[2][: rows // 2, :] = ins[2 * k][...]
                outs[2][rows // 2 :, :] = ins[2 * k + 1][...]

        gate = dot(outs[2][...], ins[8][...])
        outs[0][...] = gate.astype(BF)
        outs[1][...] = (ins[9][...].astype(F32) * gate * jax.nn.sigmoid(gate)).astype(BF)

    return run(
        body,
        "gate_product",
        (4,),
        [(h, whole(h.shape)) for h in hats]
        + [(w_gate, whole(w_gate.shape)), (d_hidden, down_rows(rows, columns))],
        [(array((4 * rows, cols)), down_rows(rows, cols)) for cols in (columns, columns, depth)],
    )


def up_product(chunks, hat, w_up, gate, d_hidden, rows, needs, before=()):
    columns = w_up.shape[1]
    first = chunks[0]

    def body(ins, outs, _):
        up = dot(ins[0][...], ins[1][...])
        gate = ins[2][...].astype(F32)
        sigma = jax.nn.sigmoid(gate)
        silu = gate * sigma
        outs[0][...] = (silu * up).astype(BF)
        slope = sigma + silu * (1.0 - sigma)
        outs[1][...] = (ins[3][...].astype(F32) * up * slope).astype(BF)

    spec = lambda cols: pl.BlockSpec((rows, cols), lambda i: (first + i, 0))
    ins = [
        (hat, spec(hat.shape[1])),
        (w_up, whole(w_up.shape)),
        (gate, spec(columns)),
        (d_hidden, spec(columns)),
    ]
    return run(
        body,
        "up_product",
        (len(chunks),),
        ins + [(b, ANYWHERE) for b in before],
        [(array((4 * rows, columns)), spec(columns))] * 2,
        needs,
        aliases={len(ins) + i: i for i in range(len(before))},
    )


def chunk_outs(chunks, rows, cols, block):
    outs = []
    for k in chunks:
        parts = 1 if k == 0 else 2
        outs += [(array((rows // parts, cols)), along_cols(rows // parts, block))] * parts
    return outs


def put_chunk(outs, value):
    rows = outs[0].shape[0]
    if rows == value.shape[0]:
        outs[0][...] = value.astype(BF)
        return outs[1:]
    outs[0][...] = value[:rows].astype(BF)
    outs[1][...] = value[rows:].astype(BF)
    return outs[2:]


def back_product(chunks, d_gate, d_up, w_gate, w_up, rows, needs=()):
    depth, columns = w_gate.shape
    block = depth // 4
    count = len(chunks)

    def body(ins, outs, _):
        w_one, w_two = ins[2 * count][...], ins[2 * count + 1][...]
        left = outs
        for i in range(count):
            left = put_chunk(
                left, dot(ins[i][...], w_one, NT) + dot(ins[count + i][...], w_two, NT)
            )

    return run(
        body,
        "back_first" if 3 in chunks else "back_product",
        (depth // block,),
        [(d_gate, down_rows(rows, columns, k)) for k in chunks]
        + [(d_up, down_rows(rows, columns, k)) for k in chunks]
        + [(w_gate, down_rows(block, columns)), (w_up, down_rows(block, columns))],
        chunk_outs(chunks, rows, depth, block),
        needs,
    )


def down_product(hidden, w_down, rows, needs):
    columns, depth = w_down.shape
    block = depth // 4

    def body(ins, outs, _):
        left = outs
        for k in range(4):
            left = put_chunk(left, dot(ins[0][k * rows : (k + 1) * rows, :], ins[1][...]))

    return run(
        body,
        "down_product",
        (4,),
        [(hidden, whole(hidden.shape)), (w_down, along_cols(columns, block))],
        chunk_outs(range(4), rows, depth, block),
        needs,
    )


def spans(spot, count, size):
    return [pl.ds(pl.multiple_of(spot[1 + k], 128), size) for k in range(count)]


def output_product(spot, mixes, w_outs, tokens):
    rows, depth = tokens.shape
    quarter = depth // 4
    flat = [w for pair in w_outs for w in pair]
    count = spot.shape[0] - 1

    def body(ins, outs, scratch):
        mine = ins[0][0]
        blocks = spans(ins[0], count, depth // count)
        mix, weights, x = ins[1:5], ins[5:13], ins[13]
        mixed_one, mixed_two, middle, hat_one, hat_two = outs
        mixed = scratch[0]
        half = rows // 2
        place = lambda k: pl.ds(pl.multiple_of((mine ^ k) * quarter, 128), quarter)
        for k in range(4):
            mixed[:, place(k)] = mix[k][...]
        mixed_one[...] = mixed[:half, :]
        mixed_two[...] = mixed[half:, :]
        sides = [mixed[:, block] for block in blocks]
        near = jnp.concatenate(sides[: count // 2], axis=1)
        other = jnp.concatenate(sides[count // 2 :], axis=1)
        for k in range(4):
            part = dot(near, weights[2 * k][...]) + dot(other, weights[2 * k + 1][...])
            middle[:, place(k)] = part + x[:, place(k)].astype(F32)
        value = middle[...]
        scale = lax.rsqrt(jnp.mean(value * value, axis=1, keepdims=True) + EPS)
        hat_one[...] = (value * scale)[:half].astype(BF)
        hat_two[...] = (value * scale)[half:].astype(BF)

    piece = (array((rows // 2, depth)), INSIDE)
    return run(
        body,
        "output_product",
        (),
        [(spot, SCALARS)] + [(v, INSIDE) for v in (*mixes, *flat, tokens)],
        [piece, piece, (array((rows, depth), F32), INSIDE), piece, piece],
        scratch=[pltpu.VMEM((rows, depth), BF)],
    )


def sum_parts(parts):
    own, *others = (p[...].astype(F32) for p in parts)
    return own + jnp.concatenate([others[0] + others[2], others[1] + others[3]], axis=0)


def norm_back(upstream, value):
    scale = lax.rsqrt(jnp.mean(value * value, axis=1, keepdims=True) + EPS)
    inner = jnp.mean(upstream * value, axis=1, keepdims=True)
    return scale * upstream - value * (scale * scale * scale * inner)


def middle_back(spot, parts, middle, dy, w_outs, needs):
    rows, depth = middle.shape
    quarter = depth // 4
    flat = [w for pair in w_outs for w in pair]
    count = spot.shape[0] - 1

    def body(ins, outs, scratch):
        mine = ins[0][0]
        blocks = spans(ins[0], count, depth // count)
        value, grad = ins[6:8]
        weights = ins[8:16]
        d_mixed, d_all = scratch
        upstream = sum_parts(ins[1:6])
        d_middle = grad[...].astype(F32) + norm_back(upstream, value[...])
        outs[0][...] = d_middle
        d_all[...] = d_middle.astype(BF)
        place = lambda k: pl.ds(pl.multiple_of((mine ^ k) * quarter, 128), quarter)
        near, other = 0.0, 0.0
        for k in range(4):
            part = d_all[:, place(k)]
            outs[1 + k][:, quarter:] = part
            near = near + dot(part, weights[2 * k][...], NT)
            other = other + dot(part, weights[2 * k + 1][...], NT)
        both = jnp.concatenate([near, other], axis=1).astype(BF)
        for k, block in enumerate(blocks):
            d_mixed[:, block] = both[:, k * (depth // count) : (k + 1) * (depth // count)]
        for k in range(4):
            outs[1 + k][:, :quarter] = d_mixed[:, place(k)]

    return run(
        body,
        "middle_back",
        (),
        [(spot, SCALARS)] + [(v, INSIDE) for v in (*parts, middle, dy, *flat)],
        [(array((rows, depth), F32), INSIDE)] + [(array((rows, 2 * quarter)), INSIDE)] * 4,
        needs,
        [pltpu.VMEM((rows, depth), BF), pltpu.VMEM((rows, depth), BF)],
    )


def project_back(dq, d_kv, cos_t, sin_t, weight, rows, hat, before):
    depth, wide = weight.shape
    block = depth // 4
    first = before.shape[1]

    def body(ins, outs, scratch):
        dq_ref, kv_ref, cos_ref, sin_ref, w_ref, hat_ref, before_ref = ins
        joined = scratch[0]

        @pl.when(pl.program_id(0) == 0)
        def _():
            joined[:, : wide - 128] = dq_ref[...]
            values = kv_ref[...].astype(F32)
            lane = lax.broadcasted_iota(jnp.int32, values.shape, 1)
            turned = turn(values, cos_ref[...], -sin_ref[...])
            joined[:, wide - 128 :] = jnp.where(lane < 64, turned, values).astype(BF)

        outs[0][:, :first] = before_ref[...]
        outs[0][:, first:] = dot(hat_ref[...], joined[...], TN).astype(BF)
        left = outs[1:]
        for k in range(4):
            left = put_chunk(
                left, dot(joined[k * rows : (k + 1) * rows, :], w_ref[...], NT)
            )

    return run(
        body,
        "project_back",
        (4,),
        [(v, whole(v.shape)) for v in (dq, d_kv, cos_t, sin_t)]
        + [
            (weight, down_rows(block, wide)),
            (hat, along_cols(4 * rows, block)),
            (before, down_rows(block, first)),
        ],
        [(array((depth, first + wide)), down_rows(block, first + wide))]
        + chunk_outs(range(4), rows, depth, block),
        scratch=[pltpu.VMEM((4 * rows, wide), BF)],
    )


def sum_output(parts, middle, needs):
    def body(ins, outs, _):
        outs[0][...] = (sum_parts(ins[:5]) + ins[5][...]).astype(BF)

    return run(
        body,
        "sum_output",
        (),
        [(v, INSIDE) for v in (*parts, middle)],
        [(array(middle.shape), INSIDE)],
        needs,
    )[0]


def sum_tokens(parts, tokens, d_middle, needs=()):
    def body(ins, outs, _):
        outs[0][...] = ins[6][...] + norm_back(sum_parts(ins[:5]), ins[5][...].astype(F32))

    return run(
        body,
        "sum_tokens",
        (),
        [(v, INSIDE) for v in (*parts, tokens, d_middle)],
        [(array(tokens.shape, F32), INSIDE)],
        needs,
    )[0]


def down_rows_in_order(spot, parts, needs):
    rows, cols = parts[0].shape
    if rows % 16:
        return in_order(parts, 0, F32)

    def body(ins, outs, _):
        for k in range(4):
            first = pl.multiple_of((ins[0][0] ^ k) * rows, 16)
            outs[0][pl.ds(first, rows), :] = ins[1 + k][...].astype(F32)

    return run(
        body,
        "finish",
        (),
        [(spot, SCALARS)] + [(v, INSIDE) for v in parts],
        [(array((4 * rows, cols), F32), INSIDE)],
        needs,
    )[0]


def finish_attention(mine, parts, gain, output, query, key, value):
    rows, depth = output.shape
    quarter, wide = depth // 4, query.shape[1] // 4
    weights = (query, key, value)

    def body(ins, outs, scratch):
        scale, total = ins[5][...], 0.0
        joined = scratch[0]
        for k in range(4):
            joined[ins[0][0] ^ k] = ins[1 + k][...]
        begin = 0
        for i, size in enumerate((quarter, wide, HEAD_DIM, HEAD_DIM)):
            raw = jnp.concatenate(
                [joined[k][:, begin : begin + size].astype(F32) for k in range(4)], axis=1
            )
            begin += size
            if i == 0:
                outs[0][...] = raw
            else:
                weight = ins[5 + i][...].astype(F32)
                total = total + jnp.sum(raw * weight, axis=1, keepdims=True)
                outs[i][...] = raw * scale
        outs[4][...] = total

    return run(
        body,
        "finish",
        (),
        [(mine, SCALARS)] + [(v, INSIDE) for v in (*parts, gain, *weights)],
        [(array(w.shape, F32), INSIDE) for w in (output, *weights)]
        + [(array((rows, 1), F32), INSIDE)],
        scratch=[pltpu.VMEM((4, rows, parts[0].shape[1]), BF)],
    )


def hop(value, step):
    return lax.ppermute(value, "dp", [(i, i ^ step) for i in range(4)])


def gather_halves(one, two, hold=()):
    next_two, other_one = hop(two, 1), hop(one, 2)
    next_one, other_two = hop(one, 1), hop(two, 2)
    if hold:
        hold = (*hold, next_one, other_two)
        next_two, other_one = tie(next_two, *hold), tie(other_one, *hold)
    far = [hop(other_one, 1), hop(next_two, 2)]
    return [one, two, next_one, next_two, other_one, other_two, *far]


def gather_plane(value, hold=()):
    half = value.shape[0] // 2
    one = hop(value, 1)
    two = hop(value, 2)
    if hold:
        one, two = tie(one, *hold), tie(two, *hold)
    return [value, one, two, hop(two[:half], 1), hop(one[half:], 2)]


def join(parts):
    return jnp.concatenate(parts, axis=0)


def gather_direct(value):
    return [value] + [hop(value, k) for k in range(1, 4)]


def reduce_first(parts):
    return hop(parts[5], 1), hop(parts[6], 2)


def reduce_plain(parts, hold=None):
    one_a, two_b = parts[1], parts[4]
    if hold is not None:
        one_a, two_b = tie(one_a, hold), tie(two_b, hold)
    return hop(one_a, 1), hop(two_b, 2)


def reduce_second(parts, came, needs=()):
    own, _, one_b, two_a = parts[:4]
    by_one, by_two, next_a, other_b = came

    def body(ins, outs, _):
        for k in range(2):
            outs[k][...] = (ins[k][...].astype(F32) + ins[2 + k][...].astype(F32)).astype(BF)

    one_b, two_a = run(
        body,
        "merge",
        (),
        [(v, INSIDE) for v in (one_b, two_a, by_two, by_one)],
        [(array(one_b.shape), INSIDE)] * 2,
        needs,
    )
    return one_b, (own, next_a, hop(one_b, 1), hop(two_a, 2), other_b)


def core_swap(value):
    size = lax.axis_size("seq")
    return lax.ppermute(value, "seq", [(i, i ^ 1) for i in range(size)])


def in_order(parts, axis, dtype=None):
    mine = lax.axis_index("dp")
    shape = list(parts[0].shape)
    size = shape[axis]
    shape[axis] = 4 * size
    out = jnp.zeros(shape, dtype or parts[0].dtype)
    for k, part in enumerate(parts):
        out = lax.dynamic_update_slice_in_dim(
            out, part.astype(out.dtype), (mine ^ k) * size, axis
        )
    return out


def local(
    tokens,
    lengths,
    attention_gain,
    query_weight,
    key_weight,
    value_weight,
    output_weight,
    feedforward_gain,
    gate_weight,
    up_weight,
    down_weight,
    cotangent,
):
    rows, depth = tokens.shape
    shards = lax.axis_size("seq")
    mine = lax.axis_index("dp")
    place = lax.axis_index("seq")
    core = place % 2
    wide = HEADS // KV_HEADS * HEAD_DIM
    side = depth // 2
    near = lambda v: lax.all_gather(v, "seq", axis=0, tiled=True)
    far = lambda v: lax.psum_scatter(v, "seq", scatter_dimension=0, tiled=True)

    gain_a = attention_gain.astype(F32)[:, None]
    gain_f = feedforward_gain.astype(F32)[:, None]
    own_qkv = jnp.concatenate(
        [
            lax.dynamic_slice_in_dim(query_weight, mine * wide, wide, 1),
            lax.dynamic_slice_in_dim(key_weight, mine * HEAD_DIM, HEAD_DIM, 1),
            lax.dynamic_slice_in_dim(value_weight, mine * HEAD_DIM, HEAD_DIM, 1),
        ],
        axis=1,
    )
    w_qkv = near((own_qkv.astype(F32) * gain_a).astype(BF))
    own_block = lax.dynamic_slice_in_dim(
        output_weight, mine * (depth // 4), depth // 4, 1
    )
    sizes = join([lengths] + [hop(lengths, k) for k in range(1, 4)])
    xs = gather_plane(tokens)
    own_out = near(tie(own_block, w_qkv, xs[1], xs[2], sizes))
    spot = jnp.stack([mine, core * side, (1 - core) * side])
    piece = down_weight.shape[0] // 4
    w_down = near(lax.dynamic_slice_in_dim(down_weight, mine * piece, piece, 0))
    own_gate, own_up = pick_columns(mine[None], gain_f, gate_weight, up_weight, shards)
    w_gate = near(own_gate)
    w_up = near(own_up)

    count = sizes.shape[1]
    before = jnp.arange(count)[:, None] <= jnp.arange(count)[None, :]
    ends = jnp.sum(jnp.where(before[None], sizes[:, :, None], 0), axis=1)
    index = place * rows + jnp.arange(rows, dtype=jnp.int32)
    passed = ends[:, None, :] <= index[None, :, None]
    begin = jnp.max(jnp.where(passed, ends[:, None, :], 0), axis=2)
    position = (index[None, :] - begin).astype(F32).reshape(4 * rows)
    half = HEAD_DIM // 2
    inverse = ROPE_BASE ** (-jnp.arange(half, dtype=F32) * 2.0 / HEAD_DIM)
    theta = position[:, None] * inverse[None, :]
    cos_h, sin_h = jnp.cos(theta), jnp.sin(theta)
    cos_t = jnp.concatenate([cos_h] * 4, axis=1)
    sin_t = jnp.concatenate([-sin_h, sin_h] * 2, axis=1)
    bounds = jnp.stack([begin, jnp.broadcast_to(index[None, :], begin.shape)], axis=1)
    bounds = jnp.concatenate([bounds] * (wide // HEAD_DIM), axis=2)
    low = begin[:, 0] // rows
    split = jnp.clip((begin[:, rows - 1] + rows - 1) // rows, low, place)
    where = jnp.concatenate([low, split, place[None]])

    made = ()
    for k, pieces in enumerate((xs[0:1], xs[1:2], xs[2:3], xs[3:5])):
        made = project(k, pieces, w_qkv, cos_t, sin_t, rows, made)
    hat, queries, own_kv = made
    own_half, own_rest = (
        lax.dynamic_slice_in_dim(own_out, c * side, side, 0) for c in (core, 1 - core)
    )
    kv = lax.all_gather(tie(own_kv, own_half), "seq", axis=0)
    own_half = tie(own_half, xs[3], xs[4])
    own_half, got_one, got_two, far_one, far_two = gather_plane(own_half)
    got = [own_half, got_one, got_two]
    swapped = [own_rest, core_swap(got_one), core_swap(got_two)]
    dy_own = tie(cotangent, got_one, got_two)
    dy_one, dy_two = hop(dy_own, 1), hop(dy_own, 2)
    mixed_heads, lse = attend(
        where, queries, kv, bounds, rows, (got_one, got_two, *swapped[1:])
    )
    mixed_heads = tie(mixed_heads, far_one, far_two, dy_one, dy_two)
    got.append(join([tie(far_one, mixed_heads), far_two]))
    swapped.append(core_swap(got[3]))
    w_outs = list(zip(got, swapped, strict=True))
    mixes = [mixed_heads[:rows]] + [
        hop(mixed_heads[k * rows : (k + 1) * rows], k) for k in range(1, 4)
    ]
    mixed_one, mixed_two, middle, hat_one, hat_two = output_product(
        spot, mixes, w_outs, tokens
    )

    part = rows // 2
    dy_far = hop(tie(dy_two[:part], *mixes), 1), hop(tie(dy_one[part:], *mixes), 2)
    dy_all = join([tie(dy_own, hat_one), dy_one, dy_two, *dy_far])
    d_hidden = row_product("hidden_back", dy_all, w_down, NT, rows, (hat_two,))
    hats = gather_halves(hat_one, hat_two, (d_hidden,))
    mixes_all = gather_halves(tie(mixed_one, *hats[6:]), tie(mixed_two, *hats[6:]))
    gate, d_up, hat_all = gate_product(hats, w_gate, d_hidden, rows)
    up_raw = row_product("up_gradient", hat_all, d_up, TN, wide)
    up_part = far(up_raw)
    ups_of = functools.partial(
        up_product, hat=hat_all, w_up=w_up, gate=gate, d_hidden=d_hidden, rows=rows
    )
    back = functools.partial(back_product, d_up=d_up, w_gate=w_gate, w_up=w_up, rows=rows)
    some = ups_of((3,), needs=(up_raw, *mixes_all[2:6]))
    far_one, far_two = back((3,), d_gate=some[1], needs=mixes_all[6:])
    hidden, d_gate = ups_of((0, 1, 2), needs=(far_one,), before=some)
    came = reduce_first([None] * 5 + [far_one, far_two])
    down_raw = column_product("down_gradient", hidden, dy_all, TN, wide)
    down_part = far(down_raw)
    sides = back((1, 2), d_gate=d_gate, needs=(down_raw, *came))
    came += reduce_plain((None, *sides))
    first, terms = reduce_second((None, *sides), came)
    (d_own,) = back((0,), d_gate=d_gate, needs=(first,))
    terms = (d_own, *terms[1:])
    mixed_all = join(mixes_all)
    d_middle, *blocks = middle_back(
        spot, terms, middle, cotangent, w_outs, (up_part, mixed_all)
    )

    d_heads = join([blocks[0]] + [hop(blocks[k], k) for k in range(1, 4)])
    gate_raw = row_product("gate_gradient", hat_all, d_gate, TN, wide, (blocks[0],))
    gate_part = far(gate_raw)
    outs = down_product(hidden, w_down, rows, (gate_raw,))
    ups_one, ups_two = hop(up_part, 1), hop(up_part, 2)
    dq, dkv = attend_back(
        where, queries, kv, bounds, d_heads, mixed_heads, lse, cos_t, sin_t, rows, (outs[6], ups_one, ups_two)
    )
    came = reduce_first(outs)
    downs_one, downs_two = hop(down_part, 1), hop(down_part, 2)
    ups_far = hop(up_part, 3)
    dkv = tie(dkv, gate_part, *came, downs_one, downs_two, ups_far)
    came += reduce_plain(outs, dkv)
    own_dkv = far(dkv.reshape(shards * 4 * rows, 128))
    first, terms = reduce_second(outs, came, (dkv,))
    out_raw = output_gradient_of(mixed_all, d_heads, wide, (first,))
    downs_far = hop(tie(down_part, dkv), 3)
    own_dkv = tie(own_dkv, out_raw, *terms[1:], downs_far)
    gate_part = tie(gate_part, own_dkv)
    gates_one, gates_two = hop(gate_part, 1), hop(gate_part, 2)
    both_raw, *fs = project_back(
        dq, own_dkv, cos_t, sin_t, w_qkv, rows, hat, out_raw
    )
    fs[5], fs[6] = (tie(f, gates_one, gates_two) for f in fs[5:])
    both_part = far(both_raw)
    layer_output = sum_output(terms, middle, (fs[6],))
    came = (*reduce_first(fs), *reduce_plain(fs))
    first, terms = reduce_second(fs, came, came[2:])
    half_rows = gate_part.shape[0] // 2
    gates_one, gates_two = tie(gates_one, first), tie(gates_two, first)
    gates_far = [hop(gates_two[:half_rows], 1), hop(gates_one[half_rows:], 2)]
    token_gradient = sum_tokens(terms, tokens, d_middle)

    gate_gradient, gain_g = spread_columns(
        "spread_gate",
        mine[None],
        jnp.stack([gate_part, gates_one, gates_two, join(gates_far)]),
        gain_f,
        gate_weight,
        shards,
    )
    up_gradient, gain_u = spread_columns(
        "spread_up", mine[None], jnp.stack([tie(up_part, both_raw), ups_one, ups_two, ups_far]), gain_f, up_weight, shards
    )
    down_gradient = down_rows_in_order(
        spot, [down_part, downs_one, downs_two, downs_far], (both_raw,)
    )
    gradients = finish_attention(
        mine[None],
        gather_direct(both_part),
        gain_a,
        output_weight,
        query_weight,
        key_weight,
        value_weight,
    )
    output_gradient, query_gradient, key_gradient, value_gradient, gain_a_gradient = gradients
    return (
        layer_output,
        token_gradient,
        gain_a_gradient[:, 0],
        query_gradient,
        key_gradient,
        value_gradient,
        output_gradient,
        (gain_g + gain_u)[:, 0],
        gate_gradient,
        up_gradient,
        down_gradient,
    )


def solution(mesh):
    both = P(("dp", "seq"), None)
    flat = P("seq")
    split = P("seq", None)
    return jax.shard_map(
        local,
        mesh=mesh,
        in_specs=(
            both,
            P("dp", None),
            flat,
            split,
            split,
            split,
            split,
            flat,
            split,
            split,
            split,
            both,
        ),
        out_specs=(
            both,
            both,
            flat,
            split,
            split,
            split,
            split,
            flat,
            split,
            split,
            split,
        ),
        check_vma=False,
    )
```

```python
import functools

import jax
import jax.numpy as jnp
from jax import lax
from jax.experimental import pallas as pl
from jax.experimental.pallas import tpu as pltpu
from jax.sharding import PartitionSpec as P

HEADS = 32
HEAD_DIM = 64
KV_HEADS = 4
EPS = 1e-05
ROPE_BASE = 10000.0
NEG = -1e30
TILE_FORTH = 2560
TILE_BACK = 2560
VMEM_LIMIT = 56 * 2**20
BF = jnp.bfloat16
F32 = jnp.float32

NT = (((1,), (1,)), ((), ()))
TN = (((0,), (0,)), ((), ()))
NN = (((1,), (0,)), ((), ()))


def dot(left, right, dims=NN):
    return lax.dot_general(left, right, dims, preferred_element_type=F32)


def params(*semantics):
    return pltpu.CompilerParams(
        dimension_semantics=semantics, vmem_limit_bytes=VMEM_LIMIT
    )


FREE = pl.CostEstimate(flops=1, bytes_accessed=1, transcendentals=0)
TIMES = {
    "project": 0.1,
    "attend": 400,
    "attend_back": 1000,
    "merge": 1,
    "output_product": 3,
    "hidden_back": 4,
    "gate_product": 2,
    "up_gradient": 2,
    "up_product": 100,
    "back_product": 4,
    "back_first": 4,
    "down_gradient": 0.2,
    "gate_gradient": 2,
    "middle_back": 200,
    "down_product": 4,
    "output_gradient": 2,
    "project_back": 50,
    "join_gradients": 50,
    "sum_output": 100,
    "sum_tokens": 100,
    "spread_up": 300,
    "spread_gate": 0.1,
    "pick_columns": 2,
    "finish": 3,
}


def cost(name):
    time = TIMES[name]
    return pl.CostEstimate(
        flops=int(time * 8e8), bytes_accessed=int(time * 2.5e6), transcendentals=0
    )
ANYWHERE = pl.BlockSpec(memory_space=pl.ANY)
SCALARS = pl.BlockSpec(memory_space=pltpu.SMEM)
INSIDE = pl.BlockSpec(memory_space=pltpu.VMEM)


def array(shape, dtype=BF):
    return jax.ShapeDtypeStruct(tuple(shape), dtype)


def tie(value, *others):
    return pl.pallas_call(
        lambda *refs: None,
        out_shape=array(value.shape, value.dtype),
        in_specs=[ANYWHERE] * (1 + len(others)),
        out_specs=ANYWHERE,
        input_output_aliases={0: 0},
        cost_estimate=FREE,
        name="tie",
    )(value, *others)


def run(body, name, grid, ins, outs, needs=(), scratch=(), aliases=None):
    count, made = len(ins), len(outs)

    def kernel(*refs):
        body(refs[:count], refs[count + len(needs) :][:made], refs[count + len(needs) + made :])

    result = pl.pallas_call(
        kernel,
        grid=grid,
        out_shape=tuple(shape for shape, _ in outs),
        in_specs=[spec for _, spec in ins] + [ANYWHERE] * len(needs),
        out_specs=tuple(spec for _, spec in outs),
        scratch_shapes=list(scratch),
        input_output_aliases=aliases or {},
        compiler_params=params(*["arbitrary"] * len(grid)),
        cost_estimate=cost(name),
        name=name,
    )(*[value for value, _ in ins], *needs)
    return result


def whole(shape):
    return pl.BlockSpec(tuple(shape), lambda i: (0,) * len(shape), pipeline_mode=pl.Buffered(1))


def down_rows(rows, cols, at=None):
    return pl.BlockSpec((rows, cols), (lambda i: (i, 0)) if at is None else (lambda i: (at, 0)))


def along_cols(rows, cols, at=0):
    return pl.BlockSpec((rows, cols), lambda i: (at, i))


def pick_kernel(which, gain, gate, up, gate_out, up_out, *, shards):
    piece = gate.shape[1] // (4 * shards)
    scale = gain[...]
    for quarter in range(4):

        @pl.when(which[0] == quarter)
        def _():
            for source, out in ((gate, gate_out), (up, up_out)):
                whole = source[...].astype(F32) * scale
                parts = []
                for shard in range(shards):
                    first = (shard * 4 + quarter) * piece
                    parts.append(whole[:, first : first + piece])
                out[...] = jnp.concatenate(parts, axis=1).astype(BF)


def pick_columns(quarter, gain, gate, up, shards):
    rows, width = gate.shape
    vmem = pl.BlockSpec(memory_space=pltpu.VMEM)
    shape = jax.ShapeDtypeStruct((rows, width // 4), BF)
    return pl.pallas_call(
        functools.partial(pick_kernel, shards=shards),
        out_shape=(shape, shape),
        in_specs=[pl.BlockSpec(memory_space=pltpu.SMEM), vmem, vmem, vmem],
        out_specs=(vmem, vmem),
        compiler_params=params(),
        cost_estimate=cost("pick_columns"),
        name="pick_columns",
    )(quarter, gain, gate, up)


def spread_kernel(which, grads, gain, weight, out, gain_out, *, shards):
    piece = grads.shape[2] // shards
    chunks = [grads[which[0] ^ quarter].astype(F32) for quarter in range(4)]
    whole = jnp.concatenate(
        [
            chunks[quarter][:, shard * piece : (shard + 1) * piece]
            for shard in range(shards)
            for quarter in range(4)
        ],
        axis=1,
    )
    gain_out[...] = jnp.sum(whole * weight[...].astype(F32), axis=1, keepdims=True)
    out[...] = whole * gain[...]


def spread_columns(name, mine, grads, gain, weight, shards):
    rows, width = weight.shape
    block = min(rows, 64)
    row = lambda cols: pl.BlockSpec((block, cols), lambda i: (i, 0))
    return pl.pallas_call(
        functools.partial(spread_kernel, shards=shards),
        grid=(rows // block,),
        out_shape=(
            jax.ShapeDtypeStruct((rows, width), F32),
            jax.ShapeDtypeStruct((rows, 1), F32),
        ),
        in_specs=[
            pl.BlockSpec(memory_space=pltpu.SMEM),
            pl.BlockSpec((4, block, width // 4), lambda i: (0, i, 0)),
            row(1),
            row(width),
        ],
        out_specs=(row(width), row(1)),
        compiler_params=params("arbitrary"),
        cost_estimate=cost(name),
        name=name,
    )(mine, grads, gain, weight)


def turn(values, cos_t, sin_t):
    lane = lax.broadcasted_iota(jnp.int32, values.shape, 1)
    other = jnp.where(
        lane % 64 < 32, pltpu.roll(values, 96, 1), pltpu.roll(values, 32, 1)
    )
    return values * cos_t + other * sin_t


def project_kernel(ins, outs, _):
    *xs, w_ref, cos_ref, sin_ref = ins
    hat_ref, q_ref, kv_ref = outs
    rows = hat_ref.shape[0] // len(xs)
    for i, x_ref in enumerate(xs):
        span = slice(i * rows, (i + 1) * rows)
        x = x_ref[...].astype(F32)
        scale = lax.rsqrt(jnp.mean(x * x, axis=1, keepdims=True) + EPS)
        hat_ref[span, :] = (x * scale).astype(BF)
    out = dot(hat_ref[...], w_ref[...])
    cos_t, sin_t = cos_ref[...], sin_ref[...]
    wide = q_ref.shape[1]
    for pair in range(wide // 128):
        part = turn(out[:, pair * 128 : pair * 128 + 128], cos_t, sin_t)
        q_ref[:, pair * 128 : pair * 128 + 128] = (part * HEAD_DIM**-0.5).astype(BF)
    kv = out[:, wide : wide + 128]
    lane = lax.broadcasted_iota(jnp.int32, kv.shape, 1)
    kv_ref[...] = jnp.where(lane < 64, turn(kv, cos_t, sin_t), kv).astype(BF)


def project(chunk, xs, weight, cos_t, sin_t, rows, before=()):
    depth, wide = weight.shape[0], weight.shape[1] - 128
    ins = [(x, whole(x.shape)) for x in xs] + [
        (weight, whole(weight.shape)),
        (cos_t, down_rows(rows, 128, chunk)),
        (sin_t, down_rows(rows, 128, chunk)),
    ]

    def body(refs, outs, scratch):
        project_kernel(refs[: len(xs) + 3], outs, scratch)

    first = len(ins)
    return run(
        body,
        "project",
        (1,),
        ins + [(b, ANYWHERE) for b in before],
        [
            (array((4 * rows, cols)), down_rows(rows, cols, chunk))
            for cols in (depth, wide, 128)
        ],
        aliases={first + i: i for i in range(len(before))},
    )


def stack_heads(source, target, rows, upper):
    lane = lax.broadcasted_iota(jnp.int32, (rows, 128), 1)
    keep = (lane >= 64) if upper else (lane < 64)
    for head in range(source.shape[1] // 64):
        slab = source[:, head // 2 * 128 : head // 2 * 128 + 128].astype(F32)
        if (head % 2 == 1) != upper:
            slab = pltpu.roll(slab, 64, 1)
        target[head * rows : head * rows + rows, :] = jnp.where(keep, slab, 0.0).astype(BF)


def allowed(bounds, chunk, rows):
    low = bounds[0:1, :] - chunk * rows
    high = bounds[1:2, :] - chunk * rows
    place = lax.broadcasted_iota(jnp.int32, (rows, bounds.shape[1]), 0)
    return (place >= low) & (place <= high)


def over_chunks(where, step):
    group = pl.program_id(0)
    first, split, last = where[group], where[4 + group], where[8]
    edge = split - first

    def edges(i, carry):
        step(jnp.where(i < edge, first + i, last), True)
        return carry

    def inner(chunk, carry):
        step(chunk, False)
        return carry

    lax.fori_loop(split, last, inner, 0)
    lax.fori_loop(0, edge + 1, edges, 0)


def tiles_of(width, tile):
    return [slice(i, i + tile) for i in range(0, width, tile)]


def attend_kernel(where, q_ref, kv_ref, bound_ref, *rest, rows):
    out_ref, lse_ref, stacked, tops, totals, accs = rest[-6:]
    pairs = q_ref.shape[1] // 128
    stack_heads(q_ref, stacked, rows, False)
    lane = lax.broadcasted_iota(jnp.int32, (rows, 128), 1)
    tops[...] = jnp.full(tops.shape, NEG, F32)
    totals[...] = jnp.zeros(totals.shape, F32)
    accs[...] = jnp.zeros(accs.shape, F32)

    def step(chunk, masked):
        kv = kv_ref[chunk]
        for tile in tiles_of(2 * pairs * rows, TILE_FORTH):
            scores = dot(kv, stacked[tile, :], NT)
            if masked:
                mask = allowed(bound_ref[0, :, tile], chunk, rows)
                scores = jnp.where(mask, scores, NEG)
            top = tops[:, tile]
            peak = jnp.maximum(top, jnp.max(scores, axis=0, keepdims=True))
            fade = jnp.exp(top - peak)
            weights = jnp.exp(scores - peak)
            tops[:, tile] = peak
            totals[:, tile] = totals[:, tile] * fade + jnp.sum(
                weights, axis=0, keepdims=True
            )
            accs[:, tile] = accs[:, tile] * fade + dot(kv, weights.astype(BF), TN)[64:128]

    over_chunks(where, step)
    lse_ref[0] = tops[...] + jnp.log(totals[...])
    for pair in range(pairs):
        both = slice(pair * 2 * rows, (pair + 1) * 2 * rows)
        half = accs[:, both] / totals[:, both]
        flat = jnp.concatenate([half, half], axis=0).T
        out_ref[:, pair * 128 : pair * 128 + 128] = jnp.where(
            lane < 64, flat[:rows], flat[rows:]
        ).astype(BF)


def attend(where, queries, kv, bounds, rows, needs=()):
    shards = kv.shape[0]
    wide = queries.shape[1]
    lanes = wide // 64 * rows
    return pl.pallas_call(
        functools.partial(attend_kernel, rows=rows),
        grid_spec=pltpu.PrefetchScalarGridSpec(
            num_scalar_prefetch=1,
            grid=(4,),
            in_specs=[
                pl.BlockSpec((rows, wide), lambda g, w: (g, 0)),
                pl.BlockSpec((shards, rows, 128), lambda g, w: (0, g, 0)),
                pl.BlockSpec((1, 2, lanes), lambda g, w: (g, 0, 0)),
                *[ANYWHERE] * len(needs),
            ],
            out_specs=(
                pl.BlockSpec((rows, wide), lambda g, w: (g, 0)),
                pl.BlockSpec((1, 1, lanes), lambda g, w: (g, 0, 0)),
            ),
            scratch_shapes=[
                pltpu.VMEM((lanes, 128), BF),
                pltpu.VMEM((1, lanes), F32),
                pltpu.VMEM((1, lanes), F32),
                pltpu.VMEM((64, lanes), F32),
            ],
        ),
        out_shape=(
            jax.ShapeDtypeStruct((4 * rows, wide), BF),
            jax.ShapeDtypeStruct((4, 1, lanes), F32),
        ),
        compiler_params=params("arbitrary"),
        cost_estimate=cost("attend"),
        name="attend",
    )(where, queries, kv, bounds, *needs)


def attend_back_kernel(
    where,
    q_ref,
    kv_ref,
    bound_ref,
    up_ref,
    out_ref,
    lse_ref,
    cos_ref,
    sin_ref,
    *rest,
    rows,
):
    dq_ref, dkv_ref, stacked, upward, dq_acc, deltas = rest[-6:]
    group = pl.program_id(0)
    first, last = where[group], where[8]
    shards = kv_ref.shape[0]
    pairs = q_ref.shape[1] // 128
    stack_heads(q_ref, stacked, rows, False)
    stack_heads(up_ref, upward, rows, True)
    lane = lax.broadcasted_iota(jnp.int32, (rows, 128), 1)
    for pair in range(pairs):
        slab = up_ref[:, pair * 128 : pair * 128 + 128].astype(F32)
        slab = slab * out_ref[:, pair * 128 : pair * 128 + 128].astype(F32)
        both = jnp.concatenate(
            [jnp.where(lane < 64, slab, 0.0), jnp.where(lane < 64, 0.0, slab)], axis=0
        )
        deltas[:, pair * 2 * rows : (pair + 1) * 2 * rows] = jnp.sum(
            both.T, axis=0, keepdims=True
        )
    dq_acc[...] = jnp.zeros(dq_acc.shape, F32)

    def clear(chunk, carry):
        dkv_ref[chunk] = jnp.zeros((rows, 128), BF)
        return carry

    lax.fori_loop(0, first, clear, 0)
    lax.fori_loop(last + 1, shards, clear, 0)

    def step(chunk, masked):
        kv = kv_ref[chunk]
        total = jnp.zeros((rows, 128), F32)
        for tile in tiles_of(2 * pairs * rows, TILE_BACK):
            queries = stacked[tile, :]
            ups = upward[tile, :]
            weights = jnp.exp(dot(kv, queries, NT) - lse_ref[0, :, tile])
            if masked:
                mask = allowed(bound_ref[0, :, tile], chunk, rows)
                weights = jnp.where(mask, weights, 0.0)
            d_scores = (weights * (dot(kv, ups, NT) - deltas[:, tile])).astype(BF)
            total = total + dot(d_scores, queries) + dot(weights.astype(BF), ups)
            dq_acc[:, tile] += dot(kv, d_scores, TN)[0:64]
        dkv_ref[chunk] = total.astype(BF)

    over_chunks(where, step)
    cos_t, sin_t = cos_ref[...], sin_ref[...]
    for pair in range(pairs):
        half = dq_acc[:, pair * 2 * rows : (pair + 1) * 2 * rows]
        flat = jnp.concatenate([half, half], axis=0).T
        slab = jnp.where(lane < 64, flat[:rows], flat[rows:])
        dq_ref[:, pair * 128 : pair * 128 + 128] = turn(
            slab * HEAD_DIM**-0.5, cos_t, -sin_t
        ).astype(BF)


def attend_back(
    where, queries, kv, bounds, upstream, out, lse, cos_t, sin_t, rows, needs=()
):
    shards = kv.shape[0]
    wide = queries.shape[1]
    lanes = wide // 64 * rows
    row = lambda cols: pl.BlockSpec((rows, cols), lambda g, w: (g, 0))
    every = pl.BlockSpec((shards, rows, 128), lambda g, w: (0, g, 0))
    line = lambda count: pl.BlockSpec((1, count, lanes), lambda g, w: (g, 0, 0))
    return pl.pallas_call(
        functools.partial(attend_back_kernel, rows=rows),
        grid_spec=pltpu.PrefetchScalarGridSpec(
            num_scalar_prefetch=1,
            grid=(4,),
            in_specs=[
                row(wide),
                every,
                line(2),
                row(wide),
                row(wide),
                line(1),
                row(128),
                row(128),
                *[ANYWHERE] * len(needs),
            ],
            out_specs=(row(wide), every),
            scratch_shapes=[
                pltpu.VMEM((lanes, 128), BF),
                pltpu.VMEM((lanes, 128), BF),
                pltpu.VMEM((64, lanes), F32),
                pltpu.VMEM((1, lanes), F32),
            ],
        ),
        out_shape=(
            jax.ShapeDtypeStruct((4 * rows, wide), BF),
            jax.ShapeDtypeStruct(kv.shape, BF),
        ),
        compiler_params=params("arbitrary"),
        cost_estimate=cost("attend_back"),
        name="attend_back",
    )(where, queries, kv, bounds, upstream, out, lse, cos_t, sin_t, *needs)


def row_product(name, left, right, dims, block, needs=()):
    total = left.shape[1] if dims is TN else left.shape[0]
    cols = right.shape[0] if dims is NT else right.shape[1]
    spec = (
        along_cols(left.shape[0], block) if dims is TN else down_rows(block, left.shape[1])
    )

    def body(ins, outs, _):
        outs[0][...] = dot(ins[0][...], ins[1][...], dims).astype(BF)

    return run(
        body,
        name,
        (total // block,),
        [(left, spec), (right, whole(right.shape))],
        [(array((total, cols)), down_rows(block, cols))],
        needs,
    )[0]


def column_product(name, left, right, dims, block, needs=()):
    total = left.shape[1] if dims is TN else left.shape[0]
    cols = right.shape[0] if dims is NT else right.shape[1]
    spec = (
        down_rows(block, right.shape[1]) if dims is NT else along_cols(right.shape[0], block)
    )

    def body(ins, outs, _):
        outs[0][...] = dot(ins[0][...], ins[1][...], dims).astype(BF)

    return run(
        body,
        name,
        (cols // block,),
        [(left, whole(left.shape)), (right, spec)],
        [(array((total, cols)), along_cols(total, block))],
        needs,
    )[0]


def output_gradient_of(mixed, d_heads, block, needs):
    total, cols = d_heads.shape[0], d_heads.shape[1] // 2

    def body(ins, outs, _):
        outs[0][...] = dot(ins[0][...], ins[1][...], TN).astype(BF)

    return run(
        body,
        "output_gradient",
        (mixed.shape[1] // block,),
        [
            (mixed, along_cols(total, block)),
            (d_heads, pl.BlockSpec((total, cols), lambda i: (0, 1))),
        ],
        [(array((mixed.shape[1], cols)), down_rows(block, cols))],
        needs,
    )[0]


def gate_product(hats, w_gate, d_hidden, rows):
    depth, columns = w_gate.shape

    def body(ins, outs, _):
        for k in range(4):

            @pl.when(pl.program_id(0) == k)
            def _():
                outs[2][: rows // 2, :] = ins[2 * k][...]
                outs[2][rows // 2 :, :] = ins[2 * k + 1][...]

        gate = dot(outs[2][...], ins[8][...])
        outs[0][...] = gate.astype(BF)
        outs[1][...] = (ins[9][...].astype(F32) * gate * jax.nn.sigmoid(gate)).astype(BF)

    return run(
        body,
        "gate_product",
        (4,),
        [(h, whole(h.shape)) for h in hats]
        + [(w_gate, whole(w_gate.shape)), (d_hidden, down_rows(rows, columns))],
        [(array((4 * rows, cols)), down_rows(rows, cols)) for cols in (columns, columns, depth)],
    )


def up_product(chunks, hat, w_up, gate, d_hidden, rows, needs, before=()):
    columns = w_up.shape[1]
    first = chunks[0]

    def body(ins, outs, _):
        up = dot(ins[0][...], ins[1][...])
        gate = ins[2][...].astype(F32)
        sigma = jax.nn.sigmoid(gate)
        silu = gate * sigma
        outs[0][...] = (silu * up).astype(BF)
        slope = sigma + silu * (1.0 - sigma)
        outs[1][...] = (ins[3][...].astype(F32) * up * slope).astype(BF)

    spec = lambda cols: pl.BlockSpec((rows, cols), lambda i: (first + i, 0))
    ins = [
        (hat, spec(hat.shape[1])),
        (w_up, whole(w_up.shape)),
        (gate, spec(columns)),
        (d_hidden, spec(columns)),
    ]
    return run(
        body,
        "up_product",
        (len(chunks),),
        ins + [(b, ANYWHERE) for b in before],
        [(array((4 * rows, columns)), spec(columns))] * 2,
        needs,
        aliases={len(ins) + i: i for i in range(len(before))},
    )


def chunk_outs(chunks, rows, cols, block):
    outs = []
    for k in chunks:
        parts = 1 if k == 0 else 2
        outs += [(array((rows // parts, cols)), along_cols(rows // parts, block))] * parts
    return outs


def put_chunk(outs, value):
    rows = outs[0].shape[0]
    if rows == value.shape[0]:
        outs[0][...] = value.astype(BF)
        return outs[1:]
    outs[0][...] = value[:rows].astype(BF)
    outs[1][...] = value[rows:].astype(BF)
    return outs[2:]


def back_product(chunks, d_gate, d_up, w_gate, w_up, rows, needs=()):
    depth, columns = w_gate.shape
    block = depth // 4
    count = len(chunks)

    def body(ins, outs, _):
        w_one, w_two = ins[2 * count][...], ins[2 * count + 1][...]
        left = outs
        for i in range(count):
            left = put_chunk(
                left, dot(ins[i][...], w_one, NT) + dot(ins[count + i][...], w_two, NT)
            )

    return run(
        body,
        "back_first" if 3 in chunks else "back_product",
        (depth // block,),
        [(d_gate, down_rows(rows, columns, k)) for k in chunks]
        + [(d_up, down_rows(rows, columns, k)) for k in chunks]
        + [(w_gate, down_rows(block, columns)), (w_up, down_rows(block, columns))],
        chunk_outs(chunks, rows, depth, block),
        needs,
    )


def down_product(hidden, w_down, rows, needs):
    columns, depth = w_down.shape
    block = depth // 4

    def body(ins, outs, _):
        left = outs
        for k in range(4):
            left = put_chunk(left, dot(ins[0][k * rows : (k + 1) * rows, :], ins[1][...]))

    return run(
        body,
        "down_product",
        (4,),
        [(hidden, whole(hidden.shape)), (w_down, along_cols(columns, block))],
        chunk_outs(range(4), rows, depth, block),
        needs,
    )


def spans(spot, count, size):
    return [pl.ds(pl.multiple_of(spot[1 + k], 128), size) for k in range(count)]


def output_product(spot, mixes, w_outs, tokens):
    rows, depth = tokens.shape
    quarter = depth // 4
    flat = [w for pair in w_outs for w in pair]
    count = spot.shape[0] - 1

    def body(ins, outs, scratch):
        mine = ins[0][0]
        blocks = spans(ins[0], count, depth // count)
        mix, weights, x = ins[1:5], ins[5:13], ins[13]
        mixed_one, mixed_two, middle, hat_one, hat_two = outs
        mixed = scratch[0]
        half = rows // 2
        place = lambda k: pl.ds(pl.multiple_of((mine ^ k) * quarter, 128), quarter)
        for k in range(4):
            mixed[:, place(k)] = mix[k][...]
        mixed_one[...] = mixed[:half, :]
        mixed_two[...] = mixed[half:, :]
        sides = [mixed[:, block] for block in blocks]
        near = jnp.concatenate(sides[: count // 2], axis=1)
        other = jnp.concatenate(sides[count // 2 :], axis=1)
        for k in range(4):
            part = dot(near, weights[2 * k][...]) + dot(other, weights[2 * k + 1][...])
            middle[:, place(k)] = part + x[:, place(k)].astype(F32)
        value = middle[...]
        scale = lax.rsqrt(jnp.mean(value * value, axis=1, keepdims=True) + EPS)
        hat_one[...] = (value * scale)[:half].astype(BF)
        hat_two[...] = (value * scale)[half:].astype(BF)

    piece = (array((rows // 2, depth)), INSIDE)
    return run(
        body,
        "output_product",
        (),
        [(spot, SCALARS)] + [(v, INSIDE) for v in (*mixes, *flat, tokens)],
        [piece, piece, (array((rows, depth), F32), INSIDE), piece, piece],
        scratch=[pltpu.VMEM((rows, depth), BF)],
    )


def sum_parts(parts):
    own, *others = (p[...].astype(F32) for p in parts)
    return own + jnp.concatenate([others[0] + others[2], others[1] + others[3]], axis=0)


def norm_back(upstream, value):
    scale = lax.rsqrt(jnp.mean(value * value, axis=1, keepdims=True) + EPS)
    inner = jnp.mean(upstream * value, axis=1, keepdims=True)
    return scale * upstream - value * (scale * scale * scale * inner)


def middle_back(spot, parts, middle, dy, w_outs, needs):
    rows, depth = middle.shape
    quarter = depth // 4
    flat = [w for pair in w_outs for w in pair]
    count = spot.shape[0] - 1

    def body(ins, outs, scratch):
        mine = ins[0][0]
        blocks = spans(ins[0], count, depth // count)
        value, grad = ins[6:8]
        weights = ins[8:16]
        d_mixed, d_all = scratch
        upstream = sum_parts(ins[1:6])
        d_middle = grad[...].astype(F32) + norm_back(upstream, value[...])
        outs[0][...] = d_middle
        d_all[...] = d_middle.astype(BF)
        place = lambda k: pl.ds(pl.multiple_of((mine ^ k) * quarter, 128), quarter)
        near, other = 0.0, 0.0
        for k in range(4):
            part = d_all[:, place(k)]
            outs[1 + k][:, quarter:] = part
            near = near + dot(part, weights[2 * k][...], NT)
            other = other + dot(part, weights[2 * k + 1][...], NT)
        both = jnp.concatenate([near, other], axis=1).astype(BF)
        for k, block in enumerate(blocks):
            d_mixed[:, block] = both[:, k * (depth // count) : (k + 1) * (depth // count)]
        for k in range(4):
            outs[1 + k][:, :quarter] = d_mixed[:, place(k)]

    return run(
        body,
        "middle_back",
        (),
        [(spot, SCALARS)] + [(v, INSIDE) for v in (*parts, middle, dy, *flat)],
        [(array((rows, depth), F32), INSIDE)] + [(array((rows, 2 * quarter)), INSIDE)] * 4,
        needs,
        [pltpu.VMEM((rows, depth), BF), pltpu.VMEM((rows, depth), BF)],
    )


def join_gradients(dq, d_kv, cos_t, sin_t, rows, hat, before):
    depth, wide = hat.shape[1], dq.shape[1] + 128
    block = depth // 4
    first = before.shape[1]

    def body(ins, outs, _):
        dq_ref, kv_ref, cos_ref, sin_ref, hat_ref, before_ref = ins
        both, joined = outs

        @pl.when(pl.program_id(0) == 0)
        def _():
            joined[:, : wide - 128] = dq_ref[...]
            values = kv_ref[...].astype(F32)
            lane = lax.broadcasted_iota(jnp.int32, values.shape, 1)
            turned = turn(values, cos_ref[...], -sin_ref[...])
            joined[:, wide - 128 :] = jnp.where(lane < 64, turned, values).astype(BF)

        both[:, :first] = before_ref[...]
        both[:, first:] = dot(hat_ref[...], joined[...], TN).astype(BF)

    return run(
        body,
        "join_gradients",
        (4,),
        [(v, whole(v.shape)) for v in (dq, d_kv, cos_t, sin_t)]
        + [(hat, along_cols(4 * rows, block)), (before, down_rows(block, first))],
        [
            (array((depth, first + wide)), down_rows(block, first + wide)),
            (array((4 * rows, wide)), whole((4 * rows, wide))),
        ],
    )


def project_back(joined, weight, rows, needs):
    depth, wide = weight.shape
    block = depth // 4

    def body(ins, outs, _):
        left = outs
        for k in range(4):
            left = put_chunk(
                left, dot(ins[0][k * rows : (k + 1) * rows, :], ins[1][...], NT)
            )

    return run(
        body,
        "project_back",
        (4,),
        [(joined, whole(joined.shape)), (weight, down_rows(block, wide))],
        chunk_outs(range(4), rows, depth, block),
        needs,
    )


def sum_output(parts, middle, needs):
    def body(ins, outs, _):
        outs[0][...] = (sum_parts(ins[:5]) + ins[5][...]).astype(BF)

    return run(
        body,
        "sum_output",
        (),
        [(v, INSIDE) for v in (*parts, middle)],
        [(array(middle.shape), INSIDE)],
        needs,
    )[0]


def sum_tokens(parts, tokens, d_middle, needs=()):
    def body(ins, outs, _):
        outs[0][...] = ins[6][...] + norm_back(sum_parts(ins[:5]), ins[5][...].astype(F32))

    return run(
        body,
        "sum_tokens",
        (),
        [(v, INSIDE) for v in (*parts, tokens, d_middle)],
        [(array(tokens.shape, F32), INSIDE)],
        needs,
    )[0]


def down_rows_in_order(spot, parts, needs):
    rows, cols = parts[0].shape
    if rows % 16:
        return in_order(parts, 0, F32)

    def body(ins, outs, _):
        for k in range(4):
            first = pl.multiple_of((ins[0][0] ^ k) * rows, 16)
            outs[0][pl.ds(first, rows), :] = ins[1 + k][...].astype(F32)

    return run(
        body,
        "finish",
        (),
        [(spot, SCALARS)] + [(v, INSIDE) for v in parts],
        [(array((4 * rows, cols), F32), INSIDE)],
        needs,
    )[0]


def finish_attention(mine, parts, gain, output, query, key, value):
    rows, depth = output.shape
    quarter, wide = depth // 4, query.shape[1] // 4
    weights = (query, key, value)

    def body(ins, outs, scratch):
        scale, total = ins[5][...], 0.0
        joined = scratch[0]
        for k in range(4):
            joined[ins[0][0] ^ k] = ins[1 + k][...]
        begin = 0
        for i, size in enumerate((quarter, wide, HEAD_DIM, HEAD_DIM)):
            raw = jnp.concatenate(
                [joined[k][:, begin : begin + size].astype(F32) for k in range(4)], axis=1
            )
            begin += size
            if i == 0:
                outs[0][...] = raw
            else:
                weight = ins[5 + i][...].astype(F32)
                total = total + jnp.sum(raw * weight, axis=1, keepdims=True)
                outs[i][...] = raw * scale
        outs[4][...] = total

    return run(
        body,
        "finish",
        (),
        [(mine, SCALARS)] + [(v, INSIDE) for v in (*parts, gain, *weights)],
        [(array(w.shape, F32), INSIDE) for w in (output, *weights)]
        + [(array((rows, 1), F32), INSIDE)],
        scratch=[pltpu.VMEM((4, rows, parts[0].shape[1]), BF)],
    )


def hop(value, step):
    return lax.ppermute(value, "dp", [(i, i ^ step) for i in range(4)])


def gather_halves(one, two, hold=()):
    next_two, other_one = hop(two, 1), hop(one, 2)
    next_one, other_two = hop(one, 1), hop(two, 2)
    if hold:
        hold = (*hold, next_one, other_two)
        next_two, other_one = tie(next_two, *hold), tie(other_one, *hold)
    far = [hop(other_one, 1), hop(next_two, 2)]
    return [one, two, next_one, next_two, other_one, other_two, *far]


def gather_plane(value, hold=()):
    half = value.shape[0] // 2
    one = hop(value, 1)
    two = hop(value, 2)
    if hold:
        one, two = tie(one, *hold), tie(two, *hold)
    return [value, one, two, hop(two[:half], 1), hop(one[half:], 2)]


def join(parts):
    return jnp.concatenate(parts, axis=0)


def gather_direct(value):
    return [value] + [hop(value, k) for k in range(1, 4)]


def reduce_first(parts):
    return hop(parts[5], 1), hop(parts[6], 2)


def reduce_plain(parts, hold=None):
    one_a, two_b = parts[1], parts[4]
    if hold is not None:
        one_a, two_b = tie(one_a, hold), tie(two_b, hold)
    return hop(one_a, 1), hop(two_b, 2)


def reduce_second(parts, came, needs=()):
    own, _, one_b, two_a = parts[:4]
    by_one, by_two, next_a, other_b = came

    def body(ins, outs, _):
        for k in range(2):
            outs[k][...] = (ins[k][...].astype(F32) + ins[2 + k][...].astype(F32)).astype(BF)

    one_b, two_a = run(
        body,
        "merge",
        (),
        [(v, INSIDE) for v in (one_b, two_a, by_two, by_one)],
        [(array(one_b.shape), INSIDE)] * 2,
        needs,
    )
    return one_b, (own, next_a, hop(one_b, 1), hop(two_a, 2), other_b)


def core_swap(value):
    size = lax.axis_size("seq")
    return lax.ppermute(value, "seq", [(i, i ^ 1) for i in range(size)])


def in_order(parts, axis, dtype=None):
    mine = lax.axis_index("dp")
    shape = list(parts[0].shape)
    size = shape[axis]
    shape[axis] = 4 * size
    out = jnp.zeros(shape, dtype or parts[0].dtype)
    for k, part in enumerate(parts):
        out = lax.dynamic_update_slice_in_dim(
            out, part.astype(out.dtype), (mine ^ k) * size, axis
        )
    return out


def local(
    tokens,
    lengths,
    attention_gain,
    query_weight,
    key_weight,
    value_weight,
    output_weight,
    feedforward_gain,
    gate_weight,
    up_weight,
    down_weight,
    cotangent,
):
    rows, depth = tokens.shape
    shards = lax.axis_size("seq")
    mine = lax.axis_index("dp")
    place = lax.axis_index("seq")
    core = place % 2
    wide = HEADS // KV_HEADS * HEAD_DIM
    side = depth // 2
    near = lambda v: lax.all_gather(v, "seq", axis=0, tiled=True)
    far = lambda v: lax.psum_scatter(v, "seq", scatter_dimension=0, tiled=True)

    gain_a = attention_gain.astype(F32)[:, None]
    gain_f = feedforward_gain.astype(F32)[:, None]
    own_qkv = jnp.concatenate(
        [
            lax.dynamic_slice_in_dim(query_weight, mine * wide, wide, 1),
            lax.dynamic_slice_in_dim(key_weight, mine * HEAD_DIM, HEAD_DIM, 1),
            lax.dynamic_slice_in_dim(value_weight, mine * HEAD_DIM, HEAD_DIM, 1),
        ],
        axis=1,
    )
    w_qkv = near((own_qkv.astype(F32) * gain_a).astype(BF))
    own_block = lax.dynamic_slice_in_dim(
        output_weight, mine * (depth // 4), depth // 4, 1
    )
    sizes = join([lengths] + [hop(lengths, k) for k in range(1, 4)])
    xs = gather_plane(tokens)
    own_out = near(tie(own_block, w_qkv, xs[1], xs[2], sizes))
    spot = jnp.stack([mine, core * side, (1 - core) * side])
    piece = down_weight.shape[0] // 4
    w_down = near(lax.dynamic_slice_in_dim(down_weight, mine * piece, piece, 0))
    own_gate, own_up = pick_columns(mine[None], gain_f, gate_weight, up_weight, shards)
    w_gate = near(own_gate)
    w_up = near(own_up)

    count = sizes.shape[1]
    before = jnp.arange(count)[:, None] <= jnp.arange(count)[None, :]
    ends = jnp.sum(jnp.where(before[None], sizes[:, :, None], 0), axis=1)
    index = place * rows + jnp.arange(rows, dtype=jnp.int32)
    passed = ends[:, None, :] <= index[None, :, None]
    begin = jnp.max(jnp.where(passed, ends[:, None, :], 0), axis=2)
    position = (index[None, :] - begin).astype(F32).reshape(4 * rows)
    half = HEAD_DIM // 2
    inverse = ROPE_BASE ** (-jnp.arange(half, dtype=F32) * 2.0 / HEAD_DIM)
    theta = position[:, None] * inverse[None, :]
    cos_h, sin_h = jnp.cos(theta), jnp.sin(theta)
    cos_t = jnp.concatenate([cos_h] * 4, axis=1)
    sin_t = jnp.concatenate([-sin_h, sin_h] * 2, axis=1)
    bounds = jnp.stack([begin, jnp.broadcast_to(index[None, :], begin.shape)], axis=1)
    bounds = jnp.concatenate([bounds] * (wide // HEAD_DIM), axis=2)
    low = begin[:, 0] // rows
    split = jnp.clip((begin[:, rows - 1] + rows - 1) // rows, low, place)
    where = jnp.concatenate([low, split, place[None]])

    made = ()
    for k, pieces in enumerate((xs[0:1], xs[1:2], xs[2:3], xs[3:5])):
        made = project(k, pieces, w_qkv, cos_t, sin_t, rows, made)
    hat, queries, own_kv = made
    own_half, own_rest = (
        lax.dynamic_slice_in_dim(own_out, c * side, side, 0) for c in (core, 1 - core)
    )
    kv = lax.all_gather(tie(own_kv, own_half), "seq", axis=0)
    own_half = tie(own_half, xs[3], xs[4])
    own_half, got_one, got_two, far_one, far_two = gather_plane(own_half)
    got = [own_half, got_one, got_two]
    swapped = [own_rest, core_swap(got_one), core_swap(got_two)]
    dy_own = tie(cotangent, got_one, got_two)
    dy_one, dy_two = hop(dy_own, 1), hop(dy_own, 2)
    mixed_heads, lse = attend(
        where, queries, kv, bounds, rows, (got_one, got_two, *swapped[1:])
    )
    mixed_heads = tie(mixed_heads, far_one, far_two, dy_one, dy_two)
    got.append(join([tie(far_one, mixed_heads), far_two]))
    swapped.append(core_swap(got[3]))
    w_outs = list(zip(got, swapped, strict=True))
    mixes = [mixed_heads[:rows]] + [
        hop(mixed_heads[k * rows : (k + 1) * rows], k) for k in range(1, 4)
    ]
    mixed_one, mixed_two, middle, hat_one, hat_two = output_product(
        spot, mixes, w_outs, tokens
    )

    part = rows // 2
    dy_far = hop(tie(dy_two[:part], *mixes), 1), hop(tie(dy_one[part:], *mixes), 2)
    dy_all = join([tie(dy_own, hat_one), dy_one, dy_two, *dy_far])
    d_hidden = row_product("hidden_back", dy_all, w_down, NT, rows, (hat_two,))
    hats = gather_halves(hat_one, hat_two, (d_hidden,))
    mixes_all = gather_halves(tie(mixed_one, *hats[6:]), tie(mixed_two, *hats[6:]))
    gate, d_up, hat_all = gate_product(hats, w_gate, d_hidden, rows)
    up_raw = row_product("up_gradient", hat_all, d_up, TN, wide)
    up_part = far(up_raw)
    ups_of = functools.partial(
        up_product, hat=hat_all, w_up=w_up, gate=gate, d_hidden=d_hidden, rows=rows
    )
    back = functools.partial(back_product, d_up=d_up, w_gate=w_gate, w_up=w_up, rows=rows)
    some = ups_of((3,), needs=(up_raw, *mixes_all[2:6]))
    far_one, far_two = back((3,), d_gate=some[1], needs=mixes_all[6:])
    hidden, d_gate = ups_of((0, 1, 2), needs=(far_one,), before=some)
    came = reduce_first([None] * 5 + [far_one, far_two])
    down_raw = column_product("down_gradient", hidden, dy_all, TN, wide)
    down_part = far(down_raw)
    sides = back((1, 2), d_gate=d_gate, needs=(down_raw, *came))
    came += reduce_plain((None, *sides))
    first, terms = reduce_second((None, *sides), came)
    (d_own,) = back((0,), d_gate=d_gate, needs=(first,))
    terms = (d_own, *terms[1:])
    mixed_all = join(mixes_all)
    d_middle, *blocks = middle_back(
        spot, terms, middle, cotangent, w_outs, (up_part, mixed_all)
    )

    d_heads = join([blocks[0]] + [hop(blocks[k], k) for k in range(1, 4)])
    gate_raw = row_product("gate_gradient", hat_all, d_gate, TN, wide, (blocks[0],))
    gate_part = far(gate_raw)
    outs = down_product(hidden, w_down, rows, (gate_raw,))
    ups_one, ups_two = hop(up_part, 1), hop(up_part, 2)
    dq, dkv = attend_back(
        where, queries, kv, bounds, d_heads, mixed_heads, lse, cos_t, sin_t, rows, (outs[6], ups_one, ups_two)
    )
    came = reduce_first(outs)
    downs_one, downs_two = hop(down_part, 1), hop(down_part, 2)
    ups_far = hop(up_part, 3)
    dkv = tie(dkv, gate_part, *came, downs_one, downs_two, ups_far)
    came += reduce_plain(outs, dkv)
    own_dkv = far(dkv.reshape(shards * 4 * rows, 128))
    first, terms = reduce_second(outs, came, (dkv,))
    out_raw = output_gradient_of(mixed_all, d_heads, wide, (first,))
    downs_far = hop(tie(down_part, dkv), 3)
    own_dkv = tie(own_dkv, out_raw, *terms[1:], downs_far)
    gate_part = tie(gate_part, own_dkv)
    gates_one, gates_two = hop(gate_part, 1), hop(gate_part, 2)
    both_raw, d_qkv = join_gradients(dq, own_dkv, cos_t, sin_t, rows, hat, out_raw)
    fs = list(project_back(d_qkv, w_qkv, rows, (both_raw,)))
    fs[5], fs[6] = (tie(f, gates_one, gates_two) for f in fs[5:])
    both_part = far(both_raw)
    layer_output = sum_output(terms, middle, (fs[6],))
    came = (*reduce_first(fs), *reduce_plain(fs))
    first, terms = reduce_second(fs, came, came[2:])
    half_rows = gate_part.shape[0] // 2
    gates_one, gates_two = tie(gates_one, first), tie(gates_two, first)
    gates_far = [hop(gates_two[:half_rows], 1), hop(gates_one[half_rows:], 2)]
    token_gradient = sum_tokens(terms, tokens, d_middle)

    gate_gradient, gain_g = spread_columns(
        "spread_gate",
        mine[None],
        jnp.stack([gate_part, gates_one, gates_two, join(gates_far)]),
        gain_f,
        gate_weight,
        shards,
    )
    up_gradient, gain_u = spread_columns(
        "spread_up", mine[None], jnp.stack([tie(up_part, both_raw), ups_one, ups_two, ups_far]), gain_f, up_weight, shards
    )
    down_gradient = down_rows_in_order(
        spot, [down_part, downs_one, downs_two, downs_far], (both_raw,)
    )
    gradients = finish_attention(
        mine[None],
        gather_direct(both_part),
        gain_a,
        output_weight,
        query_weight,
        key_weight,
        value_weight,
    )
    output_gradient, query_gradient, key_gradient, value_gradient, gain_a_gradient = gradients
    return (
        layer_output,
        token_gradient,
        gain_a_gradient[:, 0],
        query_gradient,
        key_gradient,
        value_gradient,
        output_gradient,
        (gain_g + gain_u)[:, 0],
        gate_gradient,
        up_gradient,
        down_gradient,
    )


def solution(mesh):
    both = P(("dp", "seq"), None)
    flat = P("seq")
    split = P("seq", None)
    return jax.shard_map(
        local,
        mesh=mesh,
        in_specs=(
            both,
            P("dp", None),
            flat,
            split,
            split,
            split,
            split,
            flat,
            split,
            split,
            split,
            both,
        ),
        out_specs=(
            both,
            both,
            flat,
            split,
            split,
            split,
            split,
            flat,
            split,
            split,
            split,
        ),
        check_vma=False,
    )
```
